32 devices in a mesh: dp: 8 (over z, x), row: 2 (over y), col: 2 (over core).
Axes of the slice: x: 2, y: 2, z: 4, core: 2. Of those that a mesh axis runs over, the one named last changes fastest.
Arguments:
- latents: bfloat16 [4096, 768], P(('dp', 'row'), 'col'), may hold values from -6 to 6
- labels: int32 [16], P('dp'), may hold values from 0 to 999
- timesteps: int32 [16], P('dp'), may hold values from 0 to 999
- class_table: bfloat16 [1000, 768], P(None, 'row'), may hold values from -6 to 6
- mod_weight: bfloat16 [768, 6, 768], P('row', None, 'col'), may hold values from -0.21875 to 0.21875
- mod_bias: bfloat16 [6, 768], P(None, 'col'), may hold values from -3 to 3
- qkv_weight: bfloat16 [768, 12, 3, 64], P('col', 'row'), may hold values from -0.21875 to 0.21875
- query_value_bias: bfloat16 [2, 12, 64], P(None, ('row', 'col')), may hold values from -3 to 3
- out_weight: bfloat16 [12, 64, 768], P('row', None, 'col'), may hold values from -0.21875 to 0.21875
- out_bias: bfloat16 [768], P('col'), may hold values from -3 to 3
- up_weight: bfloat16 [768, 3072], P('col', 'row'), may hold values from -0.21875 to 0.21875
- up_bias: bfloat16 [3072], P('row'), may hold values from -3 to 3
- down_weight: bfloat16 [3072, 768], P('row', 'col'), may hold values from -0.109375 to 0.109375
- down_bias: bfloat16 [768], P('col'), may hold values from -3 to 3
- cotangent: bfloat16 [4096, 768], P(('dp', 'row'), 'col'), may hold values from -6 to 6
Outputs:
- output: bfloat16 [4096, 768], P(('dp', 'row'), 'col')
- grad_latents: float32 [4096, 768], P(('dp', 'row'), 'col')
- grad_cond: float32 [16, 768], P('dp', 'row')
- grad_mod_weight: float32 [768, 6, 2, 384], P('row', None, 'col', 'dp')
- grad_mod_bias: float32 [6, 2, 384], P(None, 'col', 'dp')
- grad_qkv_weight: float32 [2, 384, 12, 3, 64], P('col', 'dp', 'row')
- grad_query_value_bias: float32 [2, 12, 64], P(None, ('row', 'col'), 'dp')
- grad_out_weight: float32 [12, 64, 2, 384], P('row', None, 'col', 'dp')
- grad_out_bias: float32 [2, 384], P('col', 'dp')
- grad_up_weight: float32 [768, 2, 1536], P('col', 'row', 'dp')
- grad_up_bias: float32 [2, 1536], P('row', 'dp')
- grad_down_weight: float32 [3072, 2, 384], P('row', 'col', 'dp')
- grad_down_bias: float32 [2, 384], P('col', 'dp')
The draws below stay inside these ranges and needn't reach their ends.
All inputs are finite; a program needn't handle non-finite values.
Results may differ from the reference program's by a relative error of at most 0.017.
Values may be sent and summed in bfloat16 or wider, within the bound.
No kernel may reach another device: no remote copies, remote signals or barrier semaphores. Data moves between devices by JAX's collectives and lax.ppermute only.
A program may use at most 128 MiB of HBM per device.

```python
import math
import jax
import jax.numpy as jnp
from jax import lax

D = 768
H = 12
HD = 64
FF = 3072
SEQ = 256
CLASSES = 1000
IMAGES = 16
TOKENS = 4096
N_ROW = 2
N_COL = 2


def set_ends(result, own_key, least, largest):
    shape = result.shape
    spot = [jax.random.randint(jax.random.fold_in(own_key, axis), (), 0, shape[axis]) for axis in range(len(shape))]
    result = result.at[tuple(spot)].set(least)
    longest = shape.index(max(shape))
    spot[longest] = (spot[longest] + 1) % shape[longest]
    return result.at[tuple(spot)].set(largest)


def levels(own_key, shape, split, smallest, top_value):
    def one(dim, shards_of):
        draws = jax.random.uniform(jax.random.fold_in(jax.random.fold_in(own_key, 6), dim), (shards_of,), jnp.float32, smallest / len(split), top_value / len(split))
        return jnp.repeat(jnp.exp(draws), shape[dim] // shards_of).reshape((-1,) + (1,) * (len(shape) - dim - 1))

    loudness = one(*split[0])
    for cut in split[1:]:
        loudness = loudness * one(*cut)
    return loudness


def centred(own_key, extent, deviation, most, pieces=(), kind=jnp.bfloat16):
    values = jax.random.normal(own_key, extent, jnp.float32) * deviation
    if len(pieces) > 0:
        values = levels(own_key, extent, pieces, -0.22, 0.18) * values
    return jnp.clip(values, min=-most, max=most).astype(kind)


def setup_inputs(seed: int = 0) -> dict:
    keys = jax.random.split(jax.random.key(seed), 16)
    return {
        "latents": centred(keys[0], (TOKENS, D), 1.0, 6.0, ((0, 16), (1, 2))),
        "labels": set_ends(jax.random.randint(keys[1], (IMAGES,), 0, CLASSES), jax.random.fold_in(keys[1], 1), 0, CLASSES - 1).astype(jnp.int32),
        "timesteps": set_ends(jax.random.randint(keys[2], (IMAGES,), 0, 1000), jax.random.fold_in(keys[2], 1), 0, 999).astype(jnp.int32),
        "class_table": centred(keys[3], (CLASSES, D), 1.0, 6.0, ((1, 2),)),
        "mod_weight": centred(keys[4], (D, 6, D), D ** -0.5, 0.21875, ((0, 2), (2, 2))),
        "mod_bias": centred(keys[5], (6, D), 0.5, 3.0, ((1, 2),)),
        "qkv_weight": centred(keys[6], (D, H, 3, HD), D ** -0.5, 0.21875, ((0, 2), (1, 2))),
        "query_value_bias": centred(keys[7], (2, H, HD), 0.5, 3.0, ((1, 4),)),
        "out_weight": centred(keys[8], (H, HD, D), (H * HD) ** -0.5, 0.21875, ((0, 2), (2, 2))),
        "out_bias": centred(keys[9], (D,), 0.5, 3.0, ((0, 2),)),
        "up_weight": centred(keys[10], (D, FF), D ** -0.5, 0.21875, ((0, 2), (1, 2))),
        "up_bias": centred(keys[11], (FF,), 0.5, 3.0, ((0, 2),)),
        "down_weight": centred(keys[12], (FF, D), FF ** -0.5, 0.109375, ((0, 2), (1, 2))),
        "down_bias": centred(keys[13], (D,), 0.5, 3.0, ((0, 2),)),
        "cotangent": centred(keys[14], (TOKENS, D), 1.0, 6.0, ((0, 16), (1, 2))),
    }


HIGH = lax.Precision.HIGHEST
EPSILON = 1e-06

@jax.custom_vjp
def low(v):
    return lax.optimization_barrier(v.astype(jnp.bfloat16)).astype(jnp.float32)

@jax.custom_vjp
def low_back(v):
    return v

def low_keep(v):
    return (low(v), None)

def low_pass(kept, grad):
    return (grad,)

def back_keep(v):
    return (v, None)

def back_low(kept, grad):
    return (low(grad),)
low.defvjp(low_keep, low_pass)
low_back.defvjp(back_keep, back_low)

def embed(labels, timesteps, class_table):
    half_width = D // 2
    frequency = jnp.exp(-math.log(10000.0) * jnp.arange(half_width, dtype=jnp.float32) / half_width)
    angles = timesteps.astype(jnp.float32)[:, None] * frequency[None, :]
    wave_rows = jnp.concatenate([jnp.cos(angles), jnp.sin(angles)], axis=1)
    return class_table.astype(jnp.float32)[labels] + wave_rows

def normalize(values):
    centre = lax.optimization_barrier(jnp.mean(values, axis=-1, keepdims=True))
    centered = values - centre
    return centered * lax.rsqrt(lax.optimization_barrier(jnp.mean(centered * centered, axis=-1, keepdims=True)) + EPSILON)

def layer(latents, cond, mod_weight, mod_bias, qkv_weight, query_value_bias, out_weight, out_bias, up_weight, up_bias, down_weight, down_bias):
    soft_cond = low(jax.nn.silu(cond))
    modulation = jnp.einsum('id,dkf->ikf', soft_cond, mod_weight, precision=HIGH) + mod_bias[None]
    zeros_row = jnp.zeros((H, HD), jnp.float32)
    qkv_bias = jnp.stack([query_value_bias[0], zeros_row, query_value_bias[1]], axis=1)
    factor = 1.0 / math.sqrt(HD)
    count = math.gcd(IMAGES, 16)

    def group(item):
        latent, mods = item
        shift_one = mods[:, 0][:, None]
        scale_one = mods[:, 1][:, None]
        gate_one = mods[:, 2][:, None]
        shift_two = mods[:, 3][:, None]
        scale_two = mods[:, 4][:, None]
        gate_two = mods[:, 5][:, None]
        normed_one = low(normalize(latent) * (1.0 + scale_one) + shift_one)
        packed = low_back(low(jnp.einsum('gsd,dhcf->gshcf', normed_one, qkv_weight, precision=HIGH) + qkv_bias))
        query = packed[:, :, :, 0]
        keys_all = packed[:, :, :, 1]
        values = packed[:, :, :, 2]
        scores = low_back(jnp.einsum('gqhf,gkhf->ghqk', query, keys_all, precision=HIGH) * factor)
        probs = low(jax.nn.softmax(scores, axis=-1))
        attended = low_back(low(jnp.einsum('ghqk,gkhf->gqhf', probs, values, precision=HIGH)))
        branch_one = low_back(jnp.einsum('gqhf,hfd->gqd', attended, out_weight, precision=HIGH) + out_bias)
        resid_one = latent + gate_one * branch_one
        normed_two = low(normalize(resid_one) * (1.0 + scale_two) + shift_two)
        hidden_pre = low_back(jnp.einsum('gsd,df->gsf', normed_two, up_weight, precision=HIGH) + up_bias)
        active = low(jax.nn.gelu(hidden_pre, approximate=True))
        branch_two = low_back(jnp.einsum('gsf,fd->gsd', active, down_weight, precision=HIGH) + down_bias)
        return resid_one + gate_two * branch_two
    blocks = lax.map(jax.checkpoint(group), (latents.reshape(IMAGES // count, count, SEQ, D), modulation.reshape(IMAGES // count, count, 6, D)))
    return blocks.reshape(TOKENS, D)

def reference(latents, labels, timesteps, class_table, mod_weight, mod_bias, qkv_weight, query_value_bias, out_weight, out_bias, up_weight, up_bias, down_weight, down_bias, cotangent):
    cond = embed(labels, timesteps, class_table)
    primals = [latents.astype(jnp.float32), cond] + [arr.astype(jnp.float32) for arr in (mod_weight, mod_bias, qkv_weight, query_value_bias, out_weight, out_bias, up_weight, up_bias, down_weight, down_bias)]
    output, pullback = jax.vjp(layer, *primals)
    grads = pullback(cotangent.astype(jnp.float32))
    dc = D // N_COL
    return (output.astype(jnp.bfloat16), grads[0], grads[1], grads[2].reshape(D, 6, N_COL, dc), grads[3].reshape(6, N_COL, dc), grads[4].reshape(N_COL, dc, H, 3, HD), grads[5], grads[6].reshape(H, HD, N_COL, dc), grads[7].reshape(N_COL, dc), grads[8].reshape(D, N_ROW, FF // N_ROW), grads[9].reshape(N_ROW, FF // N_ROW), grads[10].reshape(FF, N_COL, dc), grads[11].reshape(N_COL, dc))
```

```python
import functools
import math

import jax
import jax.numpy as jnp
from jax import lax
from jax.experimental import pallas as pl
from jax.experimental.pallas import tpu as pltpu
from jax.sharding import PartitionSpec as P

D = 768
HALF = 384
SEQ = 256
HEADS = 6
HD = 64
QKV = HEADS * 3 * HD
FEED = 1536
EPSILON = 1e-06
HIGH = lax.Precision.HIGHEST
F32 = jnp.float32
BF16 = jnp.bfloat16
SWAP = [(0, 1), (1, 0)]
ALPHA = 0.7978845608
CUBIC = 0.044715


def mm(first, second, dims, precision=None):
    return lax.dot_general(
        first, second, ((dims[:1], dims[1:]), ((), ())), precision=precision, preferred_element_type=F32
    )


def call(kernel, outs, inputs, micros, name, after=(), scratch=(), limit=40):
    size = sum(math.prod(a.shape) * a.dtype.itemsize for a in inputs)
    size += sum(math.prod(s) * jnp.dtype(t).itemsize for s, t in outs)
    count = len(after)

    def body(*refs):
        kernel(*refs[count:])

    return pl.pallas_call(
        body if count else kernel,
        out_shape=[jax.ShapeDtypeStruct(s, t) for s, t in outs],
        in_specs=[pl.BlockSpec(memory_space=pl.ANY)] * count
        + [pl.BlockSpec(memory_space=pltpu.VMEM)] * len(inputs),
        out_specs=[pl.BlockSpec(memory_space=pltpu.VMEM)] * len(outs),
        scratch_shapes=list(scratch),
        compiler_params=pltpu.CompilerParams(vmem_limit_bytes=limit * 1024 * 1024),
        cost_estimate=pl.CostEstimate(flops=int(micros * 1.15e9), bytes_accessed=int(size), transcendentals=0),
        name=name,
    )(*after, *inputs)


def row_mean(values):
    return jnp.sum(values, axis=1, keepdims=True) * (1.0 / D)


def norm_of(values):
    centred = values - row_mean(values)
    inverse = lax.rsqrt(row_mean(centred * centred) + EPSILON)
    return centred * inverse, inverse


def halves(first, second):
    return jnp.concatenate([first, second], axis=1)


def blocks(step=64):
    return [slice(i, i + step) for i in range(0, SEQ, step)]


def mod_kernel(cond, weight, part, soft):
    place = lax.broadcasted_iota(jnp.int32, (16, HALF), 0)
    values = jnp.where(place == 0, cond[0:1, :], jnp.where(place == 1, cond[1:2, :], 0.0))
    soft16 = (values / (1.0 + jnp.exp(-values))).astype(BF16)
    soft[...] = soft16.astype(F32)[0:2]
    part[...] = jnp.zeros((16, HALF), F32)
    for k in range(6):
        both = mm(soft16, weight[k], (1, 0))
        part[k : k + 1, :] = both[0:1]
        part[8 + k : 9 + k, :] = both[1:2]


def mix_kernel(part, part_recv, bias, vectors, keep, other):
    total = part[...] + part_recv[...]
    here = lax.axis_index("col") == 0
    shift = bias[...].astype(F32)
    keep[...] = jnp.where(here, total[0:6], total[8:14]) + shift
    other[0:6, :] = jnp.where(here, total[8:14], total[0:6]) + shift
    other[6:8, :] = jnp.zeros((2, HALF), F32)
    other[8:16, :] = vectors[...]


def pick_image(own, from_row, from_col, from_diag, rows):
    same = lax.axis_index("row") == lax.axis_index("col")
    first = jnp.where(same, own[rows, :].astype(F32), from_row[rows, :].astype(F32))
    second = jnp.where(same, from_col[rows, :].astype(F32), from_diag[rows, :].astype(F32))
    return halves(first, second)


def norm_kernel(own, from_row, from_col, from_diag, lat, normal, cot):
    for rows in blocks():
        values = pick_image(own, from_row, from_col, from_diag, rows)
        lat[rows, :] = values.astype(BF16)
        normal[rows, :] = norm_of(values)[0]
        later = slice(rows.start + SEQ, rows.stop + SEQ)
        cot[rows, :] = pick_image(own, from_row, from_col, from_diag, later).astype(BF16)


def first_kernel(
    normal, keep, other, other_col, qkv_own, qkv_peer, out_own, out_peer,
    mod, bias, normed_own, normed_peer, packed, attended, part,
):
    mods = halves(keep[...], other_col[0:6, :])
    mod[...] = mods
    shift, scale = mods[0:1], 1.0 + mods[1:2]
    for rows in blocks():
        normed = (normal[rows, :] * scale + shift).astype(BF16)
        normed_own[rows, :] = normed[:, :HALF]
        normed_peer[rows, :] = normed[:, HALF:]
    bias[...] = halves(other[8:16, :], other_col[8:16, :])
    place = lax.broadcasted_iota(jnp.int32, (16, SEQ), 0)
    one_hot = (place == 0).astype(BF16)
    mine = lax.axis_index("col")
    front = jnp.where(mine == 0, other[10:11, :], other_col[10:11, :])
    back = jnp.where(mine == 0, other_col[10:11, :], other[10:11, :])
    wide = lax.broadcasted_iota(jnp.int32, (16, 3 * HD), 0)
    for h in range(HEADS):
        rows = slice(h * 192, h * 192 + 192)
        source, spot = (front if h < 3 else back), (h % 3) * HD
        line = jnp.concatenate(
            [source[:, spot : spot + HD], jnp.zeros((1, HD), F32), source[:, 192 + spot : 192 + spot + HD]], axis=1
        )
        full = mm(qkv_own[rows, :], normed_own[...], (1, 1))
        full = full + mm(qkv_peer[rows, :], normed_peer[...], (1, 1))
        full = full + mm(jnp.where(wide == 0, line, 0.0).astype(BF16), one_hot, (0, 0))
        full = full.astype(BF16)
        packed[rows, :] = full
        query, key, value = full[0:64], full[64:128], full[128:192]
        scores = mm(key, query, (0, 0)) * 0.125
        expon = jnp.exp(scores - jnp.max(scores, axis=0, keepdims=True))
        probs = (expon * (1.0 / jnp.sum(expon, axis=0, keepdims=True))).astype(BF16)
        attended[h * 64 : h * 64 + 64, :] = mm(value, probs, (1, 0)).astype(BF16)
    part[:, :HALF] = mm(attended[...], out_own[...], (0, 0)).astype(BF16)
    part[:, HALF:] = mm(attended[...], out_peer[...], (0, 0)).astype(BF16)


def early_kernel(cot, mod, down_own, down_peer, grad_own, grad_peer, grad_active):
    gate = mod[5:6, :]
    for rows in blocks():
        grads = (cot[rows, :].astype(F32) * gate).astype(BF16)
        grad_own[rows, :] = grads[:, :HALF]
        grad_peer[rows, :] = grads[:, HALF:]
    for cols in [slice(j, j + 256) for j in range(0, FEED, 256)]:
        grad_active[:, cols] = mm(grad_own[...], down_own[cols, :], (1, 1)) + mm(
            grad_peer[...], down_peer[cols, :], (1, 1)
        )


def branch(part, part_recv, bias, rows):
    return part[rows, :].astype(F32) + part_recv[rows, :].astype(F32) + bias


def resid_of(lat, mod, bias, part, part_recv, rows):
    gate = mod[2:3, :]
    one = branch(part, part_recv, bias[0:1, :], rows)
    return lat[rows, :].astype(F32) + gate * one, one


def second_kernel(
    lat, mod, bias, part, part_recv, up_own, up_peer, up_bias, grad_active,
    normed_own, normed_peer, active, hidden, part_two,
):
    shift, scale = mod[3:4, :], 1.0 + mod[4:5, :]
    for rows in blocks():
        resid, unused = resid_of(lat, mod, bias, part, part_recv, rows)
        normal, unused = norm_of(resid)
        normed = (normal * scale + shift).astype(BF16)
        normed_own[rows, :] = normed[:, :HALF]
        normed_peer[rows, :] = normed[:, HALF:]
    for cols in [slice(j, j + 256) for j in range(0, FEED, 256)]:
        pre = mm(normed_own[...], up_own[:, cols], (1, 0)) + mm(normed_peer[...], up_peer[:, cols], (1, 0))
        pre = pre + up_bias[:, cols].astype(F32)
        square = pre * pre
        bend = jnp.tanh(ALPHA * (pre + CUBIC * (pre * square)))
        half = 0.5 * (1.0 + bend)
        active[:, cols] = (pre * half).astype(BF16)
        slope = half + 0.5 * pre * (1.0 - bend * bend) * (ALPHA * (1.0 + (3.0 * CUBIC) * square))
        hidden[:, cols] = (grad_active[:, cols] * slope).astype(BF16)
    part_two[:, :HALF] = mm(hidden[...], up_own[...], (1, 1)).astype(BF16)
    part_two[:, HALF:] = mm(hidden[...], up_peer[...], (1, 1)).astype(BF16)


def down_kernel(active, cot, down_own, down_peer, part, sums):
    sums[...] = jnp.zeros((8, D), F32)
    for cols, weight in ((slice(0, HALF), down_own), (slice(HALF, D), down_peer)):
        here = mm(active[...], weight[...], (1, 0)).astype(BF16)
        part[:, cols] = here
        sums[0:1, cols] = jnp.sum(here.astype(F32) * cot[:, cols].astype(F32), axis=0, keepdims=True)


def spots(left, bit):
    step = 1 << (len(left) - 1 - left.index(bit))
    return step, [q for q in range(1 << len(left)) if q & step == 0]


def bit_here(bit):
    return lax.rem(lax.div(lax.axis_index("dp"), 1 << bit), 2)


def split_store(full, left, bit, send, keep):
    here = bit_here(bit)
    size = full.shape[0] >> len(left)
    step, places = spots(left, bit)
    for q, place in enumerate(places):
        low = full[place * size : (place + 1) * size]
        high = full[(place + step) * size : (place + step + 1) * size]
        keep[q] = jnp.where(here == 0, low, high).astype(BF16)
        send[q] = jnp.where(here == 0, high, low).astype(BF16)


def tokens(own, recv, axis=0):
    return jnp.concatenate([own[...], recv[...]], axis=axis)


def up_grad_kernel(left, bit, normed, normed_recv, hidden, hidden_recv, send, keep, bias):
    rows = tokens(normed, normed_recv)
    grads = tokens(hidden, hidden_recv)
    ones = jnp.ones((16, 2 * SEQ), BF16)
    bias[...] = mm(ones, grads, (1, 0))[0:1]
    split_store(mm(grads, rows, (0, 0)), left, bit, send, keep)


def down_grad_kernel(left, bit, grad, grad_recv, active, active_recv, send, keep, bias):
    grads = tokens(grad, grad_recv)
    acts = tokens(active, active_recv)
    ones = jnp.ones((16, 2 * SEQ), BF16)
    bias[...] = mm(ones, grads, (1, 0))[0:1]
    split_store(mm(grads, acts, (0, 0)), left, bit, send, keep)


def third_kernel(
    lat, mod, bias, part, part_recv, grad_two, grad_two_recv, cot, packed, sums,
    qkv_own, qkv_peer, out_own, out_peer,
    grad_resid, grad_own, grad_peer, grad_packed, part_three,
):
    gate, scale = mod[2:3, :], 1.0 + mod[4:5, :]
    for rows in blocks():
        resid, unused = resid_of(lat, mod, bias, part, part_recv, rows)
        normal, inverse = norm_of(resid)
        weighted = (grad_two[rows, :].astype(F32) + grad_two_recv[rows, :].astype(F32)) * scale
        back = inverse * (weighted - row_mean(weighted) - normal * row_mean(weighted * normal))
        grads = cot[rows, :].astype(F32) + back
        grad_resid[rows, :] = grads
        gated = (grads * gate).astype(BF16)
        grad_own[rows, :] = gated[:, :HALF]
        grad_peer[rows, :] = gated[:, HALF:]
    for h in range(HEADS):
        base = h * 192
        query, key = packed[base : base + 64, :], packed[base + 64 : base + 128, :]
        value = packed[base + 128 : base + 192, :]
        wide = slice(h * 64, h * 64 + 64)
        grad_att = mm(out_own[wide, :], grad_own[...], (1, 1)) + mm(out_peer[wide, :], grad_peer[...], (1, 1))
        grad_att = grad_att.astype(BF16)
        scores = mm(key, query, (0, 0)) * 0.125
        expon = jnp.exp(scores - jnp.max(scores, axis=0, keepdims=True))
        probs = expon * (1.0 / jnp.sum(expon, axis=0, keepdims=True))
        grad_probs = mm(value, grad_att, (0, 0))
        total = jnp.sum(probs * grad_probs, axis=0, keepdims=True)
        grad_scores = (probs * (grad_probs - total)).astype(BF16)
        grad_packed[base : base + 64, :] = (mm(key, grad_scores, (1, 0)) * 0.125).astype(BF16)
        grad_packed[base + 64 : base + 128, :] = (mm(query, grad_scores, (1, 1)) * 0.125).astype(BF16)
        grad_packed[base + 128 : base + 192, :] = mm(grad_att, probs.astype(BF16), (1, 1)).astype(BF16)
    part_three[0:SEQ, :HALF] = mm(grad_packed[...], qkv_own[...], (0, 0)).astype(BF16)
    part_three[0:SEQ, HALF:] = mm(grad_packed[...], qkv_peer[...], (0, 0)).astype(BF16)
    values = sums[0:1, :]
    high = values.astype(BF16).astype(F32)
    middle = (values - high).astype(BF16).astype(F32)
    place = lax.broadcasted_iota(jnp.int32, (16, D), 0)
    terms = jnp.where(place == 0, high, jnp.where(place == 1, middle, jnp.where(place == 2, values - high - middle, 0.0)))
    part_three[SEQ : SEQ + 16, :] = terms.astype(BF16)


def proj_grad_kernel(
    left, bit, normed, normed_recv, packed, packed_recv, grad, grad_recv, attended, attended_recv,
    send, keep, out_bias, pack_bias,
):
    rows = tokens(normed, normed_recv)
    packs = tokens(packed, packed_recv, 1)
    grads = tokens(grad, grad_recv)
    atts = tokens(attended, attended_recv, 1)
    ones = jnp.ones((16, 2 * SEQ), BF16)
    out_bias[...] = mm(ones, grads, (1, 0))[0:1]
    sums = mm(ones, packs, (1, 1))[0:1]
    pack_bias[...] = jnp.where(lax.axis_index("col") == 0, sums[:, : QKV // 2], sums[:, QKV // 2 :])
    full = halves(mm(rows, packs, (0, 1)), mm(grads, atts, (0, 1)))
    split_store(full, left, bit, send, keep)


def last_kernel(
    lat, mod, bias, part, part_recv, grad_two, grad_two_recv, cot,
    grad_resid, grad_one, grad_one_recv, part_two, part_two_recv, branch_sums,
    out_own, out_peer, lat_own, lat_peer, mod_own, mod_peer,
):
    gate, scale = mod[5:6, :], 1.0 + mod[1:2, :]
    sums = [jnp.zeros((1, D), F32)] * 6
    for rows in blocks():
        resid, one = resid_of(lat, mod, bias, part, part_recv, rows)
        two = branch(part_two, part_two_recv, bias[1:2, :], rows)
        result = (resid + gate * two).astype(BF16)
        out_own[rows, :] = result[:, :HALF]
        out_peer[rows, :] = result[:, HALF:]
        normal_two, unused = norm_of(resid)
        normal, inverse = norm_of(lat[rows, :].astype(F32))
        normed_grad = grad_one[rows, :].astype(F32) + grad_one_recv[rows, :].astype(F32)
        normed_two = grad_two[rows, :].astype(F32) + grad_two_recv[rows, :].astype(F32)
        resid_grad = grad_resid[rows, :]
        weighted = normed_grad * scale
        back = inverse * (weighted - row_mean(weighted) - normal * row_mean(weighted * normal))
        grads = resid_grad + back
        lat_own[rows, :] = grads[:, :HALF]
        lat_peer[rows, :] = grads[:, HALF:]
        terms = (
            normed_grad,
            normed_grad * normal,
            resid_grad * one,
            normed_two,
            normed_two * normal_two,
            cot[rows, :].astype(F32),
        )
        sums = [s + jnp.sum(t, axis=0, keepdims=True) for s, t in zip(sums, terms)]
    far = grad_one_recv[SEQ : SEQ + 16, :].astype(F32)
    far = far[0:1] + far[1:2] + far[2:3]
    sums[5] = sums[5] * bias[1:2, :] + branch_sums[0:1, :] + far
    for k in range(6):
        mod_own[k : k + 1, :] = sums[k][:, :HALF]
        mod_peer[k : k + 1, :] = sums[k][:, HALF:]


def payload_kernel(mod_own, mod_recv, soft, up_bias, down_bias, out_bias, pack_bias, weight, payload, part_cond):
    col_index = lax.axis_index("col")
    own, recv = mod_own[...], mod_recv[...]
    zero = jnp.where(col_index == 0, own, recv)
    one = jnp.where(col_index == 0, recv, own)
    payload = payload.at[0]
    payload[...] = jnp.zeros(payload.shape, F32)
    payload[0:6, :] = zero
    payload[6:7, :] = soft[0:1, :]
    payload[8:14, :] = one
    payload[14:15, :] = soft[1:2, :]
    for k in range(4):
        payload[16 + k : 17 + k, :] = up_bias[:, k * HALF : k * HALF + HALF]
    payload[20:21, :] = down_bias[...]
    payload[21:22, :] = out_bias[...]
    payload[22:23, :] = pack_bias[:, :HALF]
    payload[23:24, 0:192] = pack_bias[:, HALF:]
    place = lax.broadcasted_iota(jnp.int32, (16, HALF), 0)
    total = jnp.zeros((16, HALF), F32)
    for k in range(6):
        pair = jnp.where(place == 0, zero[k : k + 1], jnp.where(place == 1, one[k : k + 1], 0.0))
        high = pair.astype(BF16)
        rest = pair - high.astype(F32)
        mid = rest.astype(BF16)
        low = (rest - mid.astype(F32)).astype(BF16)
        for piece in (high, mid, low):
            total = total + mm(piece, weight[k], (1, 1))
    part_cond[...] = total[0:2]


def add_kernel(left, bit, keep, recv, send_next, keep_next):
    here = bit_here(bit)
    step, places = spots(left, bit)
    for q, first in enumerate(places):
        for place, out in ((first + step * here, keep_next), (first + step * (1 - here), send_next)):
            out[q] = (keep[place].astype(F32) + recv[place].astype(F32)).astype(BF16)


def join_kernel(first, second, out):
    count = first.shape[0]
    out[0:count] = first[...]
    out[count : 2 * count] = second[...]


def sum_kernel(up_keep, up_recv, down_keep, down_recv, proj_keep, proj_recv, up, down, qkv, out):
    up[...] = up_keep[0].astype(F32) + up_recv[0].astype(F32)
    down[...] = down_keep[0].astype(F32) + down_recv[0].astype(F32)
    both = proj_keep[0].astype(F32) + proj_recv[0].astype(F32)
    for k in range(3 * HEADS):
        qkv[k] = both[:, k * HD : k * HD + HD]
    for h in range(HEADS):
        out[h] = both[:, QKV + h * HD : QKV + h * HD + HD]


def mod_sum_kernel(loads, weight, bias, vectors, full):
    shards = loads.shape[0]
    width = weight.shape[1]
    place = lax.axis_index("dp") * (HALF // shards) if width < HALF else 0
    images = [loads[s, 8 * i : 8 * i + 8, :] for s in range(shards) for i in range(2)]
    soft = jnp.concatenate([image[6:7] for image in images], axis=0)
    for k in range(6):
        rows = jnp.concatenate([image[k : k + 1] for image in images], axis=0)
        bias[k : k + 1, :] = jnp.sum(rows, axis=0, keepdims=True)
        full[...] = mm(rows, soft, (0, 0), HIGH)
        weight[k] = full[pl.ds(pl.multiple_of(place, 8), width), :]
    total = loads[0, 16:24, :]
    for s in range(1, shards):
        total = total + loads[s, 16:24, :]
    vectors[...] = total


def row_swap(values):
    return lax.ppermute(values, "row", SWAP)


def col_swap(values):
    return lax.ppermute(values, "col", SWAP)


def both_swap(values):
    return lax.ppermute(values, ("row", "col"), [(0, 3), (3, 0), (1, 2), (2, 1)])


def image_parts(values):
    from_row = lax.ppermute(values, ("row", "col"), [(0, 2), (3, 1)])
    from_col = lax.ppermute(values, ("row", "col"), [(1, 0), (2, 3)])
    from_diag = lax.ppermute(values, ("row", "col"), [(1, 2), (2, 1)])
    return values, from_row, from_col, from_diag


def swap_bit(values, bit, dp_size):
    return lax.ppermute(values, "dp", [(p, p ^ (1 << bit)) for p in range(dp_size)])


class Sums:
    def __init__(self, name, order, dp_size):
        self.name, self.order, self.dp_size = name, order, dp_size
        self.left, self.step = tuple(sorted(order, reverse=True)), 0

    def begin(self, send, keep):
        self.keep, self.recv = keep, swap_bit(send, self.order[0], self.dp_size)

    def advance(self, after):
        if self.step + 1 >= len(self.order):
            return after[0]
        self.left = tuple(b for b in self.left if b != self.order[self.step])
        self.step += 1
        bit = self.order[self.step]
        shape = (self.keep.shape[0] // 2,) + self.keep.shape[1:]
        kernel = functools.partial(add_kernel, self.left, bit)
        send, keep = call(kernel, [(shape, BF16)] * 2, [self.keep, self.recv], 1.2, self.name, after)
        self.begin_next(send, keep)
        return keep

    def begin_next(self, send, keep):
        self.keep, self.recv = keep, swap_bit(send, self.order[self.step], self.dp_size)


def shards_fn(
    dp_size,
    latents,
    labels,
    timesteps,
    class_table,
    mod_weight,
    mod_bias,
    qkv_weight,
    query_value_bias,
    out_weight,
    out_bias,
    up_weight,
    up_bias,
    down_weight,
    down_bias,
    cotangent,
):
    row_index = lax.axis_index("row")
    same = row_index == lax.axis_index("col")
    bits = dp_size.bit_length() - 1
    wide = (SEQ, D)
    slim = (SEQ, HALF)
    pieces = dp_size // 2
    rows_down, rows_up = HALF // dp_size, FEED // dp_size
    every = tuple(range(bits))
    left = every[::-1]
    up = Sums("up_add", every, dp_size)
    down = Sums("down_add", every, dp_size)
    proj = Sums("proj_add", every, dp_size)
    inputs = image_parts(jnp.concatenate([latents, cotangent], axis=0))
    qkv_own = jnp.transpose(qkv_weight, (1, 2, 3, 0)).reshape(QKV, HALF)
    out_own = out_weight.reshape(HALF, HALF)
    qkv_peer, out_peer = col_swap(qkv_own), col_swap(out_own)

    classes = class_table.shape[0]
    picks = (labels[:, None] == jnp.arange(classes, dtype=jnp.int32)[None, :]).astype(BF16)
    looked = jnp.dot(picks, class_table, preferred_element_type=F32)
    frequency = jnp.exp(-math.log(10000.0) * jnp.arange(HALF, dtype=F32) / HALF)
    angles = timesteps.astype(F32)[:, None] * frequency[None, :]
    cond = looked + jnp.where(row_index == 0, jnp.cos(angles), jnp.sin(angles))
    mod_rows = jnp.transpose(mod_weight, (1, 0, 2))
    mod_part, soft = call(
        mod_kernel,
        [((16, HALF), F32), ((2, HALF), F32)],
        [cond, mod_rows],
        1,
        "mod",
        [inputs[2], qkv_peer, out_peer],
    )
    mod_part_recv = row_swap(mod_part)
    vectors = jnp.stack([out_bias, down_bias, query_value_bias.reshape(-1)]).astype(F32)
    vectors = jnp.pad(vectors, ((0, 5), (0, 0)))
    keep, other = call(
        mix_kernel,
        [((6, HALF), F32), ((16, HALF), F32)],
        [mod_part, mod_part_recv, mod_bias, vectors],
        0.3,
        "mix",
    )
    other_col = col_swap(other)
    lat, normal, cot = call(
        norm_kernel, [(wide, BF16), (wide, F32), (wide, BF16)], [*inputs], 1.5, "norm", [keep]
    )
    down_peer, up_peer = col_swap(down_weight), col_swap(up_weight)
    mod, bias, normed_own, normed_peer, packed, attended, part_one = call(
        first_kernel,
        [((6, D), F32), ((8, D), F32), (slim, BF16), (slim, BF16), ((QKV, SEQ), BF16), ((HALF, SEQ), BF16), (wide, BF16)],
        [normal, keep, other, other_col, qkv_own, qkv_peer, out_own, out_peer],
        5,
        "first",
    )
    part_one_recv = row_swap(part_one)
    two_grad_own, two_grad_peer, grad_active = call(
        early_kernel,
        [(slim, BF16), (slim, BF16), ((SEQ, FEED), F32)],
        [cot, mod, down_weight, down_peer],
        1,
        "early",
        [part_one],
    )
    normed_recv, attended_recv = col_swap(normed_peer), col_swap(attended)
    two_grad_recv = col_swap(two_grad_peer)
    resid_args = [lat, mod, bias, part_one, part_one_recv]
    second_own, second_peer, active, hidden, part_two = call(
        second_kernel,
        [(slim, BF16), (slim, BF16), ((SEQ, FEED), BF16), ((SEQ, FEED), BF16), (wide, BF16)],
        [*resid_args, up_weight, up_peer, up_bias.reshape(1, FEED), grad_active],
        3,
        "second",
        [normed_recv, attended_recv, two_grad_recv],
    )
    part_two_recv = row_swap(part_two)
    active_recv, hidden_recv, second_recv = col_swap(active), col_swap(hidden), col_swap(second_peer)
    branch_part, branch_sums = call(
        down_kernel, [(wide, BF16), ((8, D), F32)], [active, cot, down_weight, down_peer], 1, "down"
    )
    branch_recv = lax.ppermute(branch_part, ("row", "col"), [(1, 3), (2, 0)])
    down_send, down_keep, down_sum = call(
        functools.partial(down_grad_kernel, left, down.order[0]),
        [((pieces, rows_down, FEED), BF16), ((pieces, rows_down, FEED), BF16), ((1, HALF), F32)],
        [two_grad_own, two_grad_recv, active, active_recv],
        0.9,
        "down_grad",
        [branch_part],
    )
    down.begin(down_send, down_keep)
    up_send, up_keep, up_sum = call(
        functools.partial(up_grad_kernel, left, up.order[0]),
        [((pieces, rows_up, HALF), BF16), ((pieces, rows_up, HALF), BF16), ((1, FEED), F32)],
        [second_own, second_recv, hidden, hidden_recv],
        1.2,
        "up_grad",
        [down_send],
    )
    up.begin(up_send, up_keep)
    grad_resid, one_grad_own, one_grad_peer, grad_packed, part_three = call(
        third_kernel,
        [(wide, F32), (slim, BF16), (slim, BF16), ((QKV, SEQ), BF16), ((SEQ + 16, D), BF16)],
        [*resid_args, part_two, part_two_recv, cot, packed, branch_sums, qkv_own, qkv_peer, out_own, out_peer],
        5.6,
        "third",
        [up_send],
    )
    part_three_recv = row_swap(part_three)
    packed_recv, one_grad_recv = col_swap(grad_packed), col_swap(one_grad_peer)
    token = down.advance([part_three, branch_recv])
    proj_send, proj_keep, out_sum, pack_sum = call(
        functools.partial(proj_grad_kernel, left, proj.order[0]),
        [((pieces, rows_down, FEED), BF16), ((pieces, rows_down, FEED), BF16), ((1, HALF), F32), ((1, QKV // 2), F32)],
        [normed_own, normed_recv, grad_packed, packed_recv, one_grad_own, one_grad_recv, attended, attended_recv],
        1.3,
        "proj_grad",
        [token],
    )
    proj.begin(proj_send, proj_keep)
    token = down.advance([proj_send])
    result_own, result_peer, lat_grad_own, lat_grad_peer, mod_own, mod_peer = call(
        last_kernel,
        [(slim, BF16), (slim, BF16), (slim, F32), (slim, F32), ((6, HALF), F32), ((6, HALF), F32)],
        [
            *resid_args, part_two, part_two_recv, cot, grad_resid, part_three, part_three_recv,
            branch_part, branch_recv, branch_sums,
        ],
        1.6,
        "last",
        [token],
    )
    mod_recv, result_recv, lat_recv = col_swap(mod_peer), col_swap(result_peer), col_swap(lat_grad_peer)
    token = up.advance([mod_own])
    payload, part_cond = call(
        payload_kernel,
        [((1, 24, HALF), F32), ((2, HALF), F32)],
        [mod_own, mod_recv, soft, up_sum, down_sum, out_sum, pack_sum, mod_rows],
        1.6,
        "payload",
        [token],
    )
    part_cond_recv = col_swap(part_cond)
    token = payload
    for bit in every:
        recv = swap_bit(payload, bit, dp_size)
        for part in (([up], [proj], [proj])[bit] if bit < 3 else [up, down, proj]):
            token = part.advance([token])
        (payload,) = call(join_kernel, [((2 << bit, 24, HALF), F32)], [payload, recv], 1, "join", [token])
        token = payload
    width = HALF // dp_size
    mod_grad, mod_sums, vectors = call(
        mod_sum_kernel,
        [((6, width if width % 8 == 0 else HALF, HALF), F32), ((6, HALF), F32), ((8, HALF), F32)],
        [payload],
        3.5,
        "mod_sum",
        scratch=[pltpu.VMEM((HALF, HALF), F32)],
    )
    output = jnp.where(same, result_own, result_recv)
    grad_latents = jnp.where(same, lat_grad_own, lat_recv)
    grad_soft = part_cond + part_cond_recv
    unused, silu_back = jax.vjp(jax.nn.silu, cond)
    grad_cond = silu_back(grad_soft)[0]
    while min(part.step for part in (up, down, proj)) + 1 < bits:
        for part in (up, down, proj):
            token = part.advance([token])
    sums = [up.keep, up.recv, down.keep, down.recv, proj.keep, proj.recv]
    up_grad, down_grad, qkv_grad, out_grad = call(
        sum_kernel,
        [((rows_up, HALF), F32), ((rows_down, FEED), F32), ((3 * HEADS, rows_down, HD), F32), ((HEADS, rows_down, HD), F32)],
        sums,
        1.5,
        "sum",
    )
    dp_index = lax.axis_index("dp")

    def block(vector, size, axis):
        return lax.dynamic_slice_in_dim(vector, dp_index * size, size, axis)

    mod_bias_grad = block(mod_sums, width, 1)
    if width % 8 > 0:
        mod_grad = block(mod_grad, width, 1)
    up_bias_grad = block(vectors[0:4].reshape(1, FEED), rows_up, 1)
    down_bias_grad = block(vectors[4:5], width, 1)
    out_bias_grad = block(vectors[5:6], width, 1)
    pack_rows = vectors[6:8].reshape(-1)[: QKV // 2].reshape(HEADS // 2, 3, HD)
    pack_rows = jnp.stack([pack_rows[:, 0], pack_rows[:, 2]])
    pack_grad = block(pack_rows, HD // dp_size, 2)
    return (
        output,
        grad_latents,
        grad_cond,
        jnp.transpose(mod_grad, (2, 0, 1))[:, :, None, :],
        mod_bias_grad[:, None, :],
        jnp.transpose(qkv_grad.reshape(HEADS, 3, rows_down, HD), (2, 0, 1, 3))[None],
        pack_grad,
        jnp.transpose(out_grad, (0, 2, 1))[:, :, None, :],
        out_bias_grad,
        jnp.transpose(up_grad)[:, None, :],
        up_bias_grad,
        jnp.transpose(down_grad)[:, None, :],
        down_bias_grad,
    )


def solution(mesh):
    in_specs = (
        P(("dp", "row"), "col"),
        P("dp"),
        P("dp"),
        P(None, "row"),
        P("row", None, "col"),
        P(None, "col"),
        P("col", "row", None, None),
        P(None, ("row", "col"), None),
        P("row", None, "col"),
        P("col"),
        P("col", "row"),
        P("row"),
        P("row", "col"),
        P("col"),
        P(("dp", "row"), "col"),
    )
    out_specs = (
        P(("dp", "row"), "col"),
        P(("dp", "row"), "col"),
        P("dp", "row"),
        P("row", None, "col", "dp"),
        P(None, "col", "dp"),
        P("col", "dp", "row", None, None),
        P(None, ("row", "col"), "dp"),
        P("row", None, "col", "dp"),
        P("col", "dp"),
        P("col", "row", "dp"),
        P("row", "dp"),
        P("row", "col", "dp"),
        P("col", "dp"),
    )
    body = functools.partial(shards_fn, mesh.shape["dp"])
    return jax.shard_map(body, mesh=mesh, in_specs=in_specs, out_specs=out_specs, check_vma=False)
```

```python
import functools
import math

import jax
import jax.numpy as jnp
from jax import lax
from jax.experimental import pallas as pl
from jax.experimental.pallas import tpu as pltpu
from jax.sharding import PartitionSpec as P

D = 768
HALF = 384
SEQ = 256
HEADS = 6
HD = 64
QKV = HEADS * 3 * HD
FEED = 1536
EPSILON = 1e-06
HIGH = lax.Precision.HIGHEST
F32 = jnp.float32
BF16 = jnp.bfloat16
SWAP = [(0, 1), (1, 0)]
ALPHA = 0.7978845608
CUBIC = 0.044715


def mm(first, second, dims, precision=None):
    return lax.dot_general(
        first, second, ((dims[:1], dims[1:]), ((), ())), precision=precision, preferred_element_type=F32
    )


def call(kernel, outs, inputs, micros, name, after=(), scratch=(), limit=16):
    count = len(after)

    def body(*refs):
        kernel(*refs[count:])

    return pl.pallas_call(
        body if count else kernel,
        out_shape=[jax.ShapeDtypeStruct(s, t) for s, t in outs],
        in_specs=[pl.BlockSpec(memory_space=pl.ANY)] * count
        + [pl.BlockSpec(memory_space=pltpu.VMEM)] * len(inputs),
        out_specs=[pl.BlockSpec(memory_space=pltpu.VMEM)] * len(outs),
        scratch_shapes=list(scratch),
        compiler_params=pltpu.CompilerParams(vmem_limit_bytes=limit * 1024 * 1024),
        cost_estimate=pl.CostEstimate(flops=int(micros * 1.15e9), bytes_accessed=1024, transcendentals=0),
        name=name,
    )(*after, *inputs)


def row_mean(values):
    return jnp.sum(values, axis=1, keepdims=True) * (1.0 / D)


def norm_of(values):
    centred = values - row_mean(values)
    inverse = lax.rsqrt(row_mean(centred * centred) + EPSILON)
    return centred * inverse, inverse


def halves(first, second):
    return jnp.concatenate([first, second], axis=1)


def blocks(step=64):
    return [slice(i, i + step) for i in range(0, SEQ, step)]


def mod_kernel(looked, cosine, sine, weight, part, soft, cond):
    place = lax.broadcasted_iota(jnp.int32, (16, HALF), 0)
    both = looked[...] + jnp.where(lax.axis_index("row") == 0, cosine[...], sine[...])
    cond[...] = both
    values = jnp.where(place == 0, both[0:1, :], jnp.where(place == 1, both[1:2, :], 0.0))
    soft16 = (values / (1.0 + jnp.exp(-values))).astype(BF16)
    soft[...] = soft16.astype(F32)[0:2]
    part[...] = jnp.zeros((16, HALF), F32)
    for k in range(6):
        pair = mm(soft16, weight[k], (1, 0))
        part[k : k + 1, :] = pair[0:1]
        part[8 + k : 9 + k, :] = pair[1:2]


def mix_kernel(part, part_recv, bias, out_bias, down_bias, pair_bias, keep, other):
    total = part[...] + part_recv[...]
    here = lax.axis_index("col") == 0
    shift = bias[...].astype(F32)
    keep[...] = jnp.where(here, total[0:6], total[8:14]) + shift
    other[0:6, :] = jnp.where(here, total[8:14], total[0:6]) + shift
    other[6:8, :] = jnp.zeros((2, HALF), F32)
    other[8:16, :] = jnp.zeros((8, HALF), F32)
    other[8:9, :] = out_bias[...].astype(F32).reshape(1, HALF)
    other[9:10, :] = down_bias[...].astype(F32).reshape(1, HALF)
    for i in range(2):
        for h in range(HEADS // 2):
            spot = (3 * i + h) * HD
            other[10:11, spot : spot + HD] = pair_bias[i, h : h + 1, :].astype(F32)


def pack_kernel(first, second, out):
    out[0:SEQ, :] = first[...]
    out[SEQ : 2 * SEQ, :] = second[...]


def pick_image(own, rows, first, col, second, place):
    same = lax.axis_index("row") == lax.axis_index("col")
    left = jnp.where(same, own[rows, :].astype(F32), first[place, :].astype(F32))
    right = jnp.where(same, col[place, :].astype(F32), second[place, :].astype(F32))
    return halves(left, right)


def norm_kernel(lat_own, cot_own, first, col, second, lat, normal, cot):
    for rows in blocks():
        values = pick_image(lat_own, rows, first, col, second, rows)
        lat[rows, :] = values.astype(BF16)
        normal[rows, :] = norm_of(values)[0]
        later = slice(rows.start + SEQ, rows.stop + SEQ)
        cot[rows, :] = pick_image(cot_own, rows, first, col, second, later).astype(BF16)


def first_kernel(
    normal, keep, other, other_col, qkv_own, qkv_peer, out_own, out_peer,
    mod, bias, normed_own, normed_peer, packed, attended, part,
):
    mods = halves(keep[...], other_col[0:6, :])
    mod[...] = mods
    shift, scale = mods[0:1], 1.0 + mods[1:2]
    for rows in blocks():
        normed = (normal[rows, :] * scale + shift).astype(BF16)
        normed_own[rows, :] = normed[:, :HALF]
        normed_peer[rows, :] = normed[:, HALF:]
    bias[...] = halves(other[8:16, :], other_col[8:16, :])
    place = lax.broadcasted_iota(jnp.int32, (16, SEQ), 0)
    one_hot = (place == 0).astype(BF16)
    mine = lax.axis_index("col")
    front = jnp.where(mine == 0, other[10:11, :], other_col[10:11, :])
    back = jnp.where(mine == 0, other_col[10:11, :], other[10:11, :])
    wide = lax.broadcasted_iota(jnp.int32, (16, 3 * HD), 0)
    for h in range(HEADS):
        rows = slice(h * 192, h * 192 + 192)
        source, spot = (front if h < 3 else back), (h % 3) * HD
        line = jnp.concatenate(
            [source[:, spot : spot + HD], jnp.zeros((1, HD), F32), source[:, 192 + spot : 192 + spot + HD]], axis=1
        )
        full = mm(qkv_own[rows, :], normed_own[...], (1, 1))
        full = full + mm(qkv_peer[rows, :], normed_peer[...], (1, 1))
        full = full + mm(jnp.where(wide == 0, line, 0.0).astype(BF16), one_hot, (0, 0))
        full = full.astype(BF16)
        packed[rows, :] = full
        query, key, value = full[0:64], full[64:128], full[128:192]
        scores = mm(key, query, (0, 0)) * 0.125
        expon = jnp.exp(scores - jnp.max(scores, axis=0, keepdims=True))
        probs = (expon * (1.0 / jnp.sum(expon, axis=0, keepdims=True))).astype(BF16)
        attended[h * 64 : h * 64 + 64, :] = mm(value, probs, (1, 0)).astype(BF16)
    part[:, :HALF] = mm(attended[...], out_own[...], (0, 0)).astype(BF16)
    part[:, HALF:] = mm(attended[...], out_peer[...], (0, 0)).astype(BF16)


def early_kernel(cot, mod, down_own, down_peer, grad_own, grad_peer, grad_active):
    gate = mod[5:6, :]
    for rows in blocks():
        grads = (cot[rows, :].astype(F32) * gate).astype(BF16)
        grad_own[rows, :] = grads[:, :HALF]
        grad_peer[rows, :] = grads[:, HALF:]
    for cols in [slice(j, j + 256) for j in range(0, FEED, 256)]:
        grad_active[:, cols] = mm(grad_own[...], down_own[cols, :], (1, 1)) + mm(
            grad_peer[...], down_peer[cols, :], (1, 1)
        )


def branch(part, part_recv, bias, rows):
    return part[rows, :].astype(F32) + part_recv[rows, :].astype(F32) + bias


def resid_of(lat, mod, bias, part, part_recv, rows):
    gate = mod[2:3, :]
    one = branch(part, part_recv, bias[0:1, :], rows)
    return lat[rows, :].astype(F32) + gate * one, one


def second_kernel(
    lat, mod, bias, part, part_recv, up_own, up_peer, up_bias, grad_active,
    normed_own, active, hidden, part_two,
):
    shift, scale = mod[3:4, :], 1.0 + mod[4:5, :]
    for rows in blocks():
        resid, unused = resid_of(lat, mod, bias, part, part_recv, rows)
        normal, unused = norm_of(resid)
        normed = (normal * scale + shift).astype(BF16)
        normed_own[rows, :] = normed[:, :HALF]
        hidden[rows, FEED:] = normed[:, HALF:]
    shift_up = up_bias[...].astype(F32).reshape(1, FEED)
    for cols in [slice(j, j + 256) for j in range(0, FEED, 256)]:
        pre = mm(normed_own[...], up_own[:, cols], (1, 0)) + mm(hidden[:, FEED:], up_peer[:, cols], (1, 0))
        pre = pre + shift_up[:, cols]
        square = pre * pre
        bend = jnp.tanh(ALPHA * (pre + CUBIC * (pre * square)))
        half = 0.5 * (1.0 + bend)
        active[:, cols] = (pre * half).astype(BF16)
        slope = half + 0.5 * pre * (1.0 - bend * bend) * (ALPHA * (1.0 + (3.0 * CUBIC) * square))
        hidden[:, cols] = (grad_active[:, cols] * slope).astype(BF16)
    part_two[:, :HALF] = mm(hidden[:, :FEED], up_own[...], (1, 1)).astype(BF16)
    part_two[:, HALF:] = mm(hidden[:, :FEED], up_peer[...], (1, 1)).astype(BF16)


def down_kernel(active, cot, down_own, down_peer, part, sums):
    sums[...] = jnp.zeros((8, D), F32)
    for cols, weight in ((slice(0, HALF), down_own), (slice(HALF, D), down_peer)):
        here = mm(active[...], weight[...], (1, 0)).astype(BF16)
        part[:, cols] = here
        sums[0:1, cols] = jnp.sum(here.astype(F32) * cot[:, cols].astype(F32), axis=0, keepdims=True)


def spots(left, bit):
    step = 1 << (len(left) - 1 - left.index(bit))
    return step, [q for q in range(1 << len(left)) if q & step == 0]


def bit_here(bit):
    return lax.rem(lax.div(lax.axis_index("dp"), 1 << bit), 2)


def split_store(full, left, bit, send, keep):
    here = bit_here(bit)
    size = full.shape[0] >> len(left)
    step, places = spots(left, bit)
    for q, place in enumerate(places):
        low = full[place * size : (place + 1) * size]
        high = full[(place + step) * size : (place + step + 1) * size]
        keep[q] = jnp.where(here == 0, low, high).astype(BF16)
        send[q] = jnp.where(here == 0, high, low).astype(BF16)


def tokens(own, recv, axis=0):
    return jnp.concatenate([own[...], recv[...]], axis=axis)


def up_grad_kernel(left, bit, normed, hidden, hidden_recv, send, keep, bias):
    rows = jnp.concatenate([normed[...], hidden_recv[:, FEED:]], axis=0)
    grads = jnp.concatenate([hidden[:, :FEED], hidden_recv[:, :FEED]], axis=0)
    ones = jnp.ones((16, 2 * SEQ), BF16)
    bias[...] = mm(ones, grads, (1, 0))[0:1]
    split_store(mm(grads, rows, (0, 0)), left, bit, send, keep)


def down_grad_kernel(left, bit, grad, grad_recv, active, active_recv, send, keep, bias):
    grads = tokens(grad, grad_recv)
    acts = tokens(active, active_recv)
    ones = jnp.ones((16, 2 * SEQ), BF16)
    bias[...] = mm(ones, grads, (1, 0))[0:1]
    split_store(mm(grads, acts, (0, 0)), left, bit, send, keep)


def third_kernel(
    lat, mod, bias, part, part_recv, grad_two, grad_two_recv, cot, packed, sums,
    qkv_own, qkv_peer, out_own, out_peer,
    grad_resid, grad_own, grad_packed, part_three, grad_peer,
):
    gate, scale = mod[2:3, :], 1.0 + mod[4:5, :]
    for rows in blocks():
        resid, unused = resid_of(lat, mod, bias, part, part_recv, rows)
        normal, inverse = norm_of(resid)
        weighted = (grad_two[rows, :].astype(F32) + grad_two_recv[rows, :].astype(F32)) * scale
        back = inverse * (weighted - row_mean(weighted) - normal * row_mean(weighted * normal))
        grads = cot[rows, :].astype(F32) + back
        grad_resid[rows, :] = grads
        gated = (grads * gate).astype(BF16)
        grad_own[rows, :] = gated[:, :HALF]
        grad_peer[rows, :] = gated[:, HALF:]
    for h in range(HEADS):
        base = h * 192
        query, key = packed[base : base + 64, :], packed[base + 64 : base + 128, :]
        value = packed[base + 128 : base + 192, :]
        wide = slice(h * 64, h * 64 + 64)
        grad_att = mm(out_own[wide, :], grad_own[...], (1, 1)) + mm(out_peer[wide, :], grad_peer[...], (1, 1))
        grad_att = grad_att.astype(BF16)
        scores = mm(key, query, (0, 0)) * 0.125
        expon = jnp.exp(scores - jnp.max(scores, axis=0, keepdims=True))
        probs = expon * (1.0 / jnp.sum(expon, axis=0, keepdims=True))
        grad_probs = mm(value, grad_att, (0, 0))
        total = jnp.sum(probs * grad_probs, axis=0, keepdims=True)
        grad_scores = (probs * (grad_probs - total)).astype(BF16)
        grad_packed[base : base + 64, :] = (mm(key, grad_scores, (1, 0)) * 0.125).astype(BF16)
        grad_packed[base + 64 : base + 128, :] = (mm(query, grad_scores, (1, 1)) * 0.125).astype(BF16)
        grad_packed[base + 128 : base + 192, :] = mm(grad_att, probs.astype(BF16), (1, 1)).astype(BF16)
    grad_packed[QKV:, :] = grad_peer[...].T
    part_three[0:SEQ, :HALF] = mm(grad_packed[0:QKV, :], qkv_own[...], (0, 0)).astype(BF16)
    part_three[0:SEQ, HALF:] = mm(grad_packed[0:QKV, :], qkv_peer[...], (0, 0)).astype(BF16)
    values = sums[0:1, :]
    high = values.astype(BF16).astype(F32)
    middle = (values - high).astype(BF16).astype(F32)
    place = lax.broadcasted_iota(jnp.int32, (16, D), 0)
    terms = jnp.where(place == 0, high, jnp.where(place == 1, middle, jnp.where(place == 2, values - high - middle, 0.0)))
    part_three[SEQ : SEQ + 16, :] = terms.astype(BF16)


def proj_grad_kernel(
    left, bit, normed, normed_recv, packed, packed_recv, grad, attended, attended_recv,
    send, keep, out_bias, pack_bias,
):
    rows = tokens(normed, normed_recv)
    packs = jnp.concatenate([packed[0:QKV, :], packed_recv[0:QKV, :]], axis=1)
    grads = jnp.concatenate([grad[...].T, packed_recv[QKV:, :]], axis=1)
    atts = tokens(attended, attended_recv, 1)
    ones = jnp.ones((16, 2 * SEQ), BF16)
    out_bias[...] = mm(ones, grads, (1, 1))[0:1]
    sums = mm(ones, packs, (1, 1))[0:1]
    pack_bias[...] = jnp.where(lax.axis_index("col") == 0, sums[:, : QKV // 2], sums[:, QKV // 2 :])
    full = halves(mm(rows, packs, (0, 1)), mm(grads, atts, (1, 1)))
    split_store(full, left, bit, send, keep)


def last_kernel(
    lat, mod, bias, part, part_recv, grad_two, grad_two_recv, cot,
    grad_resid, grad_one, grad_one_recv, branch_sums,
    lat_own, lat_peer, mod_own, mod_peer,
):
    scale = 1.0 + mod[1:2, :]
    sums = [jnp.zeros((1, D), F32)] * 6
    for rows in blocks():
        resid, one = resid_of(lat, mod, bias, part, part_recv, rows)
        normal_two, unused = norm_of(resid)
        normal, inverse = norm_of(lat[rows, :].astype(F32))
        normed_grad = grad_one[rows, :].astype(F32) + grad_one_recv[rows, :].astype(F32)
        normed_two = grad_two[rows, :].astype(F32) + grad_two_recv[rows, :].astype(F32)
        resid_grad = grad_resid[rows, :]
        weighted = normed_grad * scale
        back = inverse * (weighted - row_mean(weighted) - normal * row_mean(weighted * normal))
        grads = resid_grad + back
        lat_own[rows, :] = grads[:, :HALF]
        lat_peer[rows, :] = grads[:, HALF:]
        terms = (
            normed_grad,
            normed_grad * normal,
            resid_grad * one,
            normed_two,
            normed_two * normal_two,
            cot[rows, :].astype(F32),
        )
        sums = [s + jnp.sum(t, axis=0, keepdims=True) for s, t in zip(sums, terms)]
    far = grad_one_recv[SEQ : SEQ + 16, :].astype(F32)
    far = far[0:1] + far[1:2] + far[2:3]
    sums[5] = sums[5] * bias[1:2, :] + branch_sums[0:1, :] + far
    for k in range(6):
        mod_own[k : k + 1, :] = sums[k][:, :HALF]
        mod_peer[k : k + 1, :] = sums[k][:, HALF:]


def pick_kernel(own, recv, out):
    out[...] = jnp.where(lax.axis_index("row") == lax.axis_index("col"), own[...], recv[...])


def out_kernel(lat, mod, bias, part, part_recv, part_two, part_two_recv, own, peer):
    for rows in blocks():
        resid, unused = resid_of(lat, mod, bias, part, part_recv, rows)
        two = branch(part_two, part_two_recv, bias[1:2, :], rows)
        result = (resid + mod[5:6, :] * two).astype(BF16)
        own[rows, :] = result[:, :HALF]
        peer[rows, :] = result[:, HALF:]


def payload_kernel(mod_own, mod_recv, soft, up_bias, down_bias, out_bias, pack_bias, weight, payload, part_cond):
    col_index = lax.axis_index("col")
    own, recv = mod_own[...], mod_recv[...]
    zero = jnp.where(col_index == 0, own, recv)
    one = jnp.where(col_index == 0, recv, own)
    payload = payload.at[0]
    payload[...] = jnp.zeros(payload.shape, F32)
    payload[0:6, :] = zero
    payload[6:7, :] = soft[0:1, :]
    payload[8:14, :] = one
    payload[14:15, :] = soft[1:2, :]
    for k in range(4):
        payload[16 + k : 17 + k, :] = up_bias[:, k * HALF : k * HALF + HALF]
    payload[20:21, :] = down_bias[...]
    payload[21:22, :] = out_bias[...]
    payload[22:23, :] = pack_bias[:, :HALF]
    payload[23:24, 0:192] = pack_bias[:, HALF:]
    place = lax.broadcasted_iota(jnp.int32, (16, HALF), 0)
    total = jnp.zeros((16, HALF), F32)
    for k in range(6):
        pair = jnp.where(place == 0, zero[k : k + 1], jnp.where(place == 1, one[k : k + 1], 0.0))
        high = pair.astype(BF16)
        rest = pair - high.astype(F32)
        mid = rest.astype(BF16)
        low = (rest - mid.astype(F32)).astype(BF16)
        for piece in (high, mid, low):
            total = total + mm(piece, weight[k], (1, 1))
    part_cond[...] = total[0:2]


def add_kernel(left, bit, keep, recv, send_next, keep_next):
    here = bit_here(bit)
    step, places = spots(left, bit)
    for q, first in enumerate(places):
        for place, out in ((first + step * here, keep_next), (first + step * (1 - here), send_next)):
            out[q] = (keep[place].astype(F32) + recv[place].astype(F32)).astype(BF16)


def join_kernel(first, second, out):
    count = first.shape[0]
    out[0:count] = first[...]
    out[count : 2 * count] = second[...]


def sum_kernel(up_keep, up_recv, down_keep, down_recv, proj_keep, proj_recv, up, down, qkv, out):
    up[...] = up_keep[0].astype(F32) + up_recv[0].astype(F32)
    down[...] = down_keep[0].astype(F32) + down_recv[0].astype(F32)
    both = proj_keep[0].astype(F32) + proj_recv[0].astype(F32)
    for k in range(3 * HEADS):
        qkv[k] = both[:, k * HD : k * HD + HD]
    for h in range(HEADS):
        out[h] = both[:, QKV + h * HD : QKV + h * HD + HD]


def lanes(values, start, width):
    count = values.shape[1]
    rows = lax.broadcasted_iota(jnp.int32, (count, width), 0)
    columns = lax.broadcasted_iota(jnp.int32, (count, width), 1)
    return mm(values, (rows == columns + start).astype(F32), (1, 0), HIGH)


def mod_sum_kernel(loads, weight, mod_bias, up_bias, down_bias, out_bias, pack_bias, full):
    shards = loads.shape[0]
    width = weight.shape[1]
    dp_index = lax.axis_index("dp")
    part = HALF // shards
    place = dp_index * part if width < HALF else 0
    images = [loads[s, 8 * i : 8 * i + 8, :] for s in range(shards) for i in range(2)]
    soft = jnp.concatenate([image[6:7] for image in images], axis=0)
    for k in range(6):
        rows = jnp.concatenate([image[k : k + 1] for image in images], axis=0)
        full[...] = mm(rows, soft, (0, 0), HIGH)
        weight[k] = full[pl.ds(pl.multiple_of(place, 8), width), :]
    mods, total = images[0] + images[1], loads[0, 16:24, :]
    for s in range(1, shards):
        mods = mods + (images[2 * s] + images[2 * s + 1])
        total = total + loads[s, 16:24, :]
    mod_bias[...] = lanes(mods, dp_index * part, part)[0:6]
    start = dp_index * (4 * part)
    row = lax.div(start, HALF)
    picked = jnp.where(lax.broadcasted_iota(jnp.int32, (8, HALF), 0) == row, total, 0.0)
    up_bias[...] = lanes(jnp.sum(picked, axis=0, keepdims=True), start - row * HALF, 4 * part)
    blocks_here = lanes(total, dp_index * part, part)
    down_bias[...] = blocks_here[4:5]
    out_bias[...] = blocks_here[5:6]
    for i in range(2):
        for h in range(HEADS // 2):
            row, spot = divmod(h * 192 + i * 128, HALF)
            head = total[6 + row : 7 + row, spot : spot + HD]
            pack_bias[i, h : h + 1, :] = lanes(head, dp_index * (HD // shards), HD // shards)


def row_swap(values):
    return lax.ppermute(values, "row", SWAP)


def col_swap(values):
    return lax.ppermute(values, "col", SWAP)


def both_swap(values):
    return lax.ppermute(values, ("row", "col"), [(0, 3), (3, 0), (1, 2), (2, 1)])


def swap_bit(values, bit, dp_size):
    return lax.ppermute(values, "dp", [(p, p ^ (1 << bit)) for p in range(dp_size)])


class Sums:
    def __init__(self, name, order, dp_size):
        self.name, self.order, self.dp_size = name, order, dp_size
        self.left, self.step = tuple(sorted(order, reverse=True)), 0

    def begin(self, send, keep):
        self.keep, self.recv = keep, swap_bit(send, self.order[0], self.dp_size)

    def advance(self, after):
        if self.step + 1 >= len(self.order):
            return after[0]
        self.left = tuple(b for b in self.left if b != self.order[self.step])
        self.step += 1
        bit = self.order[self.step]
        shape = (self.keep.shape[0] // 2,) + self.keep.shape[1:]
        kernel = functools.partial(add_kernel, self.left, bit)
        send, keep = call(kernel, [(shape, BF16)] * 2, [self.keep, self.recv], 6, self.name, after)
        self.begin_next(send, keep)
        return keep

    def begin_next(self, send, keep):
        self.keep, self.recv = keep, swap_bit(send, self.order[self.step], self.dp_size)


def shards_fn(
    dp_size,
    latents,
    labels,
    timesteps,
    class_table,
    mod_weight,
    mod_bias,
    qkv_weight,
    query_value_bias,
    out_weight,
    out_bias,
    up_weight,
    up_bias,
    down_weight,
    down_bias,
    cotangent,
):
    bits = dp_size.bit_length() - 1
    wide = (SEQ, D)
    slim = (SEQ, HALF)
    pieces = dp_size // 2
    rows_down, rows_up = HALF // dp_size, FEED // dp_size
    every = tuple(range(bits))
    left = every[::-1]
    up = Sums("up_add", every[1:] + every[:1], dp_size)
    down = Sums("down_add", every, dp_size)
    proj = Sums("proj_add", every, dp_size)
    change = [(1, 2), (2, 1)]
    (pair,) = call(pack_kernel, [((2 * SEQ, HALF), BF16)], [latents, cotangent], 0.4, "pack")
    pair_col = col_swap(pair)
    pair_second = lax.ppermute(pair, ("row", "col"), change)
    pair_first = lax.ppermute(pair_col, ("row", "col"), change)
    inputs = [latents, cotangent, pair_first, pair_col, pair_second]
    qkv_own = jnp.transpose(qkv_weight, (1, 2, 3, 0)).reshape(QKV, HALF)
    out_own = out_weight.reshape(HALF, HALF)
    qkv_peer, out_peer = col_swap(qkv_own), col_swap(out_own)

    classes = class_table.shape[0]
    picks = (labels[:, None] == jnp.arange(classes, dtype=jnp.int32)[None, :]).astype(BF16)
    looked = jnp.dot(picks, class_table, preferred_element_type=F32)
    frequency = jnp.exp(-math.log(10000.0) * jnp.arange(HALF, dtype=F32) / HALF)
    angles = timesteps.astype(F32)[:, None] * frequency[None, :]
    mod_rows = jnp.transpose(mod_weight, (1, 0, 2))
    mod_part, soft, cond = call(
        mod_kernel,
        [((16, HALF), F32), ((2, HALF), F32), ((2, HALF), F32)],
        [looked, jnp.cos(angles), jnp.sin(angles), mod_rows],
        20,
        "mod",
        [pair_col, qkv_peer, out_peer],
    )
    late = lax.optimization_barrier((up_weight, down_weight, mod_part))
    up_weight, down_weight, mod_part = late
    mod_part_recv = row_swap(mod_part)
    keep, other = call(
        mix_kernel,
        [((6, HALF), F32), ((16, HALF), F32)],
        [mod_part, mod_part_recv, mod_bias, out_bias, down_bias, query_value_bias],
        0.3,
        "mix",
    )
    other_col = col_swap(other)
    lat, normal, cot = call(
        norm_kernel, [(wide, BF16), (wide, F32), (wide, BF16)], [*inputs], 1.5, "norm", [keep]
    )
    down_peer, up_peer = col_swap(down_weight), col_swap(up_weight)
    mod, bias, normed_own, normed_peer, packed, attended, part_one = call(
        first_kernel,
        [((6, D), F32), ((8, D), F32), (slim, BF16), (slim, BF16), ((QKV, SEQ), BF16), ((HALF, SEQ), BF16), (wide, BF16)],
        [normal, keep, other, other_col, qkv_own, qkv_peer, out_own, out_peer],
        5,
        "first",
    )
    part_one_recv = row_swap(part_one)
    two_grad_own, two_grad_peer, grad_active = call(
        early_kernel,
        [(slim, BF16), (slim, BF16), ((SEQ, FEED), F32)],
        [cot, mod, down_weight, down_peer],
        1,
        "early",
        [part_one],
    )
    normed_recv, attended_recv = col_swap(normed_peer), col_swap(attended)
    two_grad_recv = col_swap(two_grad_peer)
    resid_args = [lat, mod, bias, part_one, part_one_recv]
    second_own, active, hidden, part_two = call(
        second_kernel,
        [(slim, BF16), ((SEQ, FEED), BF16), ((SEQ, FEED + HALF), BF16), (wide, BF16)],
        [*resid_args, up_weight, up_peer, up_bias, grad_active],
        4,
        "second",
        [normed_recv, attended_recv, two_grad_recv],
    )
    part_two_recv = row_swap(part_two)
    active_recv, hidden_recv = col_swap(active), col_swap(hidden)
    branch_part, branch_sums = call(
        down_kernel, [(wide, BF16), ((8, D), F32)], [active, cot, down_weight, down_peer], 1, "down"
    )
    branch_recv = lax.ppermute(branch_part, ("row", "col"), [(1, 3), (2, 0)])
    down_send, down_keep, down_sum = call(
        functools.partial(down_grad_kernel, left, down.order[0]),
        [((pieces, rows_down, FEED), BF16), ((pieces, rows_down, FEED), BF16), ((1, HALF), F32)],
        [two_grad_own, two_grad_recv, active, active_recv],
        0.9,
        "down_grad",
        [branch_part],
    )
    down.begin(down_send, down_keep)
    up_send, up_keep, up_sum = call(
        functools.partial(up_grad_kernel, left, up.order[0]),
        [((pieces, rows_up, HALF), BF16), ((pieces, rows_up, HALF), BF16), ((1, FEED), F32)],
        [second_own, hidden, hidden_recv],
        1.2,
        "up_grad",
        [down_send],
    )
    up.begin(up_send, up_keep)
    grad_resid, one_grad_own, grad_packed, part_three = call(
        third_kernel,
        [(wide, F32), (slim, BF16), ((QKV + HALF, SEQ), BF16), ((SEQ + 16, D), BF16)],
        [*resid_args, part_two, part_two_recv, cot, packed, branch_sums, qkv_own, qkv_peer, out_own, out_peer],
        20,
        "third",
        [up_send],
        [pltpu.VMEM(slim, BF16)],
    )
    part_three_recv = row_swap(part_three)
    packed_recv = col_swap(grad_packed)
    token = down.advance([part_three])
    token = up.advance([token])
    proj_send, proj_keep, out_sum, pack_sum = call(
        functools.partial(proj_grad_kernel, left, proj.order[0]),
        [((pieces, rows_down, FEED), BF16), ((pieces, rows_down, FEED), BF16), ((1, HALF), F32), ((1, QKV // 2), F32)],
        [normed_own, normed_recv, grad_packed, packed_recv, one_grad_own, attended, attended_recv],
        1.3,
        "proj_grad",
        [token],
    )
    proj.begin(proj_send, proj_keep)
    token = proj_send
    lat_grad_own, lat_grad_peer, mod_own, mod_peer = call(
        last_kernel,
        [(slim, F32), (slim, F32), ((6, HALF), F32), ((6, HALF), F32)],
        [*resid_args, part_two, part_two_recv, cot, grad_resid, part_three, part_three_recv, branch_sums],
        20,
        "last",
        [token],
    )
    mod_recv = col_swap(mod_peer)
    token = down.advance([mod_own])
    token = up.advance([token])
    token = proj.advance([token])
    payload, part_cond = call(
        payload_kernel,
        [((1, 24, HALF), F32), ((2, HALF), F32)],
        [mod_own, mod_recv, soft, up_sum, down_sum, out_sum, pack_sum, mod_rows],
        1.6,
        "payload",
        [token],
    )
    part_cond_recv = col_swap(part_cond)
    lat_recv = col_swap(lax.optimization_barrier((lat_grad_peer, payload))[0])
    result_own, result_peer = call(
        out_kernel,
        [(slim, BF16), (slim, BF16)],
        [*resid_args, branch_part, branch_recv],
        1,
        "out",
        [payload],
    )
    result_recv = col_swap(result_peer)
    token = result_own
    for step, bit in enumerate(every[1:] + every[:1]):
        recv = swap_bit(payload, bit, dp_size)
        for part in (([], [proj], [])[step] if step < 3 else [up, down, proj]):
            token = part.advance([token])
        (payload,) = call(join_kernel, [((2 << step, 24, HALF), F32)], [payload, recv], 1, "join", [token])
        token = payload
    width = HALF // dp_size
    mod_grad, mod_bias_grad, up_bias_grad, down_bias_grad, out_bias_grad, pack_grad = call(
        mod_sum_kernel,
        [
            ((6, width if width % 8 == 0 else HALF, HALF), F32),
            ((6, width), F32),
            ((1, rows_up), F32),
            ((1, width), F32),
            ((1, width), F32),
            ((2, HEADS // 2, HD // dp_size), F32),
        ],
        [payload],
        20,
        "mod_sum",
        scratch=[pltpu.VMEM((HALF, HALF), F32)],
    )
    (output,) = call(pick_kernel, [(slim, BF16)], [result_own, result_recv], 0.4, "pick")
    (grad_latents,) = call(pick_kernel, [(slim, F32)], [lat_grad_own, lat_recv], 0.4, "pick")
    grad_soft = part_cond + part_cond_recv
    unused, silu_back = jax.vjp(jax.nn.silu, cond)
    grad_cond = silu_back(grad_soft)[0]
    while min(part.step for part in (up, down, proj)) + 1 < bits:
        for part in (up, down, proj):
            token = part.advance([token])
    sums = [up.keep, up.recv, down.keep, down.recv, proj.keep, proj.recv]
    up_grad, down_grad, qkv_grad, out_grad = call(
        sum_kernel,
        [((rows_up, HALF), F32), ((rows_down, FEED), F32), ((3 * HEADS, rows_down, HD), F32), ((HEADS, rows_down, HD), F32)],
        sums,
        1.5,
        "sum",
    )
    if width % 8 > 0:
        mod_grad = lax.dynamic_slice_in_dim(mod_grad, lax.axis_index("dp") * width, width, 1)
    return (
        output,
        grad_latents,
        grad_cond,
        jnp.transpose(mod_grad, (2, 0, 1))[:, :, None, :],
        mod_bias_grad[:, None, :],
        jnp.transpose(qkv_grad.reshape(HEADS, 3, rows_down, HD), (2, 0, 1, 3))[None],
        pack_grad,
        jnp.transpose(out_grad, (0, 2, 1))[:, :, None, :],
        out_bias_grad,
        jnp.transpose(up_grad)[:, None, :],
        up_bias_grad,
        jnp.transpose(down_grad)[:, None, :],
        down_bias_grad,
    )


def solution(mesh):
    in_specs = (
        P(("dp", "row"), "col"),
        P("dp"),
        P("dp"),
        P(None, "row"),
        P("row", None, "col"),
        P(None, "col"),
        P("col", "row", None, None),
        P(None, ("row", "col"), None),
        P("row", None, "col"),
        P("col"),
        P("col", "row"),
        P("row"),
        P("row", "col"),
        P("col"),
        P(("dp", "row"), "col"),
    )
    out_specs = (
        P(("dp", "row"), "col"),
        P(("dp", "row"), "col"),
        P("dp", "row"),
        P("row", None, "col", "dp"),
        P(None, "col", "dp"),
        P("col", "dp", "row", None, None),
        P(None, ("row", "col"), "dp"),
        P("row", None, "col", "dp"),
        P("col", "dp"),
        P("col", "row", "dp"),
        P("row", "dp"),
        P("row", "col", "dp"),
        P("col", "dp"),
    )
    body = functools.partial(shards_fn, mesh.shape["dp"])
    return jax.shard_map(body, mesh=mesh, in_specs=in_specs, out_specs=out_specs, check_vma=False)
```

```python
import functools
import math

import jax
import jax.numpy as jnp
from jax import lax
from jax.experimental import pallas as pl
from jax.experimental.pallas import tpu as pltpu
from jax.sharding import PartitionSpec as P

D = 768
HALF = 384
SEQ = 256
HEADS = 6
HD = 64
QKV = HEADS * 3 * HD
FEED = 1536
EPSILON = 1e-06
HIGH = lax.Precision.HIGHEST
F32 = jnp.float32
BF16 = jnp.bfloat16
SWAP = [(0, 1), (1, 0)]
ALPHA = 0.7978845608
CUBIC = 0.044715


def mm(first, second, dims, precision=None):
    return lax.dot_general(
        first, second, ((dims[:1], dims[1:]), ((), ())), precision=precision, preferred_element_type=F32
    )


def call(kernel, outs, inputs, micros, name, after=(), scratch=(), limit=16):
    count = len(after)

    def body(*refs):
        kernel(*refs[count:])

    return pl.pallas_call(
        body if count else kernel,
        out_shape=[jax.ShapeDtypeStruct(s, t) for s, t in outs],
        in_specs=[pl.BlockSpec(memory_space=pl.ANY)] * count
        + [pl.BlockSpec(memory_space=pltpu.VMEM)] * len(inputs),
        out_specs=[pl.BlockSpec(memory_space=pltpu.VMEM)] * len(outs),
        scratch_shapes=list(scratch),
        compiler_params=pltpu.CompilerParams(vmem_limit_bytes=limit * 1024 * 1024),
        cost_estimate=pl.CostEstimate(flops=int(micros * 1.15e9), bytes_accessed=1024, transcendentals=0),
        name=name,
    )(*after, *inputs)


def row_mean(values):
    return jnp.sum(values, axis=1, keepdims=True) * (1.0 / D)


def norm_of(values):
    centred = values - row_mean(values)
    inverse = lax.rsqrt(row_mean(centred * centred) + EPSILON)
    return centred * inverse, inverse


def halves(first, second):
    return jnp.concatenate([first, second], axis=1)


def blocks(step=64):
    return [slice(i, i + step) for i in range(0, SEQ, step)]


def mod_kernel(looked, cosine, sine, weight, part, soft, cond):
    place = lax.broadcasted_iota(jnp.int32, (16, HALF), 0)
    both = looked[...] + jnp.where(lax.axis_index("row") == 0, cosine[...], sine[...])
    cond[...] = both
    values = jnp.where(place == 0, both[0:1, :], jnp.where(place == 1, both[1:2, :], 0.0))
    soft16 = (values / (1.0 + jnp.exp(-values))).astype(BF16)
    soft[...] = soft16.astype(F32)[0:2]
    part[...] = jnp.zeros((16, HALF), F32)
    for k in range(6):
        pair = mm(soft16, weight[k], (1, 0))
        part[k : k + 1, :] = pair[0:1]
        part[8 + k : 9 + k, :] = pair[1:2]


def mix_kernel(part, part_recv, bias, out_bias, down_bias, pair_bias, keep, other):
    total = part[...] + part_recv[...]
    here = lax.axis_index("col") == 0
    shift = bias[...].astype(F32)
    keep[...] = jnp.where(here, total[0:6], total[8:14]) + shift
    other[0:6, :] = jnp.where(here, total[8:14], total[0:6]) + shift
    other[6:8, :] = jnp.zeros((2, HALF), F32)
    other[8:16, :] = jnp.zeros((8, HALF), F32)
    other[8:9, :] = out_bias[...].astype(F32).reshape(1, HALF)
    other[9:10, :] = down_bias[...].astype(F32).reshape(1, HALF)
    for i in range(2):
        for h in range(HEADS // 2):
            spot = (3 * i + h) * HD
            other[10:11, spot : spot + HD] = pair_bias[i, h : h + 1, :].astype(F32)


def pack_kernel(first, second, out):
    out[0:SEQ, :] = first[...]
    out[SEQ : 2 * SEQ, :] = second[...]


def pick_image(own, col, change, rows):
    same = lax.axis_index("row") == lax.axis_index("col")
    later = slice(rows.start + SEQ, rows.stop + SEQ)
    left = jnp.where(same, own[rows, :].astype(F32), change[later, :].astype(F32))
    right = jnp.where(same, col[rows, :].astype(F32), change[rows, :].astype(F32))
    return halves(left, right)


def norm_kernel(own, col, change, lat, normal):
    for rows in blocks():
        values = pick_image(own, col, change, rows)
        lat[rows, :] = values.astype(BF16)
        normal[rows, :] = norm_of(values)[0]


def first_kernel(
    normal, keep, other, other_col, qkv_own, qkv_peer, out_own, out_peer,
    mod, bias, normed_own, normed_peer, packed, attended, part,
):
    mods = halves(keep[...], other_col[0:6, :])
    mod[...] = mods
    shift, scale = mods[0:1], 1.0 + mods[1:2]
    for rows in blocks():
        normed = (normal[rows, :] * scale + shift).astype(BF16)
        normed_own[rows, :] = normed[:, :HALF]
        normed_peer[rows, :] = normed[:, HALF:]
    bias[...] = halves(other[8:16, :], other_col[8:16, :])
    place = lax.broadcasted_iota(jnp.int32, (16, SEQ), 0)
    one_hot = (place == 0).astype(BF16)
    mine = lax.axis_index("col")
    front = jnp.where(mine == 0, other[10:11, :], other_col[10:11, :])
    back = jnp.where(mine == 0, other_col[10:11, :], other[10:11, :])
    wide = lax.broadcasted_iota(jnp.int32, (16, 3 * HD), 0)
    for h in range(HEADS):
        rows = slice(h * 192, h * 192 + 192)
        source, spot = (front if h < 3 else back), (h % 3) * HD
        line = jnp.concatenate(
            [source[:, spot : spot + HD], jnp.zeros((1, HD), F32), source[:, 192 + spot : 192 + spot + HD]], axis=1
        )
        full = mm(qkv_own[rows, :], normed_own[...], (1, 1))
        full = full + mm(qkv_peer[rows, :], normed_peer[...], (1, 1))
        full = full + mm(jnp.where(wide == 0, line, 0.0).astype(BF16), one_hot, (0, 0))
        full = full.astype(BF16)
        packed[rows, :] = full
        query, key, value = full[0:64], full[64:128], full[128:192]
        scores = mm(key, query, (0, 0)) * 0.125
        expon = jnp.exp(scores - jnp.max(scores, axis=0, keepdims=True))
        probs = (expon * (1.0 / jnp.sum(expon, axis=0, keepdims=True))).astype(BF16)
        attended[h * 64 : h * 64 + 64, :] = mm(value, probs, (1, 0)).astype(BF16)
    part[:, :HALF] = mm(attended[...], out_own[...], (0, 0)).astype(BF16)
    part[:, HALF:] = mm(attended[...], out_peer[...], (0, 0)).astype(BF16)


def early_kernel(own, col, change, mod, down_own, down_peer, cot, grad_own, grad_peer, grad_active):
    gate = mod[5:6, :]
    for rows in blocks():
        values = pick_image(own, col, change, rows)
        cot[rows, :] = values.astype(BF16)
        grads = (values * gate).astype(BF16)
        grad_own[rows, :] = grads[:, :HALF]
        grad_peer[rows, :] = grads[:, HALF:]
    for cols in [slice(j, j + 256) for j in range(0, FEED, 256)]:
        grad_active[:, cols] = mm(grad_own[...], down_own[cols, :], (1, 1)) + mm(
            grad_peer[...], down_peer[cols, :], (1, 1)
        )


def branch(part, part_recv, bias, rows):
    return part[rows, :].astype(F32) + part_recv[rows, :].astype(F32) + bias


def resid_of(lat, mod, bias, part, part_recv, rows):
    gate = mod[2:3, :]
    one = branch(part, part_recv, bias[0:1, :], rows)
    return lat[rows, :].astype(F32) + gate * one, one


def second_kernel(
    lat, mod, bias, part, part_recv, up_own, up_peer, up_bias, grad_active,
    normed_own, active, hidden, part_two,
):
    shift, scale = mod[3:4, :], 1.0 + mod[4:5, :]
    for rows in blocks():
        resid, unused = resid_of(lat, mod, bias, part, part_recv, rows)
        normal, unused = norm_of(resid)
        normed = (normal * scale + shift).astype(BF16)
        normed_own[rows, :] = normed[:, :HALF]
        hidden[rows, FEED:] = normed[:, HALF:]
    shift_up = up_bias[...].astype(F32).reshape(1, FEED)
    for cols in [slice(j, j + 256) for j in range(0, FEED, 256)]:
        pre = mm(normed_own[...], up_own[:, cols], (1, 0)) + mm(hidden[:, FEED:], up_peer[:, cols], (1, 0))
        pre = pre + shift_up[:, cols]
        square = pre * pre
        bend = jnp.tanh(ALPHA * (pre + CUBIC * (pre * square)))
        half = 0.5 * (1.0 + bend)
        active[:, cols] = (pre * half).astype(BF16)
        slope = half + 0.5 * pre * (1.0 - bend * bend) * (ALPHA * (1.0 + (3.0 * CUBIC) * square))
        hidden[:, cols] = (grad_active[:, cols] * slope).astype(BF16)
    part_two[:, :HALF] = mm(hidden[:, :FEED], up_own[...], (1, 1)).astype(BF16)
    part_two[:, HALF:] = mm(hidden[:, :FEED], up_peer[...], (1, 1)).astype(BF16)


def down_kernel(active, cot, down_own, down_peer, part, sums):
    sums[...] = jnp.zeros((8, D), F32)
    for cols, weight in ((slice(0, HALF), down_own), (slice(HALF, D), down_peer)):
        here = mm(active[...], weight[...], (1, 0)).astype(BF16)
        part[:, cols] = here
        sums[0:1, cols] = jnp.sum(here.astype(F32) * cot[:, cols].astype(F32), axis=0, keepdims=True)


def spots(left, bit):
    step = 1 << (len(left) - 1 - left.index(bit))
    return step, [q for q in range(1 << len(left)) if q & step == 0]


def bit_here(bit):
    return lax.rem(lax.div(lax.axis_index("dp"), 1 << bit), 2)


def split_store(full, left, bit, send, keep):
    here = bit_here(bit)
    size = full.shape[0] >> len(left)
    step, places = spots(left, bit)
    for q, place in enumerate(places):
        low = full[place * size : (place + 1) * size]
        high = full[(place + step) * size : (place + step + 1) * size]
        keep[q] = jnp.where(here == 0, low, high).astype(BF16)
        send[q] = jnp.where(here == 0, high, low).astype(BF16)


def tokens(own, recv, axis=0):
    return jnp.concatenate([own[...], recv[...]], axis=axis)


def up_grad_kernel(left, bit, normed, hidden, hidden_recv, send, keep, bias):
    rows = jnp.concatenate([normed[...], hidden_recv[:, FEED:]], axis=0)
    grads = jnp.concatenate([hidden[:, :FEED], hidden_recv[:, :FEED]], axis=0)
    ones = jnp.ones((16, 2 * SEQ), BF16)
    bias[...] = mm(ones, grads, (1, 0))[0:1]
    split_store(mm(grads, rows, (0, 0)), left, bit, send, keep)


def down_grad_kernel(left, bit, grad, grad_recv, active, active_recv, send, keep, bias):
    grads = tokens(grad, grad_recv)
    acts = tokens(active, active_recv)
    ones = jnp.ones((16, 2 * SEQ), BF16)
    bias[...] = mm(ones, grads, (1, 0))[0:1]
    split_store(mm(grads, acts, (0, 0)), left, bit, send, keep)


def third_kernel(
    lat, mod, bias, part, part_recv, grad_two, grad_two_recv, cot, packed, sums,
    qkv_own, qkv_peer, out_own, out_peer,
    grad_resid, grad_own, grad_packed, part_three, grad_peer,
):
    gate, scale = mod[2:3, :], 1.0 + mod[4:5, :]
    for rows in blocks():
        resid, unused = resid_of(lat, mod, bias, part, part_recv, rows)
        normal, inverse = norm_of(resid)
        weighted = (grad_two[rows, :].astype(F32) + grad_two_recv[rows, :].astype(F32)) * scale
        back = inverse * (weighted - row_mean(weighted) - normal * row_mean(weighted * normal))
        grads = cot[rows, :].astype(F32) + back
        grad_resid[rows, :] = grads
        gated = (grads * gate).astype(BF16)
        grad_own[rows, :] = gated[:, :HALF]
        grad_peer[rows, :] = gated[:, HALF:]
    for h in range(HEADS):
        base = h * 192
        query, key = packed[base : base + 64, :], packed[base + 64 : base + 128, :]
        value = packed[base + 128 : base + 192, :]
        wide = slice(h * 64, h * 64 + 64)
        grad_att = mm(out_own[wide, :], grad_own[...], (1, 1)) + mm(out_peer[wide, :], grad_peer[...], (1, 1))
        grad_att = grad_att.astype(BF16)
        scores = mm(key, query, (0, 0)) * 0.125
        expon = jnp.exp(scores - jnp.max(scores, axis=0, keepdims=True))
        probs = expon * (1.0 / jnp.sum(expon, axis=0, keepdims=True))
        grad_probs = mm(value, grad_att, (0, 0))
        total = jnp.sum(probs * grad_probs, axis=0, keepdims=True)
        grad_scores = (probs * (grad_probs - total)).astype(BF16)
        grad_packed[base : base + 64, :] = (mm(key, grad_scores, (1, 0)) * 0.125).astype(BF16)
        grad_packed[base + 64 : base + 128, :] = (mm(query, grad_scores, (1, 1)) * 0.125).astype(BF16)
        grad_packed[base + 128 : base + 192, :] = mm(grad_att, probs.astype(BF16), (1, 1)).astype(BF16)
    grad_packed[QKV:, :] = grad_peer[...].T
    part_three[0:SEQ, :HALF] = mm(grad_packed[0:QKV, :], qkv_own[...], (0, 0)).astype(BF16)
    part_three[0:SEQ, HALF:] = mm(grad_packed[0:QKV, :], qkv_peer[...], (0, 0)).astype(BF16)
    values = sums[0:1, :]
    high = values.astype(BF16).astype(F32)
    middle = (values - high).astype(BF16).astype(F32)
    place = lax.broadcasted_iota(jnp.int32, (16, D), 0)
    terms = jnp.where(place == 0, high, jnp.where(place == 1, middle, jnp.where(place == 2, values - high - middle, 0.0)))
    part_three[SEQ : SEQ + 16, :] = terms.astype(BF16)


def proj_grad_kernel(
    left, bit, normed, normed_recv, packed, packed_recv, grad, attended, attended_recv,
    send, keep, out_bias, pack_bias,
):
    rows = tokens(normed, normed_recv)
    packs = jnp.concatenate([packed[0:QKV, :], packed_recv[0:QKV, :]], axis=1)
    grads = jnp.concatenate([grad[...].T, packed_recv[QKV:, :]], axis=1)
    atts = tokens(attended, attended_recv, 1)
    ones = jnp.ones((16, 2 * SEQ), BF16)
    out_bias[...] = mm(ones, grads, (1, 1))[0:1]
    sums = mm(ones, packs, (1, 1))[0:1]
    pack_bias[...] = jnp.where(lax.axis_index("col") == 0, sums[:, : QKV // 2], sums[:, QKV // 2 :])
    full = halves(mm(rows, packs, (0, 1)), mm(grads, atts, (1, 1)))
    split_store(full, left, bit, send, keep)


def last_kernel(
    lat, mod, bias, part, part_recv, grad_two, grad_two_recv, cot,
    grad_resid, grad_one, grad_one_recv, branch_sums,
    lat_own, lat_peer, mod_own, mod_peer,
):
    scale = 1.0 + mod[1:2, :]
    sums = [jnp.zeros((1, D), F32)] * 6
    for rows in blocks():
        resid, one = resid_of(lat, mod, bias, part, part_recv, rows)
        normal_two, unused = norm_of(resid)
        normal, inverse = norm_of(lat[rows, :].astype(F32))
        normed_grad = grad_one[rows, :].astype(F32) + grad_one_recv[rows, :].astype(F32)
        normed_two = grad_two[rows, :].astype(F32) + grad_two_recv[rows, :].astype(F32)
        resid_grad = grad_resid[rows, :]
        weighted = normed_grad * scale
        back = inverse * (weighted - row_mean(weighted) - normal * row_mean(weighted * normal))
        grads = resid_grad + back
        lat_own[rows, :] = grads[:, :HALF]
        lat_peer[rows, :] = grads[:, HALF:]
        terms = (
            normed_grad,
            normed_grad * normal,
            resid_grad * one,
            normed_two,
            normed_two * normal_two,
            cot[rows, :].astype(F32),
        )
        sums = [s + jnp.sum(t, axis=0, keepdims=True) for s, t in zip(sums, terms)]
    far = grad_one_recv[SEQ : SEQ + 16, :].astype(F32)
    far = far[0:1] + far[1:2] + far[2:3]
    sums[5] = sums[5] * bias[1:2, :] + branch_sums[0:1, :] + far
    for k in range(6):
        mod_own[k : k + 1, :] = sums[k][:, :HALF]
        mod_peer[k : k + 1, :] = sums[k][:, HALF:]


def out_kernel(lat, mod, bias, part, part_recv, part_two, part_two_recv, own, peer):
    for rows in blocks():
        resid, unused = resid_of(lat, mod, bias, part, part_recv, rows)
        two = branch(part_two, part_two_recv, bias[1:2, :], rows)
        result = (resid + mod[5:6, :] * two).astype(BF16)
        own[rows, :] = result[:, :HALF]
        peer[rows, :] = result[:, HALF:]


def payload_kernel(mod_own, mod_recv, soft, up_bias, down_bias, out_bias, pack_bias, payload):
    payload = payload.at[0]
    col_index = lax.axis_index("col")
    own, recv = mod_own[...], mod_recv[...]
    payload[...] = jnp.zeros(payload.shape, F32)
    payload[0:6, :] = jnp.where(col_index == 0, own, recv)
    payload[6:7, :] = soft[0:1, :]
    payload[8:14, :] = jnp.where(col_index == 0, recv, own)
    payload[14:15, :] = soft[1:2, :]
    for k in range(4):
        payload[16 + k : 17 + k, :] = up_bias[:, k * HALF : k * HALF + HALF]
    payload[20:21, :] = down_bias[...]
    payload[21:22, :] = out_bias[...]
    payload[22:23, :] = pack_bias[:, :HALF]
    payload[23:24, 0:192] = pack_bias[:, HALF:]


def cond_kernel(mod_own, mod_recv, weight, part_cond, mark):
    col_index = lax.axis_index("col")
    own, recv = mod_own[...], mod_recv[...]
    zero = jnp.where(col_index == 0, own, recv)
    one = jnp.where(col_index == 0, recv, own)
    place = lax.broadcasted_iota(jnp.int32, (16, HALF), 0)
    total = jnp.zeros((16, HALF), F32)
    for k in range(6):
        terms = jnp.zeros((16, HALF), F32)
        for i, row in enumerate((zero[k : k + 1], one[k : k + 1])):
            high = row.astype(BF16).astype(F32)
            middle = (row - high).astype(BF16).astype(F32)
            low = row - high - middle
            for j, term in enumerate((high, middle, low)):
                terms = jnp.where(place == 3 * i + j, term, terms)
        total = total + mm(terms.astype(BF16), weight[k], (1, 1))
    part_cond[0:1, :] = total[0:1] + total[1:2] + total[2:3]
    part_cond[1:2, :] = total[3:4] + total[4:5] + total[5:6]
    mark[...] = jnp.zeros(mark.shape, F32)


def finish_kernel(out_own, out_recv, lat_own, lat_recv, cond, part, part_recv, out, lat, grad_cond, mark):
    mark[...] = jnp.zeros(mark.shape, F32)
    same = lax.axis_index("row") == lax.axis_index("col")
    out[...] = jnp.where(same, out_own[...], out_recv[...])
    lat[...] = jnp.where(same, lat_own[...], lat_recv[...])
    values = cond[...]
    gate = 1.0 / (1.0 + jnp.exp(-values))
    grad_cond[...] = (part[...] + part_recv[...]) * (gate * (1.0 + values * (1.0 - gate)))


def add_kernel(left, bit, keep, recv, send_next, keep_next):
    here = bit_here(bit)
    step, places = spots(left, bit)
    for q, first in enumerate(places):
        for place, out in ((first + step * here, keep_next), (first + step * (1 - here), send_next)):
            out[q] = (keep[place].astype(F32) + recv[place].astype(F32)).astype(BF16)


def join_kernel(first, second, out):
    count = first.shape[0]
    out[0:count] = first[...]
    out[count : 2 * count] = second[...]


def sum_kernel(keep, recv, out, mark):
    out[...] = keep[0].astype(F32) + recv[0].astype(F32)
    mark[...] = jnp.zeros(mark.shape, F32)


def proj_sum_kernel(keep, recv, qkv, out):
    both = keep[0].astype(F32) + recv[0].astype(F32)
    for k in range(3 * HEADS):
        qkv[k] = both[:, k * HD : k * HD + HD]
    for h in range(HEADS):
        out[h] = both[:, QKV + h * HD : QKV + h * HD + HD]


def lanes(values, start, width):
    count = values.shape[1]
    rows = lax.broadcasted_iota(jnp.int32, (count, width), 0)
    columns = lax.broadcasted_iota(jnp.int32, (count, width), 1)
    return mm(values, (rows == columns + start).astype(F32), (1, 0), HIGH)


def mod_sum_kernel(loads, weight, mod_bias, up_bias, down_bias, out_bias, pack_bias, mark):
    shards = loads.shape[0]
    dp_index = lax.axis_index("dp")
    part = HALF // shards
    count = 2 * shards
    images = [loads[s, 8 * i : 8 * i + 8, :] for s in range(shards) for i in range(2)]
    soft = jnp.concatenate([image[6:7] for image in images], axis=0)
    rows = jnp.concatenate([image[k : k + 1] for k in range(6) for image in images], axis=0)
    rows = lanes(rows, dp_index * part, part)
    for k in range(6):
        here = rows[k * count : (k + 1) * count]
        mod_bias[k] = jnp.sum(here, axis=0, keepdims=True)
        weight[k] = mm(here, soft, (0, 0), HIGH)
    total = loads[0, 16:24, :]
    for s in range(1, shards):
        total = total + loads[s, 16:24, :]
    start = dp_index * (4 * part)
    row = lax.div(start, HALF)
    picked = jnp.where(lax.broadcasted_iota(jnp.int32, (8, HALF), 0) == row, total, 0.0)
    up_bias[...] = lanes(jnp.sum(picked, axis=0, keepdims=True), start - row * HALF, 4 * part)
    blocks_here = lanes(total, dp_index * part, part)
    down_bias[...] = blocks_here[4:5]
    out_bias[...] = blocks_here[5:6]
    heads = []
    for h in range(HEADS // 2):
        for i in range(2):
            row, spot = divmod(h * 192 + i * 128, HALF)
            heads.append(total[6 + row : 7 + row, spot : spot + HD])
    heads = lanes(jnp.concatenate(heads, axis=0), dp_index * (HD // shards), HD // shards)
    for h in range(HEADS // 2):
        pack_bias[h] = heads[2 * h : 2 * h + 2]
    mark[...] = jnp.zeros(mark.shape, F32)


def row_swap(values):
    return lax.ppermute(values, "row", SWAP)


def col_swap(values):
    return lax.ppermute(values, "col", SWAP)


def both_swap(values):
    return lax.ppermute(values, ("row", "col"), [(0, 3), (3, 0), (1, 2), (2, 1)])


def swap_bit(values, bit, dp_size):
    return lax.ppermute(values, "dp", [(p, p ^ (1 << bit)) for p in range(dp_size)])


class Sums:
    def __init__(self, name, order, dp_size):
        self.name, self.order, self.dp_size = name, order, dp_size
        self.left, self.step = tuple(sorted(order, reverse=True)), 0

    def exchange(self, send, keep, after=()):
        if after:
            send = lax.optimization_barrier((send, *after))[0]
        self.keep, self.recv = keep, swap_bit(send, self.order[self.step], self.dp_size)

    def add(self, after, micros=0.5):
        self.left = tuple(b for b in self.left if b != self.order[self.step])
        self.step += 1
        shape = (self.keep.shape[0] // 2,) + self.keep.shape[1:]
        kernel = functools.partial(add_kernel, self.left, self.order[self.step])
        return call(kernel, [(shape, BF16)] * 2, [self.keep, self.recv], micros, self.name, after)

    def advance(self, after, micros=0.5):
        if self.step + 1 >= len(self.order):
            return after[0]
        send, keep = self.add(after, micros)
        self.exchange(send, keep)
        return keep

    def finish(self, kernel, outs, after, micros=0.5):
        return call(kernel, outs, [self.keep, self.recv], micros, self.name + "_sum", after)


def shards_fn(
    dp_size,
    latents,
    labels,
    timesteps,
    class_table,
    mod_weight,
    mod_bias,
    qkv_weight,
    query_value_bias,
    out_weight,
    out_bias,
    up_weight,
    up_bias,
    down_weight,
    down_bias,
    cotangent,
):
    bits = dp_size.bit_length() - 1
    wide = (SEQ, D)
    slim = (SEQ, HALF)
    pieces = dp_size // 2
    rows_down, rows_up = HALF // dp_size, FEED // dp_size
    every = tuple(range(bits))
    left = every[::-1]
    up = Sums("up_add", every[1:2] + every[:1] + every[2:], dp_size)
    down = Sums("down_add", every[:1] + every[2:] + every[1:2], dp_size)
    proj = Sums("proj_add", every, dp_size)
    change = [(1, 2), (2, 1)]
    classes = class_table.shape[0]
    picks = (labels[:, None] == jnp.arange(classes, dtype=jnp.int32)[None, :]).astype(BF16)
    looked = jnp.dot(picks, class_table, preferred_element_type=F32)
    change = [(1, 2), (2, 1)]
    lat_col = col_swap(latents)
    cot_col = col_swap(cotangent)
    qkv_own = jnp.transpose(qkv_weight, (1, 2, 3, 0)).reshape(QKV, HALF)
    out_own = out_weight.reshape(HALF, HALF)
    qkv_peer, out_peer = col_swap(qkv_own), col_swap(out_own)

    frequency = jnp.exp(-math.log(10000.0) * jnp.arange(HALF, dtype=F32) / HALF)
    angles = timesteps.astype(F32)[:, None] * frequency[None, :]
    mod_rows = jnp.transpose(mod_weight, (1, 0, 2))
    mod_part, soft, cond = call(
        mod_kernel,
        [((16, HALF), F32), ((2, HALF), F32), ((2, HALF), F32)],
        [looked, jnp.cos(angles), jnp.sin(angles), mod_rows],
        20,
        "mod",
        [looked],
    )
    mod_part_recv = row_swap(mod_part)
    (lat_both,) = call(pack_kernel, [((2 * SEQ, HALF), BF16)], [latents, lat_col], 0.4, "pack", [mod_part])
    lat_change = lax.ppermute(lat_both, ("row", "col"), change)
    (cot_both,) = call(pack_kernel, [((2 * SEQ, HALF), BF16)], [cotangent, cot_col], 0.4, "pack", [lat_both])
    cot_change = lax.ppermute(cot_both, ("row", "col"), change)
    keep, other = call(
        mix_kernel,
        [((6, HALF), F32), ((16, HALF), F32)],
        [mod_part, mod_part_recv, mod_bias, out_bias, down_bias, query_value_bias],
        0.1,
        "mix",
        [cot_both, qkv_peer, out_peer],
    )
    other_col = col_swap(other)
    lat, normal = call(
        norm_kernel, [(wide, BF16), (wide, F32)], [latents, lat_col, lat_change], 1.8, "norm", [keep]
    )
    up_weight, down_weight = lax.optimization_barrier((up_weight, down_weight, other_col))[:2]
    down_peer, up_peer = col_swap(down_weight), col_swap(up_weight)
    mod, bias, normed_own, normed_peer, packed, attended, part_one = call(
        first_kernel,
        [((6, D), F32), ((8, D), F32), (slim, BF16), (slim, BF16), ((QKV, SEQ), BF16), ((HALF, SEQ), BF16), (wide, BF16)],
        [normal, keep, other, other_col, qkv_own, qkv_peer, out_own, out_peer],
        5,
        "first",
    )
    part_one_recv = row_swap(part_one)
    cot, two_grad_own, two_grad_peer, grad_active = call(
        early_kernel,
        [(wide, BF16), (slim, BF16), (slim, BF16), ((SEQ, FEED), F32)],
        [cotangent, cot_col, cot_change, mod, down_weight, down_peer],
        1,
        "early",
        [part_one],
    )
    normed_recv, attended_recv = col_swap(normed_peer), col_swap(attended)
    two_grad_recv = col_swap(two_grad_peer)
    resid_args = [lat, mod, bias, part_one, part_one_recv]
    second_own, active, hidden, part_two = call(
        second_kernel,
        [(slim, BF16), ((SEQ, FEED), BF16), ((SEQ, FEED + HALF), BF16), (wide, BF16)],
        [*resid_args, up_weight, up_peer, up_bias, grad_active],
        4,
        "second",
        [normed_recv, attended_recv, two_grad_recv],
    )
    part_two_recv = row_swap(part_two)
    active_recv, hidden_recv = col_swap(active), col_swap(hidden)
    branch_part, branch_sums = call(
        down_kernel, [(wide, BF16), ((8, D), F32)], [active, cot, down_weight, down_peer], 1, "down"
    )
    branch_recv = lax.ppermute(branch_part, ("row", "col"), [(1, 3), (2, 0)])
    down_send, down_keep, down_sum = call(
        functools.partial(down_grad_kernel, left, down.order[0]),
        [((pieces, rows_down, FEED), BF16), ((pieces, rows_down, FEED), BF16), ((1, HALF), F32)],
        [two_grad_own, two_grad_recv, active, active_recv],
        0.9,
        "down_grad",
        [branch_part],
    )
    down.exchange(down_send, down_keep)
    up_send, up_keep, up_sum = call(
        functools.partial(up_grad_kernel, left, up.order[0]),
        [((pieces, rows_up, HALF), BF16), ((pieces, rows_up, HALF), BF16), ((1, FEED), F32)],
        [second_own, hidden, hidden_recv],
        1.2,
        "up_grad",
        [down_send],
    )
    up.exchange(up_send, up_keep)
    grad_resid, one_grad_own, grad_packed, part_three = call(
        third_kernel,
        [(wide, F32), (slim, BF16), ((QKV + HALF, SEQ), BF16), ((SEQ + 16, D), BF16)],
        [*resid_args, part_two, part_two_recv, cot, packed, branch_sums, qkv_own, qkv_peer, out_own, out_peer],
        20,
        "third",
        [up_send],
        [pltpu.VMEM(slim, BF16)],
    )
    part_three_recv = row_swap(part_three)
    packed_recv = col_swap(grad_packed)
    token = down.advance([part_three], 6)
    token = up.advance([token], 6)
    proj_send, proj_keep, out_sum, pack_sum = call(
        functools.partial(proj_grad_kernel, left, proj.order[0]),
        [
            ((pieces, rows_down, FEED), BF16),
            ((pieces, rows_down, FEED), BF16),
            ((1, HALF), F32),
            ((1, QKV // 2), F32),
        ],
        [normed_own, normed_recv, grad_packed, packed_recv, one_grad_own, attended, attended_recv],
        1.3,
        "proj_grad",
        [token],
    )
    proj.exchange(proj_send, proj_keep)
    token = proj_send
    lat_grad_own, lat_grad_peer, mod_own, mod_peer = call(
        last_kernel,
        [(slim, F32), (slim, F32), ((6, HALF), F32), ((6, HALF), F32)],
        [*resid_args, part_two, part_two_recv, cot, grad_resid, part_three, part_three_recv, branch_sums],
        20,
        "last",
        [token],
    )
    mod_recv = col_swap(mod_peer)
    token = down.advance([mod_own])
    token = up.advance([token], 3)
    (payload,) = call(
        payload_kernel,
        [((1, 24, HALF), F32)],
        [mod_own, mod_recv, soft, up_sum, down_sum, out_sum, pack_sum],
        0.01,
        "payload",
        [token],
    )
    result_own, result_peer = call(
        out_kernel,
        [(slim, BF16), (slim, BF16)],
        [*resid_args, branch_part, branch_recv],
        0.1,
        "out",
        [payload],
    )
    result_recv = col_swap(result_peer)
    lat_recv = col_swap(lax.optimization_barrier((lat_grad_peer, result_own))[0])
    token = result_own
    mark = ((8, 128), F32)
    for step, bit in enumerate(every[::-1]):
        recv = swap_bit(payload, bit, dp_size)
        if step == 1:
            token = proj.advance([token], 20)
            while min(down.step, up.step) + 1 < bits:
                for part in (down, up):
                    token = part.advance([token], 0.1)
            token = proj.advance([token], 0.1)
        if step == 2:
            down_grad, token = down.finish(sum_kernel, [((rows_down, FEED), F32), mark], [token], 0.1)
            up_grad, token = up.finish(sum_kernel, [((rows_up, HALF), F32), mark], [token], 0.1)
        (payload,) = call(join_kernel, [((2 << step, 24, HALF), F32)], [payload, recv], 0.1, "join", [token])
        token = payload
    while proj.step + 1 < bits:
        token = proj.advance([token])
    width = HALF // dp_size
    mod_grad, mod_bias_grad, up_bias_grad, down_bias_grad, out_bias_grad, pack_grad, mod_mark = call(
        mod_sum_kernel,
        [
            ((6, width, HALF), F32),
            ((6, 1, width), F32),
            ((1, rows_up), F32),
            ((1, width), F32),
            ((1, width), F32),
            ((HEADS // 2, 2, HD // dp_size), F32),
            mark,
        ],
        [payload],
        0.1,
        "mod_sum",
        [token],
    )
    part_cond, part_cond_mark = call(
        cond_kernel, [((2, HALF), F32), mark], [mod_own, mod_recv, mod_rows], 0.1, "cond", [mod_mark]
    )
    output, grad_latents, grad_cond, finish_mark = call(
        finish_kernel,
        [(slim, BF16), (slim, F32), ((2, HALF), F32), mark],
        [result_own, result_recv, lat_grad_own, lat_recv, cond, part_cond, col_swap(part_cond)],
        0.5,
        "finish",
    )
    qkv_grad, out_grad = proj.finish(
        proj_sum_kernel,
        [((3 * HEADS, rows_down, HD), F32), ((HEADS, rows_down, HD), F32)],
        [finish_mark],
    )
    return (
        output,
        grad_latents,
        grad_cond,
        jnp.transpose(mod_grad, (2, 0, 1))[:, :, None, :],
        mod_bias_grad,
        jnp.transpose(qkv_grad.reshape(HEADS, 3, rows_down, HD), (2, 0, 1, 3))[None],
        jnp.transpose(pack_grad, (1, 0, 2)),
        jnp.transpose(out_grad, (0, 2, 1))[:, :, None, :],
        out_bias_grad,
        jnp.transpose(up_grad)[:, None, :],
        up_bias_grad,
        jnp.transpose(down_grad)[:, None, :],
        down_bias_grad,
    )


def solution(mesh):
    in_specs = (
        P(("dp", "row"), "col"),
        P("dp"),
        P("dp"),
        P(None, "row"),
        P("row", None, "col"),
        P(None, "col"),
        P("col", "row", None, None),
        P(None, ("row", "col"), None),
        P("row", None, "col"),
        P("col"),
        P("col", "row"),
        P("row"),
        P("row", "col"),
        P("col"),
        P(("dp", "row"), "col"),
    )
    out_specs = (
        P(("dp", "row"), "col"),
        P(("dp", "row"), "col"),
        P("dp", "row"),
        P("row", None, "col", "dp"),
        P(None, "col", "dp"),
        P("col", "dp", "row", None, None),
        P(None, ("row", "col"), "dp"),
        P("row", None, "col", "dp"),
        P("col", "dp"),
        P("col", "row", "dp"),
        P("row", "dp"),
        P("row", "col", "dp"),
        P("col", "dp"),
    )
    body = functools.partial(shards_fn, mesh.shape["dp"])
    return jax.shard_map(body, mesh=mesh, in_specs=in_specs, out_specs=out_specs, check_vma=False)
```

```python
import functools
import math

import jax
import jax.numpy as jnp
from jax import lax
from jax.experimental import pallas as pl
from jax.experimental.pallas import tpu as pltpu
from jax.sharding import PartitionSpec as P

D = 768
HALF = 384
SEQ = 256
HEADS = 6
HD = 64
QKV = HEADS * 3 * HD
FEED = 1536
EPSILON = 1e-06
HIGH = lax.Precision.HIGHEST
F32 = jnp.float32
BF16 = jnp.bfloat16
SWAP = [(0, 1), (1, 0)]
ALPHA = 0.7978845608
CUBIC = 0.044715


def mm(first, second, dims, precision=None):
    return lax.dot_general(
        first, second, ((dims[:1], dims[1:]), ((), ())), precision=precision, preferred_element_type=F32
    )


def call(kernel, outs, inputs, micros, name, after=(), scratch=(), limit=16):
    count = len(after)

    def body(*refs):
        kernel(*refs[count:])

    return pl.pallas_call(
        body if count else kernel,
        out_shape=[jax.ShapeDtypeStruct(s, t) for s, t in outs],
        in_specs=[pl.BlockSpec(memory_space=pl.ANY)] * count
        + [pl.BlockSpec(memory_space=pltpu.VMEM)] * len(inputs),
        out_specs=[pl.BlockSpec(memory_space=pltpu.VMEM)] * len(outs),
        scratch_shapes=list(scratch),
        compiler_params=pltpu.CompilerParams(vmem_limit_bytes=limit * 1024 * 1024),
        cost_estimate=pl.CostEstimate(flops=int(micros * 1.15e9), bytes_accessed=1024, transcendentals=0),
        name=name,
    )(*after, *inputs)


def row_mean(values):
    return jnp.sum(values, axis=1, keepdims=True) * (1.0 / D)


def norm_of(values):
    centred = values - row_mean(values)
    inverse = lax.rsqrt(row_mean(centred * centred) + EPSILON)
    return centred * inverse, inverse


def halves(first, second):
    return jnp.concatenate([first, second], axis=1)


def blocks(step=64):
    return [slice(i, i + step) for i in range(0, SEQ, step)]


def mod_kernel(looked, cosine, sine, weight, part, soft, cond):
    place = lax.broadcasted_iota(jnp.int32, (16, HALF), 0)
    both = looked[...] + jnp.where(lax.axis_index("row") == 0, cosine[...], sine[...])
    cond[...] = both
    values = jnp.where(place == 0, both[0:1, :], jnp.where(place == 1, both[1:2, :], 0.0))
    soft16 = (values / (1.0 + jnp.exp(-values))).astype(BF16)
    soft[...] = soft16.astype(F32)[0:2]
    part[...] = jnp.zeros((16, HALF), F32)
    for k in range(6):
        pair = mm(soft16, weight[k], (1, 0))
        part[k : k + 1, :] = pair[0:1]
        part[8 + k : 9 + k, :] = pair[1:2]


def mix_kernel(part, part_recv, bias, out_bias, down_bias, pair_bias, keep, other):
    total = part[...] + part_recv[...]
    here = lax.axis_index("col") == 0
    shift = bias[...].astype(F32)
    keep[...] = jnp.where(here, total[0:6], total[8:14]) + shift
    other[0:6, :] = jnp.where(here, total[8:14], total[0:6]) + shift
    other[6:8, :] = jnp.zeros((2, HALF), F32)
    other[8:16, :] = jnp.zeros((8, HALF), F32)
    other[8:9, :] = out_bias[...].astype(F32).reshape(1, HALF)
    other[9:10, :] = down_bias[...].astype(F32).reshape(1, HALF)
    for i in range(2):
        for h in range(HEADS // 2):
            spot = (3 * i + h) * HD
            other[10:11, spot : spot + HD] = pair_bias[i, h : h + 1, :].astype(F32)


def pack_kernel(first, second, out):
    out[0:SEQ, :] = first[...]
    out[SEQ : 2 * SEQ, :] = second[...]


def pick_image(own, col, change, rows):
    same = lax.axis_index("row") == lax.axis_index("col")
    later = slice(rows.start + SEQ, rows.stop + SEQ)
    left = jnp.where(same, own[rows, :].astype(F32), change[later, :].astype(F32))
    right = jnp.where(same, col[rows, :].astype(F32), change[rows, :].astype(F32))
    return halves(left, right)


def norm_kernel(own, col, change, lat, normal):
    for rows in blocks():
        values = pick_image(own, col, change, rows)
        lat[rows, :] = values.astype(BF16)
        normal[rows, :] = norm_of(values)[0]


def first_kernel(
    normal, keep, other, other_col, qkv_own, qkv_peer, out_own, out_peer,
    mod, bias, normed_own, normed_peer, packed, attended, part, probs_all,
):
    mods = halves(keep[...], other_col[0:6, :])
    mod[...] = mods
    shift, scale = mods[0:1], 1.0 + mods[1:2]
    for rows in blocks():
        normed = (normal[rows, :] * scale + shift).astype(BF16)
        normed_own[rows, :] = normed[:, :HALF]
        normed_peer[rows, :] = normed[:, HALF:]
    bias[...] = halves(other[8:16, :], other_col[8:16, :])
    place = lax.broadcasted_iota(jnp.int32, (16, SEQ), 0)
    one_hot = (place == 0).astype(BF16)
    mine = lax.axis_index("col")
    front = jnp.where(mine == 0, other[10:11, :], other_col[10:11, :])
    back = jnp.where(mine == 0, other_col[10:11, :], other[10:11, :])
    wide = lax.broadcasted_iota(jnp.int32, (16, 3 * HD), 0)
    for h in range(HEADS):
        rows = slice(h * 192, h * 192 + 192)
        source, spot = (front if h < 3 else back), (h % 3) * HD
        line = jnp.concatenate(
            [source[:, spot : spot + HD], jnp.zeros((1, HD), F32), source[:, 192 + spot : 192 + spot + HD]], axis=1
        )
        full = mm(qkv_own[rows, :], normed_own[...], (1, 1))
        full = full + mm(qkv_peer[rows, :], normed_peer[...], (1, 1))
        full = full + mm(jnp.where(wide == 0, line, 0.0).astype(BF16), one_hot, (0, 0))
        full = full.astype(BF16)
        packed[rows, :] = full
        query, key, value = full[0:64], full[64:128], full[128:192]
        scores = mm(key, query, (0, 0)) * 0.125
        expon = jnp.exp(scores - jnp.max(scores, axis=0, keepdims=True))
        probs = expon * (1.0 / jnp.sum(expon, axis=0, keepdims=True))
        probs_all[h] = probs
        attended[h * 64 : h * 64 + 64, :] = mm(value, probs.astype(BF16), (1, 0)).astype(BF16)
    part[:, :HALF] = mm(attended[...], out_own[...], (0, 0)).astype(BF16)
    part[:, HALF:] = mm(attended[...], out_peer[...], (0, 0)).astype(BF16)


def early_kernel(own, col, change, mod, down_own, down_peer, cot, grad_own, grad_peer, grad_active):
    gate = mod[5:6, :]
    for rows in blocks():
        values = pick_image(own, col, change, rows)
        cot[rows, :] = values.astype(BF16)
        grads = (values * gate).astype(BF16)
        grad_own[rows, :] = grads[:, :HALF]
        grad_peer[rows, :] = grads[:, HALF:]
    for cols in [slice(j, j + 256) for j in range(0, FEED, 256)]:
        grad_active[:, cols] = mm(grad_own[...], down_own[cols, :], (1, 1)) + mm(
            grad_peer[...], down_peer[cols, :], (1, 1)
        )


def branch(part, part_recv, bias, rows):
    return part[rows, :].astype(F32) + part_recv[rows, :].astype(F32) + bias


def resid_of(lat, mod, bias, part, part_recv, rows):
    gate = mod[2:3, :]
    one = branch(part, part_recv, bias[0:1, :], rows)
    return lat[rows, :].astype(F32) + gate * one, one


def second_kernel(
    lat, mod, bias, part, part_recv, up_own, up_peer, up_bias, grad_active,
    normed_own, active, hidden, part_two, normal_two, inverse_two,
):
    shift, scale = mod[3:4, :], 1.0 + mod[4:5, :]
    for rows in blocks():
        resid, unused = resid_of(lat, mod, bias, part, part_recv, rows)
        normal, inverse = norm_of(resid)
        normal_two[rows, :] = normal
        inverse_two[rows, :] = jnp.broadcast_to(inverse, (inverse.shape[0], 128))
        normed = (normal * scale + shift).astype(BF16)
        normed_own[rows, :] = normed[:, :HALF]
        hidden[rows, FEED:] = normed[:, HALF:]
    shift_up = up_bias[...].astype(F32).reshape(1, FEED)
    for cols in [slice(j, j + 256) for j in range(0, FEED, 256)]:
        pre = mm(normed_own[...], up_own[:, cols], (1, 0)) + mm(hidden[:, FEED:], up_peer[:, cols], (1, 0))
        pre = pre + shift_up[:, cols]
        square = pre * pre
        bend = jnp.tanh(ALPHA * (pre + CUBIC * (pre * square)))
        half = 0.5 * (1.0 + bend)
        active[:, cols] = (pre * half).astype(BF16)
        slope = half + 0.5 * pre * (1.0 - bend * bend) * (ALPHA * (1.0 + (3.0 * CUBIC) * square))
        hidden[:, cols] = (grad_active[:, cols] * slope).astype(BF16)
    part_two[:, :HALF] = mm(hidden[:, :FEED], up_own[...], (1, 1)).astype(BF16)
    part_two[:, HALF:] = mm(hidden[:, :FEED], up_peer[...], (1, 1)).astype(BF16)


def down_kernel(active, cot, down_own, down_peer, part, sums):
    sums[...] = jnp.zeros((8, D), F32)
    for cols, weight in ((slice(0, HALF), down_own), (slice(HALF, D), down_peer)):
        here = mm(active[...], weight[...], (1, 0)).astype(BF16)
        part[:, cols] = here
        sums[0:1, cols] = jnp.sum(here.astype(F32) * cot[:, cols].astype(F32), axis=0, keepdims=True)


def spots(left, bit):
    step = 1 << (len(left) - 1 - left.index(bit))
    return step, [q for q in range(1 << len(left)) if q & step == 0]


def bit_here(bit):
    return lax.rem(lax.div(lax.axis_index("dp"), 1 << bit), 2)


def split_store(full, left, bit, send, keep):
    here = bit_here(bit)
    size = full.shape[0] >> len(left)
    step, places = spots(left, bit)
    for q, place in enumerate(places):
        low = full[place * size : (place + 1) * size]
        high = full[(place + step) * size : (place + step + 1) * size]
        keep[q] = jnp.where(here == 0, low, high).astype(BF16)
        send[q] = jnp.where(here == 0, high, low).astype(BF16)


def tokens(own, recv, axis=0):
    return jnp.concatenate([own[...], recv[...]], axis=axis)


def up_grad_kernel(left, bit, normed, hidden, hidden_recv, send, keep, bias):
    rows = jnp.concatenate([normed[...], hidden_recv[:, FEED:]], axis=0)
    grads = jnp.concatenate([hidden[:, :FEED], hidden_recv[:, :FEED]], axis=0)
    ones = jnp.ones((16, 2 * SEQ), BF16)
    bias[...] = mm(ones, grads, (1, 0))[0:1]
    split_store(mm(grads, rows, (0, 0)), left, bit, send, keep)


def down_grad_kernel(left, bit, grad, grad_recv, active, active_recv, send, keep, bias):
    grads = tokens(grad, grad_recv)
    acts = tokens(active, active_recv)
    ones = jnp.ones((16, 2 * SEQ), BF16)
    bias[...] = mm(ones, grads, (1, 0))[0:1]
    split_store(mm(grads, acts, (0, 0)), left, bit, send, keep)


def third_kernel(
    normal_two, inverse_two, probs_all, mod, grad_two, grad_two_recv, cot, packed, sums,
    qkv_own, qkv_peer, out_own, out_peer,
    grad_resid, grad_own, grad_packed, part_three, grad_peer,
):
    gate, scale = mod[2:3, :], 1.0 + mod[4:5, :]
    for rows in blocks():
        normal, inverse = normal_two[rows, :], inverse_two[rows, 0:1]
        weighted = (grad_two[rows, :].astype(F32) + grad_two_recv[rows, :].astype(F32)) * scale
        back = inverse * (weighted - row_mean(weighted) - normal * row_mean(weighted * normal))
        grads = cot[rows, :].astype(F32) + back
        grad_resid[rows, :] = grads
        gated = (grads * gate).astype(BF16)
        grad_own[rows, :] = gated[:, :HALF]
        grad_peer[rows, :] = gated[:, HALF:]
    for h in range(HEADS):
        base = h * 192
        query, key = packed[base : base + 64, :], packed[base + 64 : base + 128, :]
        value = packed[base + 128 : base + 192, :]
        wide = slice(h * 64, h * 64 + 64)
        grad_att = mm(out_own[wide, :], grad_own[...], (1, 1)) + mm(out_peer[wide, :], grad_peer[...], (1, 1))
        grad_att = grad_att.astype(BF16)
        probs = probs_all[h]
        grad_probs = mm(value, grad_att, (0, 0))
        total = jnp.sum(probs * grad_probs, axis=0, keepdims=True)
        grad_scores = (probs * (grad_probs - total)).astype(BF16)
        grad_packed[base : base + 64, :] = (mm(key, grad_scores, (1, 0)) * 0.125).astype(BF16)
        grad_packed[base + 64 : base + 128, :] = (mm(query, grad_scores, (1, 1)) * 0.125).astype(BF16)
        grad_packed[base + 128 : base + 192, :] = mm(grad_att, probs.astype(BF16), (1, 1)).astype(BF16)
    grad_packed[QKV:, :] = grad_peer[...].T
    part_three[0:SEQ, :HALF] = mm(grad_packed[0:QKV, :], qkv_own[...], (0, 0)).astype(BF16)
    part_three[0:SEQ, HALF:] = mm(grad_packed[0:QKV, :], qkv_peer[...], (0, 0)).astype(BF16)
    values = sums[0:1, :]
    high = values.astype(BF16).astype(F32)
    middle = (values - high).astype(BF16).astype(F32)
    place = lax.broadcasted_iota(jnp.int32, (16, D), 0)
    terms = jnp.where(place == 0, high, jnp.where(place == 1, middle, jnp.where(place == 2, values - high - middle, 0.0)))
    part_three[SEQ : SEQ + 16, :] = terms.astype(BF16)


def proj_grad_kernel(
    left, bit, normed, normed_recv, packed, packed_recv, grad, attended, attended_recv,
    send, keep, out_bias, pack_bias,
):
    rows = tokens(normed, normed_recv)
    packs = jnp.concatenate([packed[0:QKV, :], packed_recv[0:QKV, :]], axis=1)
    grads = jnp.concatenate([grad[...].T, packed_recv[QKV:, :]], axis=1)
    atts = tokens(attended, attended_recv, 1)
    ones = jnp.ones((16, 2 * SEQ), BF16)
    out_bias[...] = mm(ones, grads, (1, 1))[0:1]
    sums = mm(ones, packs, (1, 1))[0:1]
    pack_bias[...] = jnp.where(lax.axis_index("col") == 0, sums[:, : QKV // 2], sums[:, QKV // 2 :])
    full = halves(mm(rows, packs, (0, 1)), mm(grads, atts, (1, 1)))
    split_store(full, left, bit, send, keep)


def last_kernel(
    lat, mod, bias, part, part_recv, grad_two, grad_two_recv, cot,
    grad_resid, grad_one, grad_one_recv, branch_sums, normal_two,
    lat_own, lat_peer, mod_own, mod_peer,
):
    scale = 1.0 + mod[1:2, :]
    sums = [jnp.zeros((1, D), F32)] * 6
    for rows in blocks():
        one = branch(part, part_recv, bias[0:1, :], rows)
        normal, inverse = norm_of(lat[rows, :].astype(F32))
        normed_grad = grad_one[rows, :].astype(F32) + grad_one_recv[rows, :].astype(F32)
        normed_two = grad_two[rows, :].astype(F32) + grad_two_recv[rows, :].astype(F32)
        resid_grad = grad_resid[rows, :]
        weighted = normed_grad * scale
        back = inverse * (weighted - row_mean(weighted) - normal * row_mean(weighted * normal))
        grads = resid_grad + back
        lat_own[rows, :] = grads[:, :HALF]
        lat_peer[rows, :] = grads[:, HALF:]
        terms = (
            normed_grad,
            normed_grad * normal,
            resid_grad * one,
            normed_two,
            normed_two * normal_two[rows, :],
            cot[rows, :].astype(F32),
        )
        sums = [s + jnp.sum(t, axis=0, keepdims=True) for s, t in zip(sums, terms)]
    far = grad_one_recv[SEQ : SEQ + 16, :].astype(F32)
    far = far[0:1] + far[1:2] + far[2:3]
    sums[5] = sums[5] * bias[1:2, :] + branch_sums[0:1, :] + far
    for k in range(6):
        mod_own[k : k + 1, :] = sums[k][:, :HALF]
        mod_peer[k : k + 1, :] = sums[k][:, HALF:]


def out_kernel(lat, mod, bias, part, part_recv, part_two, part_two_recv, own, peer):
    for rows in blocks():
        resid, unused = resid_of(lat, mod, bias, part, part_recv, rows)
        two = branch(part_two, part_two_recv, bias[1:2, :], rows)
        result = (resid + mod[5:6, :] * two).astype(BF16)
        own[rows, :] = result[:, :HALF]
        peer[rows, :] = result[:, HALF:]


def payload_kernel(mod_own, mod_recv, soft, up_bias, down_bias, out_bias, pack_bias, payload):
    payload = payload.at[0]
    col_index = lax.axis_index("col")
    own, recv = mod_own[...], mod_recv[...]
    payload[...] = jnp.zeros(payload.shape, F32)
    payload[0:6, :] = jnp.where(col_index == 0, own, recv)
    payload[6:7, :] = soft[0:1, :]
    payload[8:14, :] = jnp.where(col_index == 0, recv, own)
    payload[14:15, :] = soft[1:2, :]
    for k in range(4):
        payload[16 + k : 17 + k, :] = up_bias[:, k * HALF : k * HALF + HALF]
    payload[20:21, :] = down_bias[...]
    payload[21:22, :] = out_bias[...]
    payload[22:23, :] = pack_bias[:, :HALF]
    payload[23:24, 0:192] = pack_bias[:, HALF:]


def cond_kernel(mod_own, mod_recv, weight, part_cond, mark):
    col_index = lax.axis_index("col")
    own, recv = mod_own[...], mod_recv[...]
    zero = jnp.where(col_index == 0, own, recv)
    one = jnp.where(col_index == 0, recv, own)
    place = lax.broadcasted_iota(jnp.int32, (16, HALF), 0)
    total = jnp.zeros((16, HALF), F32)
    for k in range(6):
        terms = jnp.zeros((16, HALF), F32)
        for i, row in enumerate((zero[k : k + 1], one[k : k + 1])):
            high = row.astype(BF16).astype(F32)
            middle = (row - high).astype(BF16).astype(F32)
            low = row - high - middle
            for j, term in enumerate((high, middle, low)):
                terms = jnp.where(place == 3 * i + j, term, terms)
        total = total + mm(terms.astype(BF16), weight[k], (1, 1))
    part_cond[0:1, :] = total[0:1] + total[1:2] + total[2:3]
    part_cond[1:2, :] = total[3:4] + total[4:5] + total[5:6]
    mark[...] = jnp.zeros(mark.shape, F32)


def finish_kernel(out_own, out_recv, lat_own, lat_recv, cond, part, part_recv, out, lat, grad_cond, mark):
    mark[...] = jnp.zeros(mark.shape, F32)
    same = lax.axis_index("row") == lax.axis_index("col")
    out[...] = jnp.where(same, out_own[...], out_recv[...])
    lat[...] = jnp.where(same, lat_own[...], lat_recv[...])
    values = cond[...]
    gate = 1.0 / (1.0 + jnp.exp(-values))
    grad_cond[...] = (part[...] + part_recv[...]) * (gate * (1.0 + values * (1.0 - gate)))


def add_kernel(left, bit, keep, recv, send_next, keep_next):
    here = bit_here(bit)
    step, places = spots(left, bit)
    for q, first in enumerate(places):
        for place, out in ((first + step * here, keep_next), (first + step * (1 - here), send_next)):
            out[q] = (keep[place].astype(F32) + recv[place].astype(F32)).astype(BF16)


def join_kernel(first, second, out):
    count = first.shape[0]
    out[0:count] = first[...]
    out[count : 2 * count] = second[...]


def sum_kernel(keep, recv, out, mark):
    out[...] = keep[0].astype(F32) + recv[0].astype(F32)
    mark[...] = jnp.zeros(mark.shape, F32)


def proj_sum_kernel(keep, recv, qkv, out):
    both = keep[0].astype(F32) + recv[0].astype(F32)
    for k in range(3 * HEADS):
        qkv[k] = both[:, k * HD : k * HD + HD]
    for h in range(HEADS):
        out[h] = both[:, QKV + h * HD : QKV + h * HD + HD]


def lanes(values, start, width):
    count = values.shape[1]
    rows = lax.broadcasted_iota(jnp.int32, (count, width), 0)
    columns = lax.broadcasted_iota(jnp.int32, (count, width), 1)
    return mm(values, (rows == columns + start).astype(F32), (1, 0), HIGH)


def mod_sum_kernel(loads, weight, mod_bias, up_bias, down_bias, out_bias, pack_bias, mark):
    shards = loads.shape[0]
    dp_index = lax.axis_index("dp")
    part = HALF // shards
    count = 2 * shards
    images = [loads[s, 8 * i : 8 * i + 8, :] for s in range(shards) for i in range(2)]
    soft = jnp.concatenate([image[6:7] for image in images], axis=0)
    rows = jnp.concatenate([image[k : k + 1] for k in range(6) for image in images], axis=0)
    rows = lanes(rows, dp_index * part, part)
    for k in range(6):
        here = rows[k * count : (k + 1) * count]
        mod_bias[k] = jnp.sum(here, axis=0, keepdims=True)
        weight[k] = mm(here, soft, (0, 0), HIGH)
    total = loads[0, 16:24, :]
    for s in range(1, shards):
        total = total + loads[s, 16:24, :]
    start = dp_index * (4 * part)
    row = lax.div(start, HALF)
    picked = jnp.where(lax.broadcasted_iota(jnp.int32, (8, HALF), 0) == row, total, 0.0)
    up_bias[...] = lanes(jnp.sum(picked, axis=0, keepdims=True), start - row * HALF, 4 * part)
    blocks_here = lanes(total, dp_index * part, part)
    down_bias[...] = blocks_here[4:5]
    out_bias[...] = blocks_here[5:6]
    heads = []
    for h in range(HEADS // 2):
        for i in range(2):
            row, spot = divmod(h * 192 + i * 128, HALF)
            heads.append(total[6 + row : 7 + row, spot : spot + HD])
    heads = lanes(jnp.concatenate(heads, axis=0), dp_index * (HD // shards), HD // shards)
    for h in range(HEADS // 2):
        pack_bias[h] = heads[2 * h : 2 * h + 2]
    mark[...] = jnp.zeros(mark.shape, F32)


def row_swap(values):
    return lax.ppermute(values, "row", SWAP)


def col_swap(values):
    return lax.ppermute(values, "col", SWAP)


def both_swap(values):
    return lax.ppermute(values, ("row", "col"), [(0, 3), (3, 0), (1, 2), (2, 1)])


def swap_bit(values, bit, dp_size):
    return lax.ppermute(values, "dp", [(p, p ^ (1 << bit)) for p in range(dp_size)])


class Sums:
    def __init__(self, name, order, dp_size):
        self.name, self.order, self.dp_size = name, order, dp_size
        self.left, self.step = tuple(sorted(order, reverse=True)), 0

    def exchange(self, send, keep, after=()):
        if after:
            send = lax.optimization_barrier((send, *after))[0]
        self.keep, self.recv = keep, swap_bit(send, self.order[self.step], self.dp_size)

    def add(self, after, micros=0.5):
        self.left = tuple(b for b in self.left if b != self.order[self.step])
        self.step += 1
        shape = (self.keep.shape[0] // 2,) + self.keep.shape[1:]
        kernel = functools.partial(add_kernel, self.left, self.order[self.step])
        return call(kernel, [(shape, BF16)] * 2, [self.keep, self.recv], micros, self.name, after)

    def advance(self, after, micros=0.5):
        if self.step + 1 >= len(self.order):
            return after[0]
        send, keep = self.add(after, micros)
        self.exchange(send, keep)
        return keep

    def finish(self, kernel, outs, after, micros=0.5):
        return call(kernel, outs, [self.keep, self.recv], micros, self.name + "_sum", after)


def shards_fn(
    dp_size,
    latents,
    labels,
    timesteps,
    class_table,
    mod_weight,
    mod_bias,
    qkv_weight,
    query_value_bias,
    out_weight,
    out_bias,
    up_weight,
    up_bias,
    down_weight,
    down_bias,
    cotangent,
):
    bits = dp_size.bit_length() - 1
    wide = (SEQ, D)
    slim = (SEQ, HALF)
    pieces = dp_size // 2
    rows_down, rows_up = HALF // dp_size, FEED // dp_size
    every = tuple(range(bits))
    left = every[::-1]
    up = Sums("up_add", every[1:] + every[:1], dp_size)
    down = Sums("down_add", every, dp_size)
    proj = Sums("proj_add", every, dp_size)
    change = [(1, 2), (2, 1)]
    classes = class_table.shape[0]
    picks = (labels[:, None] == jnp.arange(classes, dtype=jnp.int32)[None, :]).astype(BF16)
    looked = jnp.dot(picks, class_table, preferred_element_type=F32)
    change = [(1, 2), (2, 1)]
    lat_col = col_swap(latents)
    cot_col = col_swap(cotangent)
    qkv_own = jnp.transpose(qkv_weight, (1, 2, 3, 0)).reshape(QKV, HALF)
    out_own = out_weight.reshape(HALF, HALF)
    qkv_peer, out_peer = col_swap(qkv_own), col_swap(out_own)

    frequency = jnp.exp(-math.log(10000.0) * jnp.arange(HALF, dtype=F32) / HALF)
    angles = timesteps.astype(F32)[:, None] * frequency[None, :]
    mod_rows = jnp.transpose(mod_weight, (1, 0, 2))
    mod_part, soft, cond = call(
        mod_kernel,
        [((16, HALF), F32), ((2, HALF), F32), ((2, HALF), F32)],
        [looked, jnp.cos(angles), jnp.sin(angles), mod_rows],
        20,
        "mod",
        [looked],
    )
    mod_part_recv = row_swap(mod_part)
    (lat_both,) = call(pack_kernel, [((2 * SEQ, HALF), BF16)], [latents, lat_col], 0.4, "pack", [mod_part])
    lat_change = lax.ppermute(lat_both, ("row", "col"), change)
    (cot_both,) = call(pack_kernel, [((2 * SEQ, HALF), BF16)], [cotangent, cot_col], 0.4, "pack", [lat_both])
    cot_change = lax.ppermute(cot_both, ("row", "col"), change)
    keep, other = call(
        mix_kernel,
        [((6, HALF), F32), ((16, HALF), F32)],
        [mod_part, mod_part_recv, mod_bias, out_bias, down_bias, query_value_bias],
        0.1,
        "mix",
        [cot_both, qkv_peer, out_peer],
    )
    other_col = col_swap(other)
    lat, normal = call(
        norm_kernel, [(wide, BF16), (wide, F32)], [latents, lat_col, lat_change], 1.8, "norm", [keep]
    )
    up_weight, down_weight = lax.optimization_barrier((up_weight, down_weight, other_col))[:2]
    down_peer, up_peer = col_swap(down_weight), col_swap(up_weight)
    mod, bias, normed_own, normed_peer, packed, attended, part_one, probs_all = call(
        first_kernel,
        [((6, D), F32), ((8, D), F32), (slim, BF16), (slim, BF16), ((QKV, SEQ), BF16), ((HALF, SEQ), BF16), (wide, BF16), ((HEADS, SEQ, SEQ), F32)],
        [normal, keep, other, other_col, qkv_own, qkv_peer, out_own, out_peer],
        5,
        "first",
    )
    part_one_recv = row_swap(part_one)
    cot, two_grad_own, two_grad_peer, grad_active = call(
        early_kernel,
        [(wide, BF16), (slim, BF16), (slim, BF16), ((SEQ, FEED), F32)],
        [cotangent, cot_col, cot_change, mod, down_weight, down_peer],
        1,
        "early",
        [part_one],
    )
    normed_recv, attended_recv = col_swap(normed_peer), col_swap(attended)
    two_grad_recv = col_swap(two_grad_peer)
    resid_args = [lat, mod, bias, part_one, part_one_recv]
    second_own, active, hidden, part_two, normal_two, inverse_two = call(
        second_kernel,
        [(slim, BF16), ((SEQ, FEED), BF16), ((SEQ, FEED + HALF), BF16), (wide, BF16), (wide, F32), ((SEQ, 128), F32)],
        [*resid_args, up_weight, up_peer, up_bias, grad_active],
        4,
        "second",
        [normed_recv, attended_recv, two_grad_recv],
    )
    part_two_recv = row_swap(part_two)
    active_recv, hidden_recv = col_swap(active), col_swap(hidden)
    branch_part, branch_sums = call(
        down_kernel, [(wide, BF16), ((8, D), F32)], [active, cot, down_weight, down_peer], 1, "down"
    )
    down_send, down_keep, down_sum = call(
        functools.partial(down_grad_kernel, left, down.order[0]),
        [((pieces, rows_down, FEED), BF16), ((pieces, rows_down, FEED), BF16), ((1, HALF), F32)],
        [two_grad_own, two_grad_recv, active, active_recv],
        0.9,
        "down_grad",
        [branch_part],
    )
    down.exchange(down_send, down_keep)
    up_send, up_keep, up_sum = call(
        functools.partial(up_grad_kernel, left, up.order[0]),
        [((pieces, rows_up, HALF), BF16), ((pieces, rows_up, HALF), BF16), ((1, FEED), F32)],
        [second_own, hidden, hidden_recv],
        1.2,
        "up_grad",
        [down_send],
    )
    up.exchange(up_send, up_keep)
    grad_resid, one_grad_own, grad_packed, part_three = call(
        third_kernel,
        [(wide, F32), (slim, BF16), ((QKV + HALF, SEQ), BF16), ((SEQ + 16, D), BF16)],
        [normal_two, inverse_two, probs_all, mod, part_two, part_two_recv, cot, packed, branch_sums, qkv_own, qkv_peer, out_own, out_peer],
        20,
        "third",
        [up_send],
        [pltpu.VMEM(slim, BF16)],
    )
    part_three_recv = row_swap(part_three)
    branch_recv = lax.ppermute(
        lax.optimization_barrier((branch_part, part_three))[0], ("row", "col"), [(1, 3), (2, 0)]
    )
    packed_recv = col_swap(grad_packed)
    token = down.advance([part_three], 0.3)
    token = up.advance([token], 6)
    proj_send, proj_keep, out_sum, pack_sum = call(
        functools.partial(proj_grad_kernel, left, proj.order[0]),
        [
            ((pieces, rows_down, FEED), BF16),
            ((pieces, rows_down, FEED), BF16),
            ((1, HALF), F32),
            ((1, QKV // 2), F32),
        ],
        [normed_own, normed_recv, grad_packed, packed_recv, one_grad_own, attended, attended_recv],
        1.3,
        "proj_grad",
        [token],
    )
    proj.exchange(proj_send, proj_keep)
    token = proj_send
    lat_grad_own, lat_grad_peer, mod_own, mod_peer = call(
        last_kernel,
        [(slim, F32), (slim, F32), ((6, HALF), F32), ((6, HALF), F32)],
        [*resid_args, part_two, part_two_recv, cot, grad_resid, part_three, part_three_recv, branch_sums, normal_two],
        20,
        "last",
        [token],
    )
    mod_recv = col_swap(mod_peer)
    token = down.advance([mod_own], 3.3)
    (payload,) = call(
        payload_kernel,
        [((1, 24, HALF), F32)],
        [mod_own, mod_recv, soft, up_sum, down_sum, out_sum, pack_sum],
        0.01,
        "payload",
        [token],
    )
    result_own, result_peer = call(
        out_kernel,
        [(slim, BF16), (slim, BF16)],
        [*resid_args, branch_part, branch_recv],
        0.1,
        "out",
        [payload],
    )
    result_recv = col_swap(result_peer)
    lat_recv = col_swap(lax.optimization_barrier((lat_grad_peer, result_own))[0])
    token = result_own
    mark = ((8, 128), F32)
    for step, bit in enumerate(every[::-1]):
        recv = swap_bit(payload, bit, dp_size)
        if step == 1:
            token = up.advance([token], 0.1)
            token = proj.advance([token], 0.1)
            token = proj.advance([token], 0.1)
        if step == 2:
            while down.step + 1 < bits:
                token = down.advance([token], 0.1)
            down_grad, token = down.finish(sum_kernel, [((rows_down, FEED), F32), mark], [token], 0.1)
        (payload,) = call(join_kernel, [((2 << step, 24, HALF), F32)], [payload, recv], 0.1, "join", [token])
        token = payload
    while min(up.step, proj.step) + 1 < bits:
        for part in (up, proj):
            token = part.advance([token], 0.1)
    width = HALF // dp_size
    mod_grad, mod_bias_grad, up_bias_grad, down_bias_grad, out_bias_grad, pack_grad, mod_mark = call(
        mod_sum_kernel,
        [
            ((6, width, HALF), F32),
            ((6, 1, width), F32),
            ((1, rows_up), F32),
            ((1, width), F32),
            ((1, width), F32),
            ((HEADS // 2, 2, HD // dp_size), F32),
            mark,
        ],
        [payload],
        0.1,
        "mod_sum",
        [token],
    )
    part_cond, part_cond_mark = call(
        cond_kernel, [((2, HALF), F32), mark], [mod_own, mod_recv, mod_rows], 0.1, "cond", [mod_mark]
    )
    output, grad_latents, grad_cond, finish_mark = call(
        finish_kernel,
        [(slim, BF16), (slim, F32), ((2, HALF), F32), mark],
        [result_own, result_recv, lat_grad_own, lat_recv, cond, part_cond, col_swap(part_cond)],
        0.5,
        "finish",
    )
    up_grad, token = up.finish(sum_kernel, [((rows_up, HALF), F32), mark], [finish_mark], 0.1)
    qkv_grad, out_grad = proj.finish(
        proj_sum_kernel,
        [((3 * HEADS, rows_down, HD), F32), ((HEADS, rows_down, HD), F32)],
        [token],
    )
    return (
        output,
        grad_latents,
        grad_cond,
        jnp.transpose(mod_grad, (2, 0, 1))[:, :, None, :],
        mod_bias_grad,
        jnp.transpose(qkv_grad.reshape(HEADS, 3, rows_down, HD), (2, 0, 1, 3))[None],
        jnp.transpose(pack_grad, (1, 0, 2)),
        jnp.transpose(out_grad, (0, 2, 1))[:, :, None, :],
        out_bias_grad,
        jnp.transpose(up_grad)[:, None, :],
        up_bias_grad,
        jnp.transpose(down_grad)[:, None, :],
        down_bias_grad,
    )


def solution(mesh):
    in_specs = (
        P(("dp", "row"), "col"),
        P("dp"),
        P("dp"),
        P(None, "row"),
        P("row", None, "col"),
        P(None, "col"),
        P("col", "row", None, None),
        P(None, ("row", "col"), None),
        P("row", None, "col"),
        P("col"),
        P("col", "row"),
        P("row"),
        P("row", "col"),
        P("col"),
        P(("dp", "row"), "col"),
    )
    out_specs = (
        P(("dp", "row"), "col"),
        P(("dp", "row"), "col"),
        P("dp", "row"),
        P("row", None, "col", "dp"),
        P(None, "col", "dp"),
        P("col", "dp", "row", None, None),
        P(None, ("row", "col"), "dp"),
        P("row", None, "col", "dp"),
        P("col", "dp"),
        P("col", "row", "dp"),
        P("row", "dp"),
        P("row", "col", "dp"),
        P("col", "dp"),
    )
    body = functools.partial(shards_fn, mesh.shape["dp"])
    return jax.shard_map(body, mesh=mesh, in_specs=in_specs, out_specs=out_specs, check_vma=False)
```

```python
import functools
import math

import jax
import jax.numpy as jnp
from jax import lax
from jax.experimental import pallas as pl
from jax.experimental.pallas import tpu as pltpu
from jax.sharding import PartitionSpec as P

D = 768
HALF = 384
SEQ = 256
HEADS = 6
HD = 64
QKV = HEADS * 3 * HD
FEED = 1536
EPSILON = 1e-06
HIGH = lax.Precision.HIGHEST
F32 = jnp.float32
BF16 = jnp.bfloat16
SWAP = [(0, 1), (1, 0)]
ALPHA = 0.7978845608
CUBIC = 0.044715


def mm(first, second, dims, precision=None):
    return lax.dot_general(
        first, second, ((dims[:1], dims[1:]), ((), ())), precision=precision, preferred_element_type=F32
    )


def call(kernel, outs, inputs, micros, name, after=(), scratch=(), limit=16):
    count = len(after)

    def body(*refs):
        kernel(*refs[count:])

    return pl.pallas_call(
        body if count else kernel,
        out_shape=[jax.ShapeDtypeStruct(s, t) for s, t in outs],
        in_specs=[pl.BlockSpec(memory_space=pl.ANY)] * count
        + [pl.BlockSpec(memory_space=pltpu.VMEM)] * len(inputs),
        out_specs=[pl.BlockSpec(memory_space=pltpu.VMEM)] * len(outs),
        scratch_shapes=list(scratch),
        compiler_params=pltpu.CompilerParams(vmem_limit_bytes=limit * 1024 * 1024),
        cost_estimate=pl.CostEstimate(flops=int(micros * 1.15e9), bytes_accessed=1024, transcendentals=0),
        name=name,
    )(*after, *inputs)


def row_mean(values):
    return jnp.sum(values, axis=1, keepdims=True) * (1.0 / D)


def norm_of(values):
    centred = values - row_mean(values)
    inverse = lax.rsqrt(row_mean(centred * centred) + EPSILON)
    return centred * inverse, inverse


def halves(first, second):
    return jnp.concatenate([first, second], axis=1)


def blocks(step=64):
    return [slice(i, i + step) for i in range(0, SEQ, step)]


def mod_kernel(looked, cosine, sine, weight, part, soft, cond):
    place = lax.broadcasted_iota(jnp.int32, (16, HALF), 0)
    both = looked[...] + jnp.where(lax.axis_index("row") == 0, cosine[...], sine[...])
    cond[...] = both
    values = jnp.where(place == 0, both[0:1, :], jnp.where(place == 1, both[1:2, :], 0.0))
    soft16 = (values / (1.0 + jnp.exp(-values))).astype(BF16)
    soft[...] = soft16.astype(F32)[0:2]
    part[...] = jnp.zeros((16, HALF), F32)
    for k in range(6):
        pair = mm(soft16, weight[k], (1, 0))
        part[k : k + 1, :] = pair[0:1]
        part[8 + k : 9 + k, :] = pair[1:2]


def mix_kernel(part, part_recv, bias, out_bias, down_bias, pair_bias, keep, other):
    total = part[...] + part_recv[...]
    here = lax.axis_index("col") == 0
    shift = bias[...].astype(F32)
    keep[...] = jnp.where(here, total[0:6], total[8:14]) + shift
    other[0:6, :] = jnp.where(here, total[8:14], total[0:6]) + shift
    other[6:8, :] = jnp.zeros((2, HALF), F32)
    other[8:16, :] = jnp.zeros((8, HALF), F32)
    other[8:9, :] = out_bias[...].astype(F32).reshape(1, HALF)
    other[9:10, :] = down_bias[...].astype(F32).reshape(1, HALF)
    for i in range(2):
        for h in range(HEADS // 2):
            spot = (3 * i + h) * HD
            other[10:11, spot : spot + HD] = pair_bias[i, h : h + 1, :].astype(F32)


def pack_kernel(first, second, out):
    out[0:SEQ, :] = first[...]
    out[SEQ : 2 * SEQ, :] = second[...]


def pick_image(own, col, change, rows):
    same = lax.axis_index("row") == lax.axis_index("col")
    later = slice(rows.start + SEQ, rows.stop + SEQ)
    left = jnp.where(same, own[rows, :].astype(F32), change[later, :].astype(F32))
    right = jnp.where(same, col[rows, :].astype(F32), change[rows, :].astype(F32))
    return halves(left, right)


def norm_kernel(own, col, change, lat, normal):
    for rows in blocks():
        values = pick_image(own, col, change, rows)
        lat[rows, :] = values.astype(BF16)
        normal[rows, :] = norm_of(values)[0]


def first_kernel(
    normal, keep, other, other_col, qkv_own, qkv_peer, out_own, out_peer,
    mod, bias, normed_own, normed_peer, packed, attended, part, probs_all,
):
    mods = halves(keep[...], other_col[0:6, :])
    mod[...] = mods
    shift, scale = mods[0:1], 1.0 + mods[1:2]
    for rows in blocks():
        normed = (normal[rows, :] * scale + shift).astype(BF16)
        normed_own[rows, :] = normed[:, :HALF]
        normed_peer[rows, :] = normed[:, HALF:]
    bias[...] = halves(other[8:16, :], other_col[8:16, :])
    place = lax.broadcasted_iota(jnp.int32, (16, SEQ), 0)
    one_hot = (place == 0).astype(BF16)
    mine = lax.axis_index("col")
    front = jnp.where(mine == 0, other[10:11, :], other_col[10:11, :])
    back = jnp.where(mine == 0, other_col[10:11, :], other[10:11, :])
    wide = lax.broadcasted_iota(jnp.int32, (16, 3 * HD), 0)
    for h in range(HEADS):
        rows = slice(h * 192, h * 192 + 192)
        source, spot = (front if h < 3 else back), (h % 3) * HD
        line = jnp.concatenate(
            [source[:, spot : spot + HD], jnp.zeros((1, HD), F32), source[:, 192 + spot : 192 + spot + HD]], axis=1
        )
        full = mm(qkv_own[rows, :], normed_own[...], (1, 1))
        full = full + mm(qkv_peer[rows, :], normed_peer[...], (1, 1))
        full = full + mm(jnp.where(wide == 0, line, 0.0).astype(BF16), one_hot, (0, 0))
        full = full.astype(BF16)
        packed[rows, :] = full
        query, key, value = full[0:64], full[64:128], full[128:192]
        scores = mm(key, query, (0, 0)) * 0.125
        expon = jnp.exp(scores - jnp.max(scores, axis=0, keepdims=True))
        probs = expon * (1.0 / jnp.sum(expon, axis=0, keepdims=True))
        probs_all[h] = probs
        attended[h * 64 : h * 64 + 64, :] = mm(value, probs.astype(BF16), (1, 0)).astype(BF16)
    part[:, :HALF] = mm(attended[...], out_own[...], (0, 0)).astype(BF16)
    part[:, HALF:] = mm(attended[...], out_peer[...], (0, 0)).astype(BF16)


def early_kernel(own, col, change, mod, down_own, down_peer, cot, grad_own, grad_peer, grad_active):
    gate = mod[5:6, :]
    for rows in blocks():
        values = pick_image(own, col, change, rows)
        cot[rows, :] = values.astype(BF16)
        grads = (values * gate).astype(BF16)
        grad_own[rows, :] = grads[:, :HALF]
        grad_peer[rows, :] = grads[:, HALF:]
    for cols in [slice(j, j + 256) for j in range(0, FEED, 256)]:
        grad_active[:, cols] = mm(grad_own[...], down_own[cols, :], (1, 1)) + mm(
            grad_peer[...], down_peer[cols, :], (1, 1)
        )


def branch(part, part_recv, bias, rows):
    return part[rows, :].astype(F32) + part_recv[rows, :].astype(F32) + bias


def resid_of(lat, mod, bias, part, part_recv, rows):
    gate = mod[2:3, :]
    one = branch(part, part_recv, bias[0:1, :], rows)
    return lat[rows, :].astype(F32) + gate * one, one


def second_kernel(
    lat, mod, bias, part, part_recv, up_own, up_peer, up_bias, grad_active,
    normed_own, active, hidden, part_two, normal_two, inverse_two,
):
    shift, scale = mod[3:4, :], 1.0 + mod[4:5, :]
    for rows in blocks():
        resid, unused = resid_of(lat, mod, bias, part, part_recv, rows)
        normal, inverse = norm_of(resid)
        normal_two[rows, :] = normal
        inverse_two[rows, :] = jnp.broadcast_to(inverse, (inverse.shape[0], 128))
        normed = (normal * scale + shift).astype(BF16)
        normed_own[rows, :] = normed[:, :HALF]
        hidden[rows, FEED:] = normed[:, HALF:]
    shift_up = up_bias[...].astype(F32).reshape(1, FEED)
    for cols in [slice(j, j + 256) for j in range(0, FEED, 256)]:
        pre = mm(normed_own[...], up_own[:, cols], (1, 0)) + mm(hidden[:, FEED:], up_peer[:, cols], (1, 0))
        pre = pre + shift_up[:, cols]
        square = pre * pre
        bend = jnp.tanh(ALPHA * (pre + CUBIC * (pre * square)))
        half = 0.5 * (1.0 + bend)
        active[:, cols] = (pre * half).astype(BF16)
        slope = half + 0.5 * pre * (1.0 - bend * bend) * (ALPHA * (1.0 + (3.0 * CUBIC) * square))
        hidden[:, cols] = (grad_active[:, cols] * slope).astype(BF16)
    part_two[:, :HALF] = mm(hidden[:, :FEED], up_own[...], (1, 1)).astype(BF16)
    part_two[:, HALF:] = mm(hidden[:, :FEED], up_peer[...], (1, 1)).astype(BF16)


def down_kernel(active, cot, down_own, down_peer, part, sums):
    sums[...] = jnp.zeros((8, D), F32)
    for cols, weight in ((slice(0, HALF), down_own), (slice(HALF, D), down_peer)):
        here = mm(active[...], weight[...], (1, 0)).astype(BF16)
        part[:, cols] = here
        sums[0:1, cols] = jnp.sum(here.astype(F32) * cot[:, cols].astype(F32), axis=0, keepdims=True)


def spots(left, bit):
    step = 1 << (len(left) - 1 - left.index(bit))
    return step, [q for q in range(1 << len(left)) if q & step == 0]


def bit_here(bit):
    return lax.rem(lax.div(lax.axis_index("dp"), 1 << bit), 2)


def split_store(full, left, bit, send, keep):
    here = bit_here(bit)
    size = full.shape[0] >> len(left)
    step, places = spots(left, bit)
    for q, place in enumerate(places):
        low = full[place * size : (place + 1) * size]
        high = full[(place + step) * size : (place + step + 1) * size]
        keep[q] = jnp.where(here == 0, low, high).astype(BF16)
        send[q] = jnp.where(here == 0, high, low).astype(BF16)


def tokens(own, recv, axis=0):
    return jnp.concatenate([own[...], recv[...]], axis=axis)


def up_grad_kernel(left, bit, normed, hidden, hidden_recv, send, keep, bias):
    rows = jnp.concatenate([normed[...], hidden_recv[:, FEED:]], axis=0)
    grads = jnp.concatenate([hidden[:, :FEED], hidden_recv[:, :FEED]], axis=0)
    ones = jnp.ones((16, 2 * SEQ), BF16)
    bias[...] = mm(ones, grads, (1, 0))[0:1]
    split_store(mm(grads, rows, (0, 0)), left, bit, send, keep)


def down_grad_kernel(left, bit, grad, grad_recv, active, active_recv, send, keep, bias):
    grads = tokens(grad, grad_recv)
    acts = tokens(active, active_recv)
    ones = jnp.ones((16, 2 * SEQ), BF16)
    bias[...] = mm(ones, grads, (1, 0))[0:1]
    split_store(mm(grads, acts, (0, 0)), left, bit, send, keep)


def third_kernel(
    normal_two, inverse_two, probs_all, mod, grad_two, grad_two_recv, cot, packed, sums,
    qkv_own, qkv_peer, out_own, out_peer,
    grad_resid, grad_own, grad_packed, part_three, grad_peer,
):
    gate, scale = mod[2:3, :], 1.0 + mod[4:5, :]
    for rows in blocks():
        normal, inverse = normal_two[rows, :], inverse_two[rows, 0:1]
        weighted = (grad_two[rows, :].astype(F32) + grad_two_recv[rows, :].astype(F32)) * scale
        back = inverse * (weighted - row_mean(weighted) - normal * row_mean(weighted * normal))
        grads = cot[rows, :].astype(F32) + back
        grad_resid[rows, :] = grads
        gated = (grads * gate).astype(BF16)
        grad_own[rows, :] = gated[:, :HALF]
        grad_peer[rows, :] = gated[:, HALF:]
    for h in range(HEADS):
        base = h * 192
        query, key = packed[base : base + 64, :], packed[base + 64 : base + 128, :]
        value = packed[base + 128 : base + 192, :]
        wide = slice(h * 64, h * 64 + 64)
        grad_att = mm(out_own[wide, :], grad_own[...], (1, 1)) + mm(out_peer[wide, :], grad_peer[...], (1, 1))
        grad_att = grad_att.astype(BF16)
        probs = probs_all[h]
        grad_probs = mm(value, grad_att, (0, 0))
        total = jnp.sum(probs * grad_probs, axis=0, keepdims=True)
        grad_scores = (probs * (grad_probs - total)).astype(BF16)
        grad_packed[base : base + 64, :] = (mm(key, grad_scores, (1, 0)) * 0.125).astype(BF16)
        grad_packed[base + 64 : base + 128, :] = (mm(query, grad_scores, (1, 1)) * 0.125).astype(BF16)
        grad_packed[base + 128 : base + 192, :] = mm(grad_att, probs.astype(BF16), (1, 1)).astype(BF16)
    grad_packed[QKV:, :] = grad_peer[...].T
    part_three[0:SEQ, :HALF] = mm(grad_packed[0:QKV, :], qkv_own[...], (0, 0)).astype(BF16)
    part_three[0:SEQ, HALF:] = mm(grad_packed[0:QKV, :], qkv_peer[...], (0, 0)).astype(BF16)
    values = sums[0:1, :]
    high = values.astype(BF16).astype(F32)
    middle = (values - high).astype(BF16).astype(F32)
    place = lax.broadcasted_iota(jnp.int32, (16, D), 0)
    terms = jnp.where(place == 0, high, jnp.where(place == 1, middle, jnp.where(place == 2, values - high - middle, 0.0)))
    part_three[SEQ : SEQ + 16, :] = terms.astype(BF16)


def proj_grad_kernel(
    left, bit, normed, normed_recv, packed, packed_recv, grad, attended, attended_recv,
    send, keep, out_bias, pack_bias,
):
    rows = tokens(normed, normed_recv)
    packs = jnp.concatenate([packed[0:QKV, :], packed_recv[0:QKV, :]], axis=1)
    grads = jnp.concatenate([grad[...].T, packed_recv[QKV:, :]], axis=1)
    atts = tokens(attended, attended_recv, 1)
    ones = jnp.ones((16, 2 * SEQ), BF16)
    out_bias[...] = mm(ones, grads, (1, 1))[0:1]
    sums = mm(ones, packs, (1, 1))[0:1]
    pack_bias[...] = jnp.where(lax.axis_index("col") == 0, sums[:, : QKV // 2], sums[:, QKV // 2 :])
    full = halves(mm(rows, packs, (0, 1)), mm(grads, atts, (1, 1)))
    split_store(full, left, bit, send, keep)


def last_kernel(
    lat, mod, bias, part, part_recv, grad_two, grad_two_recv, cot,
    grad_resid, grad_one, grad_one_recv, branch_sums, normal_two,
    lat_own, lat_peer, mod_own, mod_peer,
):
    scale = 1.0 + mod[1:2, :]
    sums = [jnp.zeros((1, D), F32)] * 6
    for rows in blocks():
        one = branch(part, part_recv, bias[0:1, :], rows)
        normal, inverse = norm_of(lat[rows, :].astype(F32))
        normed_grad = grad_one[rows, :].astype(F32) + grad_one_recv[rows, :].astype(F32)
        normed_two = grad_two[rows, :].astype(F32) + grad_two_recv[rows, :].astype(F32)
        resid_grad = grad_resid[rows, :]
        weighted = normed_grad * scale
        back = inverse * (weighted - row_mean(weighted) - normal * row_mean(weighted * normal))
        grads = resid_grad + back
        lat_own[rows, :] = grads[:, :HALF]
        lat_peer[rows, :] = grads[:, HALF:]
        terms = (
            normed_grad,
            normed_grad * normal,
            resid_grad * one,
            normed_two,
            normed_two * normal_two[rows, :],
            cot[rows, :].astype(F32),
        )
        sums = [s + jnp.sum(t, axis=0, keepdims=True) for s, t in zip(sums, terms)]
    far = grad_one_recv[SEQ : SEQ + 16, :].astype(F32)
    far = far[0:1] + far[1:2] + far[2:3]
    sums[5] = sums[5] * bias[1:2, :] + branch_sums[0:1, :] + far
    for k in range(6):
        mod_own[k : k + 1, :] = sums[k][:, :HALF]
        mod_peer[k : k + 1, :] = sums[k][:, HALF:]


def out_kernel(lat, mod, bias, part, part_recv, part_two, part_two_recv, own, peer):
    for rows in blocks():
        resid, unused = resid_of(lat, mod, bias, part, part_recv, rows)
        two = branch(part_two, part_two_recv, bias[1:2, :], rows)
        result = (resid + mod[5:6, :] * two).astype(BF16)
        own[rows, :] = result[:, :HALF]
        peer[rows, :] = result[:, HALF:]


def payload_kernel(mod_own, mod_recv, soft, up_bias, down_bias, out_bias, pack_bias, payload):
    payload = payload.at[0]
    col_index = lax.axis_index("col")
    own, recv = mod_own[...], mod_recv[...]
    payload[...] = jnp.zeros(payload.shape, F32)
    payload[0:6, :] = jnp.where(col_index == 0, own, recv)
    payload[6:7, :] = soft[0:1, :]
    payload[8:14, :] = jnp.where(col_index == 0, recv, own)
    payload[14:15, :] = soft[1:2, :]
    for k in range(4):
        payload[16 + k : 17 + k, :] = up_bias[:, k * HALF : k * HALF + HALF]
    payload[20:21, :] = down_bias[...]
    payload[21:22, :] = out_bias[...]
    payload[22:23, :] = pack_bias[:, :HALF]
    payload[23:24, 0:192] = pack_bias[:, HALF:]


def cond_kernel(mod_own, mod_recv, weight, part_cond, mark):
    col_index = lax.axis_index("col")
    own, recv = mod_own[...], mod_recv[...]
    zero = jnp.where(col_index == 0, own, recv)
    one = jnp.where(col_index == 0, recv, own)
    place = lax.broadcasted_iota(jnp.int32, (16, HALF), 0)
    total = jnp.zeros((16, HALF), F32)
    for k in range(6):
        terms = jnp.zeros((16, HALF), F32)
        for i, row in enumerate((zero[k : k + 1], one[k : k + 1])):
            high = row.astype(BF16).astype(F32)
            middle = (row - high).astype(BF16).astype(F32)
            low = row - high - middle
            for j, term in enumerate((high, middle, low)):
                terms = jnp.where(place == 3 * i + j, term, terms)
        total = total + mm(terms.astype(BF16), weight[k], (1, 1))
    part_cond[0:1, :] = total[0:1] + total[1:2] + total[2:3]
    part_cond[1:2, :] = total[3:4] + total[4:5] + total[5:6]
    mark[...] = jnp.zeros(mark.shape, F32)


def finish_kernel(out_own, out_recv, lat_own, lat_recv, cond, part, part_recv, out, lat, grad_cond, mark):
    mark[...] = jnp.zeros(mark.shape, F32)
    same = lax.axis_index("row") == lax.axis_index("col")
    out[...] = jnp.where(same, out_own[...], out_recv[...])
    lat[...] = jnp.where(same, lat_own[...], lat_recv[...])
    values = cond[...]
    gate = 1.0 / (1.0 + jnp.exp(-values))
    grad_cond[...] = (part[...] + part_recv[...]) * (gate * (1.0 + values * (1.0 - gate)))


def add_kernel(left, bit, keep, recv, send_next, keep_next):
    here = bit_here(bit)
    step, places = spots(left, bit)
    for q, first in enumerate(places):
        for place, out in ((first + step * here, keep_next), (first + step * (1 - here), send_next)):
            out[q] = (keep[place].astype(F32) + recv[place].astype(F32)).astype(BF16)


def join_kernel(first, second, out):
    count = first.shape[0]
    out[0:count] = first[...]
    out[count : 2 * count] = second[...]


def sum_kernel(keep, recv, out, mark):
    out[...] = keep[0].astype(F32) + recv[0].astype(F32)
    mark[...] = jnp.zeros(mark.shape, F32)


def proj_sum_kernel(keep, recv, qkv, out):
    both = keep[0].astype(F32) + recv[0].astype(F32)
    for k in range(3 * HEADS):
        qkv[k] = both[:, k * HD : k * HD + HD]
    for h in range(HEADS):
        out[h] = both[:, QKV + h * HD : QKV + h * HD + HD]


def lanes(values, start, width):
    count = values.shape[1]
    rows = lax.broadcasted_iota(jnp.int32, (count, width), 0)
    columns = lax.broadcasted_iota(jnp.int32, (count, width), 1)
    return mm(values, (rows == columns + start).astype(F32), (1, 0), HIGH)


def mod_sum_kernel(loads, weight, mod_bias, up_bias, down_bias, out_bias, pack_bias, mark):
    shards = loads.shape[0]
    dp_index = lax.axis_index("dp")
    part = HALF // shards
    count = 2 * shards
    images = [loads[s, 8 * i : 8 * i + 8, :] for s in range(shards) for i in range(2)]
    soft = jnp.concatenate([image[6:7] for image in images], axis=0)
    rows = jnp.concatenate([image[k : k + 1] for k in range(6) for image in images], axis=0)
    rows = lanes(rows, dp_index * part, part)
    for k in range(6):
        here = rows[k * count : (k + 1) * count]
        mod_bias[k] = jnp.sum(here, axis=0, keepdims=True)
        weight[k] = mm(here, soft, (0, 0), HIGH)
    total = loads[0, 16:24, :]
    for s in range(1, shards):
        total = total + loads[s, 16:24, :]
    start = dp_index * (4 * part)
    row = lax.div(start, HALF)
    picked = jnp.where(lax.broadcasted_iota(jnp.int32, (8, HALF), 0) == row, total, 0.0)
    up_bias[...] = lanes(jnp.sum(picked, axis=0, keepdims=True), start - row * HALF, 4 * part)
    blocks_here = lanes(total, dp_index * part, part)
    down_bias[...] = blocks_here[4:5]
    out_bias[...] = blocks_here[5:6]
    heads = []
    for h in range(HEADS // 2):
        for i in range(2):
            row, spot = divmod(h * 192 + i * 128, HALF)
            heads.append(total[6 + row : 7 + row, spot : spot + HD])
    heads = lanes(jnp.concatenate(heads, axis=0), dp_index * (HD // shards), HD // shards)
    for h in range(HEADS // 2):
        pack_bias[h] = heads[2 * h : 2 * h + 2]
    mark[...] = jnp.zeros(mark.shape, F32)


def row_swap(values):
    return lax.ppermute(values, "row", SWAP)


def col_swap(values):
    return lax.ppermute(values, "col", SWAP)


def both_swap(values):
    return lax.ppermute(values, ("row", "col"), [(0, 3), (3, 0), (1, 2), (2, 1)])


def swap_bit(values, bit, dp_size):
    return lax.ppermute(values, "dp", [(p, p ^ (1 << bit)) for p in range(dp_size)])


class Sums:
    def __init__(self, name, order, dp_size):
        self.name, self.order, self.dp_size = name, order, dp_size
        self.left, self.step = tuple(sorted(order, reverse=True)), 0

    def exchange(self, send, keep, after=()):
        if after:
            send = lax.optimization_barrier((send, *after))[0]
        self.keep, self.recv = keep, swap_bit(send, self.order[self.step], self.dp_size)

    def add(self, after, micros=0.5):
        self.left = tuple(b for b in self.left if b != self.order[self.step])
        self.step += 1
        shape = (self.keep.shape[0] // 2,) + self.keep.shape[1:]
        kernel = functools.partial(add_kernel, self.left, self.order[self.step])
        return call(kernel, [(shape, BF16)] * 2, [self.keep, self.recv], micros, self.name, after)

    def advance(self, after, micros=0.5):
        if self.step + 1 >= len(self.order):
            return after[0]
        send, keep = self.add(after, micros)
        self.exchange(send, keep)
        return keep

    def finish(self, kernel, outs, after, micros=0.5):
        return call(kernel, outs, [self.keep, self.recv], micros, self.name + "_sum", after)


def shards_fn(
    dp_size,
    latents,
    labels,
    timesteps,
    class_table,
    mod_weight,
    mod_bias,
    qkv_weight,
    query_value_bias,
    out_weight,
    out_bias,
    up_weight,
    up_bias,
    down_weight,
    down_bias,
    cotangent,
):
    bits = dp_size.bit_length() - 1
    wide = (SEQ, D)
    slim = (SEQ, HALF)
    pieces = dp_size // 2
    rows_down, rows_up = HALF // dp_size, FEED // dp_size
    every = tuple(range(bits))
    left = every[::-1]
    up = Sums("up_add", every[1:] + every[:1], dp_size)
    down = Sums("down_add", every, dp_size)
    proj = Sums("proj_add", every, dp_size)
    change = [(1, 2), (2, 1)]
    classes = class_table.shape[0]
    picks = (labels[:, None] == jnp.arange(classes, dtype=jnp.int32)[None, :]).astype(BF16)
    looked = jnp.dot(picks, class_table, preferred_element_type=F32)
    change = [(1, 2), (2, 1)]
    lat_col = col_swap(latents)
    cot_col = col_swap(cotangent)
    qkv_own = jnp.transpose(qkv_weight, (1, 2, 3, 0)).reshape(QKV, HALF)
    out_own = out_weight.reshape(HALF, HALF)
    qkv_peer, out_peer = col_swap(qkv_own), col_swap(out_own)

    frequency = jnp.exp(-math.log(10000.0) * jnp.arange(HALF, dtype=F32) / HALF)
    angles = timesteps.astype(F32)[:, None] * frequency[None, :]
    mod_rows = jnp.transpose(mod_weight, (1, 0, 2))
    mod_part, soft, cond = call(
        mod_kernel,
        [((16, HALF), F32), ((2, HALF), F32), ((2, HALF), F32)],
        [looked, jnp.cos(angles), jnp.sin(angles), mod_rows],
        20,
        "mod",
        [looked],
    )
    mod_part_recv = row_swap(mod_part)
    (lat_both,) = call(pack_kernel, [((2 * SEQ, HALF), BF16)], [latents, lat_col], 0.4, "pack", [mod_part])
    lat_change = lax.ppermute(lat_both, ("row", "col"), change)
    (cot_both,) = call(pack_kernel, [((2 * SEQ, HALF), BF16)], [cotangent, cot_col], 0.4, "pack", [lat_both])
    cot_change = lax.ppermute(cot_both, ("row", "col"), change)
    keep, other = call(
        mix_kernel,
        [((6, HALF), F32), ((16, HALF), F32)],
        [mod_part, mod_part_recv, mod_bias, out_bias, down_bias, query_value_bias],
        0.1,
        "mix",
        [cot_both, qkv_peer, out_peer],
    )
    other_col = col_swap(other)
    lat, normal = call(
        norm_kernel, [(wide, BF16), (wide, F32)], [latents, lat_col, lat_change], 1.8, "norm", [keep]
    )
    up_weight, down_weight = lax.optimization_barrier((up_weight, down_weight, other_col))[:2]
    down_peer, up_peer = col_swap(down_weight), col_swap(up_weight)
    mod, bias, normed_own, normed_peer, packed, attended, part_one, probs_all = call(
        first_kernel,
        [((6, D), F32), ((8, D), F32), (slim, BF16), (slim, BF16), ((QKV, SEQ), BF16), ((HALF, SEQ), BF16), (wide, BF16), ((HEADS, SEQ, SEQ), F32)],
        [normal, keep, other, other_col, qkv_own, qkv_peer, out_own, out_peer],
        5,
        "first",
    )
    part_one_recv = row_swap(part_one)
    cot, two_grad_own, two_grad_peer, grad_active = call(
        early_kernel,
        [(wide, BF16), (slim, BF16), (slim, BF16), ((SEQ, FEED), F32)],
        [cotangent, cot_col, cot_change, mod, down_weight, down_peer],
        1,
        "early",
        [part_one],
    )
    normed_recv, attended_recv = col_swap(normed_peer), col_swap(attended)
    two_grad_recv = col_swap(two_grad_peer)
    resid_args = [lat, mod, bias, part_one, part_one_recv]
    second_own, active, hidden, part_two, normal_two, inverse_two = call(
        second_kernel,
        [(slim, BF16), ((SEQ, FEED), BF16), ((SEQ, FEED + HALF), BF16), (wide, BF16), (wide, F32), ((SEQ, 128), F32)],
        [*resid_args, up_weight, up_peer, up_bias, grad_active],
        4,
        "second",
        [normed_recv, attended_recv, two_grad_recv],
    )
    part_two_recv = row_swap(part_two)
    active_recv, hidden_recv = col_swap(active), col_swap(hidden)
    branch_part, branch_sums = call(
        down_kernel, [(wide, BF16), ((8, D), F32)], [active, cot, down_weight, down_peer], 1, "down"
    )
    down_send, down_keep, down_sum = call(
        functools.partial(down_grad_kernel, left, down.order[0]),
        [((pieces, rows_down, FEED), BF16), ((pieces, rows_down, FEED), BF16), ((1, HALF), F32)],
        [two_grad_own, two_grad_recv, active, active_recv],
        0.9,
        "down_grad",
        [branch_part],
    )
    down.exchange(down_send, down_keep)
    up_send, up_keep, up_sum = call(
        functools.partial(up_grad_kernel, left, up.order[0]),
        [((pieces, rows_up, HALF), BF16), ((pieces, rows_up, HALF), BF16), ((1, FEED), F32)],
        [second_own, hidden, hidden_recv],
        1.2,
        "up_grad",
        [down_send],
    )
    up.exchange(up_send, up_keep)
    grad_resid, one_grad_own, grad_packed, part_three = call(
        third_kernel,
        [(wide, F32), (slim, BF16), ((QKV + HALF, SEQ), BF16), ((SEQ + 16, D), BF16)],
        [normal_two, inverse_two, probs_all, mod, part_two, part_two_recv, cot, packed, branch_sums, qkv_own, qkv_peer, out_own, out_peer],
        20,
        "third",
        [up_send],
        [pltpu.VMEM(slim, BF16)],
    )
    part_three_recv = row_swap(part_three)
    branch_recv = lax.ppermute(
        lax.optimization_barrier((branch_part, part_three))[0], ("row", "col"), [(1, 3), (2, 0)]
    )
    packed_recv = col_swap(grad_packed)
    token = down.advance([part_three], 0.3)
    token = up.advance([token], 6)
    proj_send, proj_keep, out_sum, pack_sum = call(
        functools.partial(proj_grad_kernel, left, proj.order[0]),
        [
            ((pieces, rows_down, FEED), BF16),
            ((pieces, rows_down, FEED), BF16),
            ((1, HALF), F32),
            ((1, QKV // 2), F32),
        ],
        [normed_own, normed_recv, grad_packed, packed_recv, one_grad_own, attended, attended_recv],
        1.3,
        "proj_grad",
        [token],
    )
    proj.exchange(proj_send, proj_keep)
    token = proj_send
    lat_grad_own, lat_grad_peer, mod_own, mod_peer = call(
        last_kernel,
        [(slim, F32), (slim, F32), ((6, HALF), F32), ((6, HALF), F32)],
        [*resid_args, part_two, part_two_recv, cot, grad_resid, part_three, part_three_recv, branch_sums, normal_two],
        20,
        "last",
        [token],
    )
    mod_recv = col_swap(mod_peer)
    token = down.advance([mod_own], 3.3)
    (payload,) = call(
        payload_kernel,
        [((1, 24, HALF), F32)],
        [mod_own, mod_recv, soft, up_sum, down_sum, out_sum, pack_sum],
        0.01,
        "payload",
        [token],
    )
    result_own, result_peer = call(
        out_kernel,
        [(slim, BF16), (slim, BF16)],
        [*resid_args, branch_part, branch_recv],
        0.1,
        "out",
        [payload],
    )
    result_recv = col_swap(result_peer)
    lat_recv = col_swap(lax.optimization_barrier((lat_grad_peer, result_own))[0])
    token = result_own
    mark = ((8, 128), F32)
    for step, bit in enumerate(every[2:] + every[:2]):
        recv = swap_bit(payload, bit, dp_size)
        if step == 1:
            token = up.advance([token], 0.1)
            token = proj.advance([token], 0.1)
        if step == 2:
            part_cond, part_cond_mark = call(
                cond_kernel, [((2, HALF), F32), mark], [mod_own, mod_recv, mod_rows], 0.1, "cond", [token]
            )
            token = proj.advance([part_cond_mark], 0.1)
            while down.step + 1 < bits:
                token = down.advance([token], 0.1)
            down_grad, token = down.finish(sum_kernel, [((rows_down, FEED), F32), mark], [token], 0.1)
            output, grad_latents, grad_cond, finish_mark = call(
                finish_kernel,
                [(slim, BF16), (slim, F32), ((2, HALF), F32), mark],
                [result_own, result_recv, lat_grad_own, lat_recv, cond, part_cond, col_swap(part_cond)],
                0.1,
                "finish",
                [token],
            )
            token = finish_mark
        (payload,) = call(join_kernel, [((2 << step, 24, HALF), F32)], [payload, recv], 0.1, "join", [token])
        token = payload
    while min(up.step, proj.step) + 1 < bits:
        for part in (up, proj):
            token = part.advance([token], 0.1)
    width = HALF // dp_size
    mod_grad, mod_bias_grad, up_bias_grad, down_bias_grad, out_bias_grad, pack_grad, mod_mark = call(
        mod_sum_kernel,
        [
            ((6, width, HALF), F32),
            ((6, 1, width), F32),
            ((1, rows_up), F32),
            ((1, width), F32),
            ((1, width), F32),
            ((HEADS // 2, 2, HD // dp_size), F32),
            mark,
        ],
        [payload],
        0.1,
        "mod_sum",
        [token],
    )
    up_grad, token = up.finish(sum_kernel, [((rows_up, HALF), F32), mark], [mod_mark], 0.1)
    qkv_grad, out_grad = proj.finish(
        proj_sum_kernel,
        [((3 * HEADS, rows_down, HD), F32), ((HEADS, rows_down, HD), F32)],
        [token],
    )
    return (
        output,
        grad_latents,
        grad_cond,
        jnp.transpose(mod_grad, (2, 0, 1))[:, :, None, :],
        mod_bias_grad,
        jnp.transpose(qkv_grad.reshape(HEADS, 3, rows_down, HD), (2, 0, 1, 3))[None],
        jnp.transpose(pack_grad, (1, 0, 2)),
        jnp.transpose(out_grad, (0, 2, 1))[:, :, None, :],
        out_bias_grad,
        jnp.transpose(up_grad)[:, None, :],
        up_bias_grad,
        jnp.transpose(down_grad)[:, None, :],
        down_bias_grad,
    )


def solution(mesh):
    in_specs = (
        P(("dp", "row"), "col"),
        P("dp"),
        P("dp"),
        P(None, "row"),
        P("row", None, "col"),
        P(None, "col"),
        P("col", "row", None, None),
        P(None, ("row", "col"), None),
        P("row", None, "col"),
        P("col"),
        P("col", "row"),
        P("row"),
        P("row", "col"),
        P("col"),
        P(("dp", "row"), "col"),
    )
    out_specs = (
        P(("dp", "row"), "col"),
        P(("dp", "row"), "col"),
        P("dp", "row"),
        P("row", None, "col", "dp"),
        P(None, "col", "dp"),
        P("col", "dp", "row", None, None),
        P(None, ("row", "col"), "dp"),
        P("row", None, "col", "dp"),
        P("col", "dp"),
        P("col", "row", "dp"),
        P("row", "dp"),
        P("row", "col", "dp"),
        P("col", "dp"),
    )
    body = functools.partial(shards_fn, mesh.shape["dp"])
    return jax.shard_map(body, mesh=mesh, in_specs=in_specs, out_specs=out_specs, check_vma=False)
```

```python
import functools
import math

import jax
import jax.numpy as jnp
from jax import lax
from jax.experimental import pallas as pl
from jax.experimental.pallas import tpu as pltpu
from jax.sharding import PartitionSpec as P

D = 768
HALF = 384
SEQ = 256
HEADS = 6
HD = 64
QKV = HEADS * 3 * HD
FEED = 1536
EPSILON = 1e-06
HIGH = lax.Precision.HIGHEST
F32 = jnp.float32
BF16 = jnp.bfloat16
SWAP = [(0, 1), (1, 0)]
ALPHA = 0.7978845608
CUBIC = 0.044715


def mm(first, second, dims, precision=None):
    return lax.dot_general(
        first, second, ((dims[:1], dims[1:]), ((), ())), precision=precision, preferred_element_type=F32
    )


def call(kernel, outs, inputs, micros, name, after=(), scratch=(), limit=16):
    count = len(after)

    def body(*refs):
        kernel(*refs[count:])

    return pl.pallas_call(
        body if count else kernel,
        out_shape=[jax.ShapeDtypeStruct(s, t) for s, t in outs],
        in_specs=[pl.BlockSpec(memory_space=pl.ANY)] * count
        + [pl.BlockSpec(memory_space=pltpu.VMEM)] * len(inputs),
        out_specs=[pl.BlockSpec(memory_space=pltpu.VMEM)] * len(outs),
        scratch_shapes=list(scratch),
        compiler_params=pltpu.CompilerParams(vmem_limit_bytes=limit * 1024 * 1024),
        cost_estimate=pl.CostEstimate(flops=int(micros * 1.15e9), bytes_accessed=1024, transcendentals=0),
        name=name,
    )(*after, *inputs)


def row_mean(values):
    return jnp.sum(values, axis=1, keepdims=True) * (1.0 / D)


def norm_of(values):
    centred = values - row_mean(values)
    inverse = lax.rsqrt(row_mean(centred * centred) + EPSILON)
    return centred * inverse, inverse


def halves(first, second):
    return jnp.concatenate([first, second], axis=1)


def blocks(step=64):
    return [slice(i, i + step) for i in range(0, SEQ, step)]


def mod_kernel(looked, cosine, sine, weight, part, soft, cond):
    place = lax.broadcasted_iota(jnp.int32, (16, HALF), 0)
    both = looked[...] + jnp.where(lax.axis_index("row") == 0, cosine[...], sine[...])
    cond[...] = both
    values = jnp.where(place == 0, both[0:1, :], jnp.where(place == 1, both[1:2, :], 0.0))
    soft16 = (values / (1.0 + jnp.exp(-values))).astype(BF16)
    soft[...] = soft16.astype(F32)[0:2]
    part[...] = jnp.zeros((16, HALF), F32)
    for k in range(6):
        pair = mm(soft16, weight[k], (1, 0))
        part[k : k + 1, :] = pair[0:1]
        part[8 + k : 9 + k, :] = pair[1:2]


def mix_kernel(part, part_recv, bias, out_bias, down_bias, pair_bias, keep, other):
    total = part[...] + part_recv[...]
    here = lax.axis_index("col") == 0
    shift = bias[...].astype(F32)
    keep[...] = jnp.where(here, total[0:6], total[8:14]) + shift
    other[0:6, :] = jnp.where(here, total[8:14], total[0:6]) + shift
    other[6:8, :] = jnp.zeros((2, HALF), F32)
    other[8:16, :] = jnp.zeros((8, HALF), F32)
    other[8:9, :] = out_bias[...].astype(F32).reshape(1, HALF)
    other[9:10, :] = down_bias[...].astype(F32).reshape(1, HALF)
    for i in range(2):
        for h in range(HEADS // 2):
            spot = (3 * i + h) * HD
            other[10:11, spot : spot + HD] = pair_bias[i, h : h + 1, :].astype(F32)


def pack_kernel(first, second, out):
    out[0:SEQ, :] = first[...]
    out[SEQ : 2 * SEQ, :] = second[...]


def pick_image(own, col, change, rows):
    same = lax.axis_index("row") == lax.axis_index("col")
    later = slice(rows.start + SEQ, rows.stop + SEQ)
    left = jnp.where(same, own[rows, :].astype(F32), change[later, :].astype(F32))
    right = jnp.where(same, col[rows, :].astype(F32), change[rows, :].astype(F32))
    return halves(left, right)


def norm_kernel(own, col, change, lat, normal):
    for rows in blocks():
        values = pick_image(own, col, change, rows)
        lat[rows, :] = values.astype(BF16)
        normal[rows, :] = norm_of(values)[0]


def first_kernel(
    normal, keep, other, other_col, qkv_own, qkv_peer, out_own, out_peer,
    mod, bias, normed_own, normed_peer, packed, attended, part, probs_all,
):
    mods = halves(keep[...], other_col[0:6, :])
    mod[...] = mods
    shift, scale = mods[0:1], 1.0 + mods[1:2]
    for rows in blocks():
        normed = (normal[rows, :] * scale + shift).astype(BF16)
        normed_own[rows, :] = normed[:, :HALF]
        normed_peer[rows, :] = normed[:, HALF:]
    bias[...] = halves(other[8:16, :], other_col[8:16, :])
    place = lax.broadcasted_iota(jnp.int32, (16, SEQ), 0)
    one_hot = (place == 0).astype(BF16)
    mine = lax.axis_index("col")
    front = jnp.where(mine == 0, other[10:11, :], other_col[10:11, :])
    back = jnp.where(mine == 0, other_col[10:11, :], other[10:11, :])
    wide = lax.broadcasted_iota(jnp.int32, (16, 3 * HD), 0)
    for h in range(HEADS):
        rows = slice(h * 192, h * 192 + 192)
        source, spot = (front if h < 3 else back), (h % 3) * HD
        line = jnp.concatenate(
            [source[:, spot : spot + HD], jnp.zeros((1, HD), F32), source[:, 192 + spot : 192 + spot + HD]], axis=1
        )
        full = mm(qkv_own[rows, :], normed_own[...], (1, 1))
        full = full + mm(qkv_peer[rows, :], normed_peer[...], (1, 1))
        full = full + mm(jnp.where(wide == 0, line, 0.0).astype(BF16), one_hot, (0, 0))
        full = full.astype(BF16)
        packed[rows, :] = full
        query, key, value = full[0:64], full[64:128], full[128:192]
        scores = mm(key, query, (0, 0)) * 0.125
        expon = jnp.exp(scores - jnp.max(scores, axis=0, keepdims=True))
        probs = expon * (1.0 / jnp.sum(expon, axis=0, keepdims=True))
        probs_all[h] = probs
        attended[h * 64 : h * 64 + 64, :] = mm(value, probs.astype(BF16), (1, 0)).astype(BF16)
    part[:, :HALF] = mm(attended[...], out_own[...], (0, 0)).astype(BF16)
    part[:, HALF:] = mm(attended[...], out_peer[...], (0, 0)).astype(BF16)


def early_kernel(own, col, change, mod, down_own, down_peer, cot, grad_own, grad_peer, grad_active):
    gate = mod[5:6, :]
    for rows in blocks():
        values = pick_image(own, col, change, rows)
        cot[rows, :] = values.astype(BF16)
        grads = (values * gate).astype(BF16)
        grad_own[rows, :] = grads[:, :HALF]
        grad_peer[rows, :] = grads[:, HALF:]
    for cols in [slice(j, j + 256) for j in range(0, FEED, 256)]:
        grad_active[:, cols] = mm(grad_own[...], down_own[cols, :], (1, 1)) + mm(
            grad_peer[...], down_peer[cols, :], (1, 1)
        )


def branch(part, part_recv, bias, rows):
    return part[rows, :].astype(F32) + part_recv[rows, :].astype(F32) + bias


def resid_of(lat, mod, bias, part, part_recv, rows):
    gate = mod[2:3, :]
    one = branch(part, part_recv, bias[0:1, :], rows)
    return lat[rows, :].astype(F32) + gate * one, one


def second_kernel(
    lat, mod, bias, part, part_recv, up_own, up_peer, up_bias, grad_active,
    normed_own, active, hidden, part_two, normal_two, inverse_two,
):
    shift, scale = mod[3:4, :], 1.0 + mod[4:5, :]
    for rows in blocks():
        resid, unused = resid_of(lat, mod, bias, part, part_recv, rows)
        normal, inverse = norm_of(resid)
        normal_two[rows, :] = normal
        inverse_two[rows, :] = jnp.broadcast_to(inverse, (inverse.shape[0], 128))
        normed = (normal * scale + shift).astype(BF16)
        normed_own[rows, :] = normed[:, :HALF]
        hidden[rows, FEED:] = normed[:, HALF:]
    shift_up = up_bias[...].astype(F32).reshape(1, FEED)
    for cols in [slice(j, j + 256) for j in range(0, FEED, 256)]:
        pre = mm(normed_own[...], up_own[:, cols], (1, 0)) + mm(hidden[:, FEED:], up_peer[:, cols], (1, 0))
        pre = pre + shift_up[:, cols]
        square = pre * pre
        bend = jnp.tanh(ALPHA * (pre + CUBIC * (pre * square)))
        half = 0.5 * (1.0 + bend)
        active[:, cols] = (pre * half).astype(BF16)
        slope = half + 0.5 * pre * (1.0 - bend * bend) * (ALPHA * (1.0 + (3.0 * CUBIC) * square))
        hidden[:, cols] = (grad_active[:, cols] * slope).astype(BF16)
    part_two[:, :HALF] = mm(hidden[:, :FEED], up_own[...], (1, 1)).astype(BF16)
    part_two[:, HALF:] = mm(hidden[:, :FEED], up_peer[...], (1, 1)).astype(BF16)


def down_kernel(active, cot, down_own, down_peer, part, sums):
    sums[...] = jnp.zeros((8, D), F32)
    for cols, weight in ((slice(0, HALF), down_own), (slice(HALF, D), down_peer)):
        here = mm(active[...], weight[...], (1, 0)).astype(BF16)
        part[:, cols] = here
        sums[0:1, cols] = jnp.sum(here.astype(F32) * cot[:, cols].astype(F32), axis=0, keepdims=True)


def spots(left, bit):
    step = 1 << (len(left) - 1 - left.index(bit))
    return step, [q for q in range(1 << len(left)) if q & step == 0]


def bit_here(bit):
    return lax.rem(lax.div(lax.axis_index("dp"), 1 << bit), 2)


def split_store(full, left, bit, send, keep):
    here = bit_here(bit)
    size = full.shape[0] >> len(left)
    step, places = spots(left, bit)
    for q, place in enumerate(places):
        low = full[place * size : (place + 1) * size]
        high = full[(place + step) * size : (place + step + 1) * size]
        keep[q] = jnp.where(here == 0, low, high).astype(BF16)
        send[q] = jnp.where(here == 0, high, low).astype(BF16)


def tokens(own, recv, axis=0):
    return jnp.concatenate([own[...], recv[...]], axis=axis)


def up_grad_kernel(left, bit, normed, hidden, hidden_recv, send, keep, bias):
    rows = jnp.concatenate([normed[...], hidden_recv[:, FEED:]], axis=0)
    grads = jnp.concatenate([hidden[:, :FEED], hidden_recv[:, :FEED]], axis=0)
    ones = jnp.ones((16, 2 * SEQ), BF16)
    bias[...] = mm(ones, grads, (1, 0))[0:1]
    split_store(mm(grads, rows, (0, 0)), left, bit, send, keep)


def down_grad_kernel(left, bit, grad, grad_recv, active, active_recv, send, keep, bias):
    grads = tokens(grad, grad_recv)
    acts = tokens(active, active_recv)
    ones = jnp.ones((16, 2 * SEQ), BF16)
    bias[...] = mm(ones, grads, (1, 0))[0:1]
    split_store(mm(grads, acts, (0, 0)), left, bit, send, keep)


def third_kernel(
    normal_two, inverse_two, probs_all, mod, grad_two, grad_two_recv, cot, packed, sums,
    qkv_own, qkv_peer, out_own, out_peer,
    grad_resid, grad_own, grad_packed, part_three, grad_peer,
):
    gate, scale = mod[2:3, :], 1.0 + mod[4:5, :]
    for rows in blocks():
        normal, inverse = normal_two[rows, :], inverse_two[rows, 0:1]
        weighted = (grad_two[rows, :].astype(F32) + grad_two_recv[rows, :].astype(F32)) * scale
        back = inverse * (weighted - row_mean(weighted) - normal * row_mean(weighted * normal))
        grads = cot[rows, :].astype(F32) + back
        grad_resid[rows, :] = grads
        gated = (grads * gate).astype(BF16)
        grad_own[rows, :] = gated[:, :HALF]
        grad_peer[rows, :] = gated[:, HALF:]
    for h in range(HEADS):
        base = h * 192
        query, key = packed[base : base + 64, :], packed[base + 64 : base + 128, :]
        value = packed[base + 128 : base + 192, :]
        wide = slice(h * 64, h * 64 + 64)
        grad_att = mm(out_own[wide, :], grad_own[...], (1, 1)) + mm(out_peer[wide, :], grad_peer[...], (1, 1))
        grad_att = grad_att.astype(BF16)
        probs = probs_all[h]
        grad_probs = mm(value, grad_att, (0, 0))
        total = jnp.sum(probs * grad_probs, axis=0, keepdims=True)
        grad_scores = (probs * (grad_probs - total)).astype(BF16)
        grad_packed[base : base + 64, :] = (mm(key, grad_scores, (1, 0)) * 0.125).astype(BF16)
        grad_packed[base + 64 : base + 128, :] = (mm(query, grad_scores, (1, 1)) * 0.125).astype(BF16)
        grad_packed[base + 128 : base + 192, :] = mm(grad_att, probs.astype(BF16), (1, 1)).astype(BF16)
    grad_packed[QKV:, :] = grad_peer[...].T
    part_three[0:SEQ, :HALF] = mm(grad_packed[0:QKV, :], qkv_own[...], (0, 0)).astype(BF16)
    part_three[0:SEQ, HALF:] = mm(grad_packed[0:QKV, :], qkv_peer[...], (0, 0)).astype(BF16)
    values = sums[0:1, :]
    high = values.astype(BF16).astype(F32)
    middle = (values - high).astype(BF16).astype(F32)
    place = lax.broadcasted_iota(jnp.int32, (16, D), 0)
    terms = jnp.where(place == 0, high, jnp.where(place == 1, middle, jnp.where(place == 2, values - high - middle, 0.0)))
    part_three[SEQ : SEQ + 16, :] = terms.astype(BF16)


def proj_grad_kernel(
    left, bit, normed, normed_recv, packed, packed_recv, grad, attended, attended_recv,
    send, keep, out_bias, pack_bias,
):
    rows = tokens(normed, normed_recv)
    packs = jnp.concatenate([packed[0:QKV, :], packed_recv[0:QKV, :]], axis=1)
    grads = jnp.concatenate([grad[...].T, packed_recv[QKV:, :]], axis=1)
    atts = tokens(attended, attended_recv, 1)
    ones = jnp.ones((16, 2 * SEQ), BF16)
    out_bias[...] = mm(ones, grads, (1, 1))[0:1]
    sums = mm(ones, packs, (1, 1))[0:1]
    pack_bias[...] = jnp.where(lax.axis_index("col") == 0, sums[:, : QKV // 2], sums[:, QKV // 2 :])
    full = halves(mm(rows, packs, (0, 1)), mm(grads, atts, (1, 1)))
    split_store(full, left, bit, send, keep)


def last_kernel(
    lat, mod, bias, part, part_recv, grad_two, grad_two_recv, cot,
    grad_resid, grad_one, grad_one_recv, branch_sums, normal_two,
    lat_own, lat_peer, mod_own, mod_peer,
):
    scale = 1.0 + mod[1:2, :]
    sums = [jnp.zeros((1, D), F32)] * 6
    for rows in blocks():
        one = branch(part, part_recv, bias[0:1, :], rows)
        normal, inverse = norm_of(lat[rows, :].astype(F32))
        normed_grad = grad_one[rows, :].astype(F32) + grad_one_recv[rows, :].astype(F32)
        normed_two = grad_two[rows, :].astype(F32) + grad_two_recv[rows, :].astype(F32)
        resid_grad = grad_resid[rows, :]
        weighted = normed_grad * scale
        back = inverse * (weighted - row_mean(weighted) - normal * row_mean(weighted * normal))
        grads = resid_grad + back
        lat_own[rows, :] = grads[:, :HALF]
        lat_peer[rows, :] = grads[:, HALF:]
        terms = (
            normed_grad,
            normed_grad * normal,
            resid_grad * one,
            normed_two,
            normed_two * normal_two[rows, :],
            cot[rows, :].astype(F32),
        )
        sums = [s + jnp.sum(t, axis=0, keepdims=True) for s, t in zip(sums, terms)]
    far = grad_one_recv[SEQ : SEQ + 16, :].astype(F32)
    far = far[0:1] + far[1:2] + far[2:3]
    sums[5] = sums[5] * bias[1:2, :] + branch_sums[0:1, :] + far
    for k in range(6):
        mod_own[k : k + 1, :] = sums[k][:, :HALF]
        mod_peer[k : k + 1, :] = sums[k][:, HALF:]


def out_kernel(lat, mod, bias, part, part_recv, part_two, part_two_recv, own, peer):
    for rows in blocks():
        resid, unused = resid_of(lat, mod, bias, part, part_recv, rows)
        two = branch(part_two, part_two_recv, bias[1:2, :], rows)
        result = (resid + mod[5:6, :] * two).astype(BF16)
        own[rows, :] = result[:, :HALF]
        peer[rows, :] = result[:, HALF:]


def payload_kernel(mod_own, mod_recv, soft, up_bias, down_bias, out_bias, pack_bias, payload):
    payload = payload.at[0]
    col_index = lax.axis_index("col")
    own, recv = mod_own[...], mod_recv[...]
    payload[...] = jnp.zeros(payload.shape, F32)
    payload[0:6, :] = jnp.where(col_index == 0, own, recv)
    payload[6:7, :] = soft[0:1, :]
    payload[8:14, :] = jnp.where(col_index == 0, recv, own)
    payload[14:15, :] = soft[1:2, :]
    for k in range(4):
        payload[16 + k : 17 + k, :] = up_bias[:, k * HALF : k * HALF + HALF]
    payload[20:21, :] = down_bias[...]
    payload[21:22, :] = out_bias[...]
    payload[22:23, :] = pack_bias[:, :HALF]
    payload[23:24, 0:192] = pack_bias[:, HALF:]


def cond_kernel(mod_own, mod_recv, weight, part_cond, mark):
    col_index = lax.axis_index("col")
    own, recv = mod_own[...], mod_recv[...]
    zero = jnp.where(col_index == 0, own, recv)
    one = jnp.where(col_index == 0, recv, own)
    place = lax.broadcasted_iota(jnp.int32, (16, HALF), 0)
    total = jnp.zeros((16, HALF), F32)
    for k in range(6):
        terms = jnp.zeros((16, HALF), F32)
        for i, row in enumerate((zero[k : k + 1], one[k : k + 1])):
            high = row.astype(BF16).astype(F32)
            middle = (row - high).astype(BF16).astype(F32)
            low = row - high - middle
            for j, term in enumerate((high, middle, low)):
                terms = jnp.where(place == 3 * i + j, term, terms)
        total = total + mm(terms.astype(BF16), weight[k], (1, 1))
    part_cond[0:1, :] = total[0:1] + total[1:2] + total[2:3]
    part_cond[1:2, :] = total[3:4] + total[4:5] + total[5:6]
    mark[...] = jnp.zeros(mark.shape, F32)


def finish_kernel(out_own, out_recv, lat_own, lat_recv, cond, part, part_recv, out, lat, grad_cond, mark):
    mark[...] = jnp.zeros(mark.shape, F32)
    same = lax.axis_index("row") == lax.axis_index("col")
    out[...] = jnp.where(same, out_own[...], out_recv[...])
    lat[...] = jnp.where(same, lat_own[...], lat_recv[...])
    values = cond[...]
    gate = 1.0 / (1.0 + jnp.exp(-values))
    grad_cond[...] = (part[...] + part_recv[...]) * (gate * (1.0 + values * (1.0 - gate)))


def add_kernel(left, bit, keep, recv, send_next, keep_next):
    here = bit_here(bit)
    step, places = spots(left, bit)
    for q, first in enumerate(places):
        for place, out in ((first + step * here, keep_next), (first + step * (1 - here), send_next)):
            out[q] = (keep[place].astype(F32) + recv[place].astype(F32)).astype(BF16)


def join_kernel(first, second, out):
    count = first.shape[0]
    out[0:count] = first[...]
    out[count : 2 * count] = second[...]


def sum_kernel(keep, recv, out, mark):
    out[...] = keep[0].astype(F32) + recv[0].astype(F32)
    mark[...] = jnp.zeros(mark.shape, F32)


def proj_sum_kernel(keep, recv, qkv, out, mark):
    mark[...] = jnp.zeros(mark.shape, F32)
    both = keep[0].astype(F32) + recv[0].astype(F32)
    for k in range(3 * HEADS):
        qkv[k] = both[:, k * HD : k * HD + HD]
    for h in range(HEADS):
        out[h] = both[:, QKV + h * HD : QKV + h * HD + HD]


def lanes(values, start, width):
    count = values.shape[1]
    rows = lax.broadcasted_iota(jnp.int32, (count, width), 0)
    columns = lax.broadcasted_iota(jnp.int32, (count, width), 1)
    return mm(values, (rows == columns + start).astype(F32), (1, 0), HIGH)


def mod_sum_kernel(loads, weight, mod_bias, up_bias, down_bias, out_bias, pack_bias, mark):
    shards = loads.shape[0]
    dp_index = lax.axis_index("dp")
    part = HALF // shards
    count = 2 * shards
    images = [loads[s, 8 * i : 8 * i + 8, :] for s in range(shards) for i in range(2)]
    soft = jnp.concatenate([image[6:7] for image in images], axis=0)
    rows = jnp.concatenate([image[k : k + 1] for k in range(6) for image in images], axis=0)
    rows = lanes(rows, dp_index * part, part)
    for k in range(6):
        here = rows[k * count : (k + 1) * count]
        mod_bias[k] = jnp.sum(here, axis=0, keepdims=True)
        weight[k] = mm(here, soft, (0, 0), HIGH)
    total = loads[0, 16:24, :]
    for s in range(1, shards):
        total = total + loads[s, 16:24, :]
    start = dp_index * (4 * part)
    row = lax.div(start, HALF)
    picked = jnp.where(lax.broadcasted_iota(jnp.int32, (8, HALF), 0) == row, total, 0.0)
    up_bias[...] = lanes(jnp.sum(picked, axis=0, keepdims=True), start - row * HALF, 4 * part)
    blocks_here = lanes(total, dp_index * part, part)
    down_bias[...] = blocks_here[4:5]
    out_bias[...] = blocks_here[5:6]
    heads = []
    for h in range(HEADS // 2):
        for i in range(2):
            row, spot = divmod(h * 192 + i * 128, HALF)
            heads.append(total[6 + row : 7 + row, spot : spot + HD])
    heads = lanes(jnp.concatenate(heads, axis=0), dp_index * (HD // shards), HD // shards)
    for h in range(HEADS // 2):
        pack_bias[h] = heads[2 * h : 2 * h + 2]
    mark[...] = jnp.zeros(mark.shape, F32)


def row_swap(values):
    return lax.ppermute(values, "row", SWAP)


def col_swap(values):
    return lax.ppermute(values, "col", SWAP)


def both_swap(values):
    return lax.ppermute(values, ("row", "col"), [(0, 3), (3, 0), (1, 2), (2, 1)])


def swap_bit(values, bit, dp_size):
    return lax.ppermute(values, "dp", [(p, p ^ (1 << bit)) for p in range(dp_size)])


class Sums:
    def __init__(self, name, order, dp_size):
        self.name, self.order, self.dp_size = name, order, dp_size
        self.left, self.step = tuple(sorted(order, reverse=True)), 0

    def exchange(self, send, keep, after=()):
        if after:
            send = lax.optimization_barrier((send, *after))[0]
        self.keep, self.recv = keep, swap_bit(send, self.order[self.step], self.dp_size)

    def add(self, after, micros=0.5):
        self.left = tuple(b for b in self.left if b != self.order[self.step])
        self.step += 1
        shape = (self.keep.shape[0] // 2,) + self.keep.shape[1:]
        kernel = functools.partial(add_kernel, self.left, self.order[self.step])
        return call(kernel, [(shape, BF16)] * 2, [self.keep, self.recv], micros, self.name, after)

    def advance(self, after, micros=0.5):
        if self.step + 1 >= len(self.order):
            return after[0]
        send, keep = self.add(after, micros)
        self.exchange(send, keep)
        return keep

    def finish(self, kernel, outs, after, micros=0.5):
        return call(kernel, outs, [self.keep, self.recv], micros, self.name + "_sum", after)


def shards_fn(
    dp_size,
    latents,
    labels,
    timesteps,
    class_table,
    mod_weight,
    mod_bias,
    qkv_weight,
    query_value_bias,
    out_weight,
    out_bias,
    up_weight,
    up_bias,
    down_weight,
    down_bias,
    cotangent,
):
    bits = dp_size.bit_length() - 1
    wide = (SEQ, D)
    slim = (SEQ, HALF)
    pieces = dp_size // 2
    rows_down, rows_up = HALF // dp_size, FEED // dp_size
    every = tuple(range(bits))
    left = every[::-1]
    up = Sums("up_add", every[1:] + every[:1], dp_size)
    down = Sums("down_add", every, dp_size)
    proj = Sums("proj_add", every, dp_size)
    change = [(1, 2), (2, 1)]
    classes = class_table.shape[0]
    picks = (labels[:, None] == jnp.arange(classes, dtype=jnp.int32)[None, :]).astype(BF16)
    looked = jnp.dot(picks, class_table, preferred_element_type=F32)
    change = [(1, 2), (2, 1)]
    lat_col = col_swap(latents)
    cot_col = col_swap(cotangent)
    qkv_own = jnp.transpose(qkv_weight, (1, 2, 3, 0)).reshape(QKV, HALF)
    out_own = out_weight.reshape(HALF, HALF)
    qkv_peer, out_peer = col_swap(qkv_own), col_swap(out_own)

    frequency = jnp.exp(-math.log(10000.0) * jnp.arange(HALF, dtype=F32) / HALF)
    angles = timesteps.astype(F32)[:, None] * frequency[None, :]
    mod_rows = jnp.transpose(mod_weight, (1, 0, 2))
    mod_part, soft, cond = call(
        mod_kernel,
        [((16, HALF), F32), ((2, HALF), F32), ((2, HALF), F32)],
        [looked, jnp.cos(angles), jnp.sin(angles), mod_rows],
        20,
        "mod",
        [looked],
    )
    mod_part_recv = row_swap(mod_part)
    (lat_both,) = call(pack_kernel, [((2 * SEQ, HALF), BF16)], [latents, lat_col], 0.4, "pack", [mod_part])
    lat_change = lax.ppermute(lat_both, ("row", "col"), change)
    (cot_both,) = call(pack_kernel, [((2 * SEQ, HALF), BF16)], [cotangent, cot_col], 0.4, "pack", [lat_both])
    cot_change = lax.ppermute(cot_both, ("row", "col"), change)
    keep, other = call(
        mix_kernel,
        [((6, HALF), F32), ((16, HALF), F32)],
        [mod_part, mod_part_recv, mod_bias, out_bias, down_bias, query_value_bias],
        0.1,
        "mix",
        [cot_both, qkv_peer, out_peer],
    )
    other_col = col_swap(other)
    lat, normal = call(
        norm_kernel, [(wide, BF16), (wide, F32)], [latents, lat_col, lat_change], 1.8, "norm", [keep]
    )
    up_weight, down_weight = lax.optimization_barrier((up_weight, down_weight, other_col))[:2]
    down_peer, up_peer = col_swap(down_weight), col_swap(up_weight)
    mod, bias, normed_own, normed_peer, packed, attended, part_one, probs_all = call(
        first_kernel,
        [((6, D), F32), ((8, D), F32), (slim, BF16), (slim, BF16), ((QKV, SEQ), BF16), ((HALF, SEQ), BF16), (wide, BF16), ((HEADS, SEQ, SEQ), F32)],
        [normal, keep, other, other_col, qkv_own, qkv_peer, out_own, out_peer],
        5,
        "first",
    )
    part_one_recv = row_swap(part_one)
    cot, two_grad_own, two_grad_peer, grad_active = call(
        early_kernel,
        [(wide, BF16), (slim, BF16), (slim, BF16), ((SEQ, FEED), F32)],
        [cotangent, cot_col, cot_change, mod, down_weight, down_peer],
        1,
        "early",
        [part_one],
    )
    normed_recv, attended_recv = col_swap(normed_peer), col_swap(attended)
    two_grad_recv = col_swap(two_grad_peer)
    resid_args = [lat, mod, bias, part_one, part_one_recv]
    second_own, active, hidden, part_two, normal_two, inverse_two = call(
        second_kernel,
        [(slim, BF16), ((SEQ, FEED), BF16), ((SEQ, FEED + HALF), BF16), (wide, BF16), (wide, F32), ((SEQ, 128), F32)],
        [*resid_args, up_weight, up_peer, up_bias, grad_active],
        4,
        "second",
        [normed_recv, attended_recv, two_grad_recv],
    )
    part_two_recv = row_swap(part_two)
    active_recv, hidden_recv = col_swap(active), col_swap(hidden)
    branch_part, branch_sums = call(
        down_kernel, [(wide, BF16), ((8, D), F32)], [active, cot, down_weight, down_peer], 1, "down"
    )
    down_send, down_keep, down_sum = call(
        functools.partial(down_grad_kernel, left, down.order[0]),
        [((pieces, rows_down, FEED), BF16), ((pieces, rows_down, FEED), BF16), ((1, HALF), F32)],
        [two_grad_own, two_grad_recv, active, active_recv],
        0.9,
        "down_grad",
        [branch_part],
    )
    down.exchange(down_send, down_keep)
    up_send, up_keep, up_sum = call(
        functools.partial(up_grad_kernel, left, up.order[0]),
        [((pieces, rows_up, HALF), BF16), ((pieces, rows_up, HALF), BF16), ((1, FEED), F32)],
        [second_own, hidden, hidden_recv],
        1.2,
        "up_grad",
        [down_send],
    )
    up.exchange(up_send, up_keep)
    grad_resid, one_grad_own, grad_packed, part_three = call(
        third_kernel,
        [(wide, F32), (slim, BF16), ((QKV + HALF, SEQ), BF16), ((SEQ + 16, D), BF16)],
        [normal_two, inverse_two, probs_all, mod, part_two, part_two_recv, cot, packed, branch_sums, qkv_own, qkv_peer, out_own, out_peer],
        20,
        "third",
        [up_send],
        [pltpu.VMEM(slim, BF16)],
    )
    part_three_recv = row_swap(part_three)
    branch_recv = lax.ppermute(
        lax.optimization_barrier((branch_part, part_three))[0], ("row", "col"), [(1, 3), (2, 0)]
    )
    packed_recv = col_swap(grad_packed)
    token = down.advance([part_three], 0.3)
    token = up.advance([token], 6)
    proj_send, proj_keep, out_sum, pack_sum = call(
        functools.partial(proj_grad_kernel, left, proj.order[0]),
        [
            ((pieces, rows_down, FEED), BF16),
            ((pieces, rows_down, FEED), BF16),
            ((1, HALF), F32),
            ((1, QKV // 2), F32),
        ],
        [normed_own, normed_recv, grad_packed, packed_recv, one_grad_own, attended, attended_recv],
        1.3,
        "proj_grad",
        [token],
    )
    proj.exchange(proj_send, proj_keep)
    token = proj_send
    lat_grad_own, lat_grad_peer, mod_own, mod_peer = call(
        last_kernel,
        [(slim, F32), (slim, F32), ((6, HALF), F32), ((6, HALF), F32)],
        [*resid_args, part_two, part_two_recv, cot, grad_resid, part_three, part_three_recv, branch_sums, normal_two],
        20,
        "last",
        [token],
    )
    mod_recv = col_swap(mod_peer)
    token = down.advance([mod_own], 3.3)
    (payload,) = call(
        payload_kernel,
        [((1, 24, HALF), F32)],
        [mod_own, mod_recv, soft, up_sum, down_sum, out_sum, pack_sum],
        0.01,
        "payload",
        [token],
    )
    result_own, result_peer = call(
        out_kernel,
        [(slim, BF16), (slim, BF16)],
        [*resid_args, branch_part, branch_recv],
        0.1,
        "out",
        [payload],
    )
    result_recv = col_swap(result_peer)
    lat_recv = col_swap(lax.optimization_barrier((lat_grad_peer, result_own))[0])
    token = result_own
    mark = ((8, 128), F32)
    for step, bit in enumerate(every[2:] + every[:2]):
        recv = swap_bit(payload, bit, dp_size)
        if step == 1:
            token = up.advance([token], 0.1)
            token = proj.advance([token], 0.1)
        if step == 2:
            part_cond, part_cond_mark = call(
                cond_kernel, [((2, HALF), F32), mark], [mod_own, mod_recv, mod_rows], 0.1, "cond", [token]
            )
            token = proj.advance([part_cond_mark], 0.1)
            while down.step + 1 < bits:
                token = down.advance([token], 0.1)
            down_grad, token = down.finish(sum_kernel, [((rows_down, FEED), F32), mark], [token], 0.1)
            output, grad_latents, grad_cond, finish_mark = call(
                finish_kernel,
                [(slim, BF16), (slim, F32), ((2, HALF), F32), mark],
                [result_own, result_recv, lat_grad_own, lat_recv, cond, part_cond, col_swap(part_cond)],
                0.1,
                "finish",
                [token],
            )
            token = finish_mark
        (payload,) = call(join_kernel, [((2 << step, 24, HALF), F32)], [payload, recv], 0.1, "join", [token])
        token = payload
    while min(up.step, proj.step) + 1 < bits:
        for part in (up, proj):
            token = part.advance([token], 0.1)
    width = HALF // dp_size
    mod_grad, mod_bias_grad, up_bias_grad, down_bias_grad, out_bias_grad, pack_grad, mod_mark = call(
        mod_sum_kernel,
        [
            ((6, width, HALF), F32),
            ((6, 1, width), F32),
            ((1, rows_up), F32),
            ((1, width), F32),
            ((1, width), F32),
            ((HEADS // 2, 2, HD // dp_size), F32),
            mark,
        ],
        [payload],
        0.1,
        "mod_sum",
        [token],
    )
    qkv_grad, out_grad, token = proj.finish(
        proj_sum_kernel,
        [((3 * HEADS, rows_down, HD), F32), ((HEADS, rows_down, HD), F32), mark],
        [mod_mark],
        0.1,
    )
    up_grad, token = up.finish(sum_kernel, [((rows_up, HALF), F32), mark], [token], 0.1)
    return (
        output,
        grad_latents,
        grad_cond,
        jnp.transpose(mod_grad, (2, 0, 1))[:, :, None, :],
        mod_bias_grad,
        jnp.transpose(qkv_grad.reshape(HEADS, 3, rows_down, HD), (2, 0, 1, 3))[None],
        jnp.transpose(pack_grad, (1, 0, 2)),
        jnp.transpose(out_grad, (0, 2, 1))[:, :, None, :],
        out_bias_grad,
        jnp.transpose(up_grad)[:, None, :],
        up_bias_grad,
        jnp.transpose(down_grad)[:, None, :],
        down_bias_grad,
    )


def solution(mesh):
    in_specs = (
        P(("dp", "row"), "col"),
        P("dp"),
        P("dp"),
        P(None, "row"),
        P("row", None, "col"),
        P(None, "col"),
        P("col", "row", None, None),
        P(None, ("row", "col"), None),
        P("row", None, "col"),
        P("col"),
        P("col", "row"),
        P("row"),
        P("row", "col"),
        P("col"),
        P(("dp", "row"), "col"),
    )
    out_specs = (
        P(("dp", "row"), "col"),
        P(("dp", "row"), "col"),
        P("dp", "row"),
        P("row", None, "col", "dp"),
        P(None, "col", "dp"),
        P("col", "dp", "row", None, None),
        P(None, ("row", "col"), "dp"),
        P("row", None, "col", "dp"),
        P("col", "dp"),
        P("col", "row", "dp"),
        P("row", "dp"),
        P("row", "col", "dp"),
        P("col", "dp"),
    )
    body = functools.partial(shards_fn, mesh.shape["dp"])
    return jax.shard_map(body, mesh=mesh, in_specs=in_specs, out_specs=out_specs, check_vma=False)
```
